32 devices in a mesh: fsdp: 4 (over y, x), tp: 8 (over z, core).
Axes of the slice: x: 2, y: 2, z: 4, core: 2. Of those that a mesh axis runs over, the one named last changes fastest.
Arguments:
- inputs: bfloat16 [16384, 2048], P(('fsdp', 'tp')), may hold values from -6 to 6
- att_proj: bfloat16 [2048, 3, 2048], P('fsdp', None, 'tp'), may hold values from -0.1875 to 0.1875
- attn_out: bfloat16 [2048, 2048], P('tp', 'fsdp'), may hold values from -0.75 to 0.75
- ff_proj: bfloat16 [2048, 2, 8192], P('fsdp', None, 'tp'), may hold values from -0.125 to 0.125
- ff_out: bfloat16 [8192, 2048], P('tp', 'fsdp'), may hold values from -0.0625 to 0.0625
- segments: int32 [16384], P('fsdp'), may hold values from 0 to 2, as said below
- pad_mask: int32 [16384], P('fsdp'), may hold values from 0 to 1, as said below
- positions: int32 [16384], P('fsdp'), may hold values from 0 to 6143, as said below
- cotangent: bfloat16 [16384, 2048], P(('fsdp', 'tp')), may hold values from -6 to 6
Outputs:
- output: bfloat16 [16384, 2048], P(('fsdp', 'tp'))
- grad_input: bfloat16 [16384, 2048], P(('fsdp', 'tp'))
- grad_att_proj: float32 [2048, 3, 2048], P('fsdp', None, 'tp')
- grad_attn_out: float32 [2048, 2048], P('tp', 'fsdp')
- grad_ff_proj: float32 [2048, 2, 8192], P('fsdp', None, 'tp')
- grad_ff_out: float32 [8192, 2048], P('tp', 'fsdp')
The draws below stay inside these ranges and needn't reach their ends.
Inputs may be any that keep to these rules, and one draw needn't show every extreme that they name: `segments`: within each packed sequence of 2048 tokens the ids never fall. `pad_mask`: in each packed sequence the padding is one run at its end, of one token or more. `positions`: within a document the position rises by one from token to token.
All inputs are finite; a program needn't handle non-finite values.
Results may differ from the reference program's by a relative error of at most 0.023.
Values may be sent and summed in bfloat16 or wider, within the bound.
A program may use at most 320 MiB of HBM per device.

```python
import jax
import jax.numpy as jnp
from jax import lax

D = 2048
HEADS = 16
HD = 128
FF = 8192
WINDOW = 1024
SEQ_LEN = 2048
TOKENS = 16384
N_TP = 8


def document_bounds(key):
    seq_total = TOKENS // SEQ_LEN
    reach = max(3, SEQ_LEN // 32)
    first_cut = jax.random.randint(jax.random.fold_in(key, 11), (seq_total, 1), 1, reach)
    last_cut = SEQ_LEN - jax.random.randint(jax.random.fold_in(key, 12), (seq_total, 1), 1, reach)
    places = jnp.arange(SEQ_LEN, dtype=jnp.int32)[None, :]
    segment = (places >= first_cut).astype(jnp.int32) + (places >= last_cut).astype(jnp.int32)
    starts = jnp.where(places >= last_cut, last_cut, jnp.where(places >= first_cut, first_cut, 0))
    return (segment, places - starts, last_cut)


def draw_segments(key, part):
    segment, offset, last_cut = document_bounds(key)
    return segment.reshape(-1).astype(jnp.int32)


def draw_positions(key, part):
    segment, offset, last_cut = document_bounds(key)
    key = jax.random.fold_in(key, 5)
    anchor = jax.random.randint(key, (TOKENS // SEQ_LEN, 3), 0, 4096)
    anchor = anchor.at[0, 0].set(0)
    anchor = anchor.at[0, 2].set(4096 + last_cut[0, 0])
    picked = jnp.where(segment == 0, anchor[:, 0:1], jnp.where(segment == 1, anchor[:, 1:2], anchor[:, 2:3]))
    return (offset + picked).reshape(-1).astype(jnp.int32)


def draw_pad_mask(key, part):
    key = jax.random.fold_in(key, 7)
    tail = jax.random.randint(key, (TOKENS // SEQ_LEN, 1), 1, max(2, SEQ_LEN // 16) + 1)
    places = jnp.arange(SEQ_LEN, dtype=jnp.int32)[None, :]
    return (places < SEQ_LEN - tail).astype(jnp.int32).reshape(-1)


def shard_levels(own_key, shape, cuts, least, high):
    gain = 1.0
    for dim, shards_of in cuts:
        draws = jax.random.uniform(jax.random.fold_in(jax.random.fold_in(own_key, 6), dim), (shards_of,), jnp.float32, least / len(cuts), high / len(cuts))
        gain = gain * jnp.repeat(jnp.exp(draws), shape[dim] // shards_of).reshape((-1,) + (1,) * (len(shape) - 1 - dim))
    return gain


def scatter_about(rng, dims, spread, bound, cuts=(), held_as=jnp.bfloat16):
    level = shard_levels(rng, dims, cuts, -0.22, 0.18) if cuts else 1.0
    values = jax.random.normal(rng, dims, jnp.float32) * spread * level
    return jnp.minimum(jnp.maximum(values, -bound), bound).astype(held_as)


def setup_inputs(seed: int = 0) -> dict:
    arg_keys = jax.random.split(jax.random.key(seed), 10)
    inputs = scatter_about(arg_keys[0], (TOKENS, D), 1.0, 6.0, ((0, 32),))
    att_proj = scatter_about(arg_keys[1], (D, 3, D), (D // 2) ** -0.5, 0.1875, ((0, 4), (2, 8)))
    attn_out = scatter_about(arg_keys[2], (D, D), (D // 32) ** -0.5, 0.75, ((0, 8), (1, 4)))
    ff_proj = scatter_about(arg_keys[3], (D, 2, FF), D ** -0.5, 0.125, ((0, 4), (2, 8)))
    ff_out = scatter_about(arg_keys[4], (FF, D), FF ** -0.5, 0.0625, ((0, 8), (1, 4)))
    segments = draw_segments(jax.random.fold_in(arg_keys[9], 71), 0)
    pad_mask = draw_pad_mask(jax.random.fold_in(arg_keys[9], 71), 0)
    positions = draw_positions(jax.random.fold_in(arg_keys[9], 71), 0)
    cotangent = scatter_about(arg_keys[8], (TOKENS, D), 1.0, 6.0, ((0, 32),))
    return {"inputs": inputs, "att_proj": att_proj, "attn_out": attn_out, "ff_proj": ff_proj, "ff_out": ff_out, "segments": segments, "pad_mask": pad_mask, "positions": positions, "cotangent": cotangent}


EPSILON = 1e-05
NEGATIVE = -1e+30
ROPE_BASE = 10000.0

@jax.custom_vjp
def low(v):
    return lax.optimization_barrier(v.astype(jnp.bfloat16)).astype(jnp.float32)

@jax.custom_vjp
def low_back(v):
    return v

def low_keep(v):
    return (low(v), None)

def low_pass(kept, grad):
    return (grad,)

def back_keep(v):
    return (v, None)

def back_low(kept, grad):
    return (low(grad),)
low.defvjp(low_keep, low_pass)
low_back.defvjp(back_keep, back_low)

def layer_norm(values):
    average = lax.optimization_barrier(jnp.mean(values, axis=-1, keepdims=True))
    centered = values - average
    variance = lax.optimization_barrier(jnp.mean(centered * centered, axis=-1, keepdims=True))
    return centered * lax.rsqrt(variance + EPSILON)

def rope_tables(positions, size):
    half_size = size // 2
    frequency = ROPE_BASE ** (-(jnp.arange(half_size, dtype=jnp.float32) * 2.0 / size))
    angles = positions.astype(jnp.float32)[:, None] * frequency[None, :]
    cosine = jnp.concatenate([jnp.cos(angles), jnp.cos(angles)], axis=-1)
    sine_part = jnp.concatenate([jnp.sin(angles), jnp.sin(angles)], axis=-1)
    return (cosine[:, None, :], sine_part[:, None, :])

def rotate(values, cosine, sine_part):
    half_size = values.shape[-1] // 2
    turned = jnp.concatenate([-values[..., half_size:], values[..., :half_size]], axis=-1)
    return values * cosine + turned * sine_part

def visible(query_place, key_place, query_doc, key_doc, key_live):
    distance = query_place[:, None] - key_place[None, :]
    same_doc = query_doc[:, None] == key_doc[None, :]
    live_key = (key_live[None, :] == 1) | (distance == 0)
    return (distance >= 0) & (distance < WINDOW) & same_doc & live_key

def sequence_attention(pieces):
    query_rot, key_rot, value_low, segment, padding = pieces
    raw_scores = jnp.einsum('qhd,khd->hqk', query_rot, key_rot, precision=lax.Precision.HIGHEST)
    scores = low_back(raw_scores) * HD ** (-0.5)
    places = jnp.arange(SEQ_LEN, dtype=jnp.int32)
    allowed = visible(places, places, segment, segment, padding)
    scores = jnp.where(allowed[None], scores, NEGATIVE)
    row_max = lax.optimization_barrier(jnp.max(scores, axis=-1, keepdims=True))
    weights = jnp.exp(scores - row_max)
    probability = weights / lax.optimization_barrier(jnp.sum(weights, axis=-1, keepdims=True))
    return jnp.einsum('hqk,khd->qhd', low(probability), value_low, precision=lax.Precision.HIGHEST)

def layer(x_float, w_attn, w_heads, w_ffn, w_down, segments, pad_mask, positions):
    tokens = x_float.shape[0]
    seq_total = tokens // SEQ_LEN
    groups = N_TP
    head_cols = D // groups
    ffn_cols = FF // groups
    normed_low = low(layer_norm(x_float))
    project_parts = []
    for group_index in range(groups):
        share = low_back(normed_low)
        weight_part = w_attn[:, :, group_index * head_cols:(group_index + 1) * head_cols].reshape(D, 3 * head_cols)
        product = jnp.dot(share, weight_part, precision=lax.Precision.HIGHEST)
        project_parts.append(product.reshape(tokens, 3, head_cols))
    project = jnp.concatenate(project_parts, axis=2).reshape(tokens, 3, HEADS, HD)
    cosine, sine_part = rope_tables(positions, HD)
    query_rot = low(rotate(low_back(project[:, 0]), cosine, sine_part))
    key_rot = low(rotate(low_back(project[:, 1]), cosine, sine_part))
    value_low = low(low_back(project[:, 2]))

    def split_seq(values):
        return values.reshape((seq_total, SEQ_LEN) + values.shape[1:])
    head_out = lax.map(jax.checkpoint(sequence_attention), (split_seq(query_rot), split_seq(key_rot), split_seq(value_low), split_seq(segments), split_seq(pad_mask)))
    heads_low = low(low_back(head_out.reshape(tokens, D)))
    resid = x_float + low_back(jnp.dot(heads_low, w_heads, precision=lax.Precision.HIGHEST))
    normed_two_low = low(layer_norm(resid))
    branch = jnp.zeros((tokens, D), jnp.float32)
    for group_index in range(groups):
        share = low_back(normed_two_low)
        weight_part = w_ffn[:, :, group_index * ffn_cols:(group_index + 1) * ffn_cols].reshape(D, 2 * ffn_cols)
        projected = jnp.dot(share, weight_part, precision=lax.Precision.HIGHEST).reshape(tokens, 2, ffn_cols)
        up_value = low_back(projected[:, 0])
        gate_value = low_back(projected[:, 1])
        hidden_low = low(jax.nn.silu(gate_value) * up_value)
        down_part = w_down[group_index * ffn_cols:(group_index + 1) * ffn_cols]
        branch = branch + low(jnp.dot(hidden_low, down_part, precision=lax.Precision.HIGHEST))
    return resid + low_back(branch)

def reference(inputs, att_proj, attn_out, ff_proj, ff_out, segments, pad_mask, positions, cotangent):

    def forward(x_float, w_attn, w_heads, w_ffn, w_down):
        return layer(x_float, w_attn, w_heads, w_ffn, w_down, segments, pad_mask, positions)
    primal = (inputs.astype(jnp.float32), att_proj.astype(jnp.float32), attn_out.astype(jnp.float32), ff_proj.astype(jnp.float32), ff_out.astype(jnp.float32))
    result, pullback = jax.vjp(forward, *primal)
    gradients = pullback(cotangent.astype(jnp.float32))
    return (result.astype(jnp.bfloat16), gradients[0].astype(jnp.bfloat16), gradients[1], gradients[2], gradients[3], gradients[4])
```

```python
import functools
import math

import jax
import jax.numpy as jnp
from jax import lax
from jax.experimental import pallas as pl
from jax.experimental.pallas import tpu as pltpu
from jax.sharding import PartitionSpec as P

HD = 128
WINDOW = 1024
SEQ_LEN = 2048
EPSILON = 1e-05
NEGATIVE = -1e30
ROPE_BASE = 10000.0
LOG2E = math.log2(math.e)
VMEM_LIMIT = 56 * 1024 * 1024
F32 = jnp.float32
BF16 = jnp.bfloat16


def dot_nn(left, right):
    return lax.dot_general(left, right, (((1,), (0,)), ((), ())), preferred_element_type=F32)


def dot_nt(left, right):
    return lax.dot_general(left, right, (((1,), (1,)), ((), ())), preferred_element_type=F32)


def dot_tn(left, right):
    return lax.dot_general(left, right, (((0,), (0,)), ((), ())), preferred_element_type=F32)


def layer_norm(values):
    average = jnp.mean(values, axis=-1, keepdims=True)
    centered = values - average
    variance = jnp.mean(centered * centered, axis=-1, keepdims=True)
    return centered * lax.rsqrt(variance + EPSILON)


def layer_norm_back(values, grad):
    average = jnp.mean(values, axis=-1, keepdims=True)
    centered = values - average
    variance = jnp.mean(centered * centered, axis=-1, keepdims=True)
    root = lax.rsqrt(variance + EPSILON)
    normed = centered * root
    inner = jnp.mean(normed * grad, axis=-1, keepdims=True)
    return root * (grad - jnp.mean(grad, axis=-1, keepdims=True) - normed * inner)


def rope_tables(positions):
    half = HD // 2
    frequency = ROPE_BASE ** (-(jnp.arange(half, dtype=F32) * 2.0 / HD))
    angles = positions.astype(F32)[:, None] * frequency[None, :]
    cosine, sine = jnp.cos(angles), jnp.sin(angles)
    return jnp.concatenate([cosine, cosine], axis=-1), jnp.concatenate([-sine, sine], axis=-1)


def project_kernel(x_ref, w_ref, cos_ref, sin_ref, out_ref):
    product = dot_nn(x_ref[...], w_ref[...])
    width = product.shape[1] // 3
    for column in range(0, 3 * width, HD):
        part = product[:, column : column + HD]
        if column < 2 * width:
            part = part * cos_ref[...] + pltpu.roll(part, HD // 2, 1) * sin_ref[...]
        out_ref[:, column : column + HD] = part.astype(BF16)


def project(x, w, cosine, sine):
    tokens, model = x.shape
    width = w.shape[1]
    block = min(512, tokens)
    return pl.pallas_call(
        project_kernel,
        grid=(tokens // block,),
        in_specs=[
            pl.BlockSpec((block, model), lambda i: (i, 0)),
            pl.BlockSpec((model, width), lambda i: (0, 0)),
            pl.BlockSpec((block, HD), lambda i: (i, 0)),
            pl.BlockSpec((block, HD), lambda i: (i, 0)),
        ],
        out_specs=pl.BlockSpec((block, width), lambda i: (i, 0)),
        out_shape=jax.ShapeDtypeStruct((tokens, width), BF16),
        compiler_params=pltpu.CompilerParams(vmem_limit_bytes=VMEM_LIMIT),
        cost_estimate=pl.CostEstimate(
            flops=2 * tokens * model * width, bytes_accessed=2 * (tokens * model + model * width + tokens * width), transcendentals=0
        ),
        name="project",
    )(x, w, cosine, sine)


def forward_kernel(block, reach, g_ref, q_ref, k_ref, v_ref, seg_ref, key_ref, out_ref, lse_ref):
    i = pl.program_id(1)
    g = g_ref[0]
    scale = LOG2E / math.sqrt(HD)

    def run(count):
        q = q_ref[...]
        row = lax.broadcasted_iota(jnp.int32, (block, block), 0)
        column = lax.broadcasted_iota(jnp.int32, (block, block), 1)
        scores, rows = [], []
        for back in range(count):
            b = i - back
            rows.append(pl.ds(pl.multiple_of((b ^ g) * block, block), block))
            keep = seg_ref[0] == key_ref[b]
            if back == 0:
                keep = (keep & (row > column)) | (row == column)
            if back == reach:
                keep = keep & (row < column)
            scores.append(jnp.where(keep, dot_nt(q, k_ref[rows[-1], :]) * scale, NEGATIVE))
        top = functools.reduce(jnp.maximum, [jnp.max(s, axis=1, keepdims=True) for s in scores])
        weights = [jnp.exp2(s - top) for s in scores]
        total = sum(jnp.sum(w, axis=1, keepdims=True) for w in weights)
        out = sum(dot_nn(w.astype(BF16), v_ref[r, :]) for w, r in zip(weights, rows))
        out_ref[...] = (out / total).astype(BF16)
        lse = top + jnp.log2(total)
        lse_ref[0, 0] = jnp.transpose(jnp.broadcast_to(lse, (block, HD)))[0:1, :]

    for i_here in range(reach):
        pl.when(i == i_here)(functools.partial(run, i_here + 1))
    pl.when(i >= reach)(functools.partial(run, reach + 1))


def attend_forward(qkv, place, segment, key_code, block):
    tokens, width = qkv.shape
    heads = width // 3 // HD
    count = tokens // block
    reach = WINDOW // block
    pairs = sum(min(i, reach) + 1 for i in range(count)) * block * block * heads
    return pl.pallas_call(
        functools.partial(forward_kernel, block, reach),
        grid_spec=pltpu.PrefetchScalarGridSpec(
            num_scalar_prefetch=1,
            grid=(heads, count),
            in_specs=[
                pl.BlockSpec((block, HD), lambda h, i, g: (i ^ g[0], h)),
                pl.BlockSpec((tokens, HD), lambda h, i, g: (0, heads + h)),
                pl.BlockSpec((tokens, HD), lambda h, i, g: (0, 2 * heads + h)),
                pl.BlockSpec((1, block, 1), lambda h, i, g: (i, 0, 0)),
                pl.BlockSpec((count, 1, block), lambda h, i, g: (0, 0, 0)),
            ],
            out_specs=[
                pl.BlockSpec((block, HD), lambda h, i, g: (i ^ g[0], h)),
                pl.BlockSpec((1, 1, 1, block), lambda h, i, g: (h, i, 0, 0)),
            ],
        ),
        out_shape=[
            jax.ShapeDtypeStruct((tokens, heads * HD), BF16),
            jax.ShapeDtypeStruct((heads, count, 1, block), F32),
        ],
        compiler_params=pltpu.CompilerParams(vmem_limit_bytes=VMEM_LIMIT),
        cost_estimate=pl.CostEstimate(flops=8 * pairs * HD, bytes_accessed=8 * tokens * heads * HD, transcendentals=pairs),
        name="attend_forward",
    )(place, qkv, qkv, qkv, segment.reshape(count, block, 1), key_code.reshape(count, 1, block))


def backward_kernel(
    block, reach, heads, g_ref, q_ref, k_ref, v_ref, grad_ref, out_ref, lse_ref, seg_ref, key_ref, cos_ref, sin_ref, result_ref, dq_ref, dk_ref, dv_ref, inner_ref
):
    h = pl.program_id(0)
    g = g_ref[0]
    count = q_ref.shape[0] // block
    scale = 1.0 / math.sqrt(HD)

    def rows_of(b):
        return pl.ds(pl.multiple_of((b ^ g) * block, block), block)

    dq_ref[...] = jnp.zeros_like(dq_ref)
    dk_ref[...] = jnp.zeros_like(dk_ref)
    dv_ref[...] = jnp.zeros_like(dv_ref)

    def inner_block(i, carry):
        rows = rows_of(i)
        product = grad_ref[rows, :].astype(F32) * out_ref[rows, :].astype(F32)
        inner_ref[i] = jnp.sum(jnp.transpose(product), axis=0, keepdims=True)
        return carry

    lax.fori_loop(0, count, inner_block, 0)
    for back in range(reach + 1):

        def pair(i, carry, back=back):
            b = i - back
            query_rows, key_rows = rows_of(i), rows_of(b)
            q, k = q_ref[query_rows, :], k_ref[key_rows, :]
            v, grad = v_ref[key_rows, :], grad_ref[query_rows, :]
            keep = key_ref[b] == seg_ref[i]
            if back == 0 or back == reach:
                key = lax.broadcasted_iota(jnp.int32, (block, block), 0)
                query = lax.broadcasted_iota(jnp.int32, (block, block), 1)
                if back == 0:
                    keep = (keep & (query > key)) | (query == key)
                else:
                    keep = keep & (query < key)
            scores = dot_nt(k, q) * (scale * LOG2E)
            weights = jnp.where(keep, jnp.exp2(scores - lse_ref[0, i]), 0.0)
            grad_weights = dot_nt(v, grad)
            grad_scores = (weights * (grad_weights - inner_ref[i]) * scale).astype(BF16)
            dv_ref[key_rows, :] += dot_nn(weights.astype(BF16), grad)
            dk_ref[key_rows, :] += dot_nn(grad_scores, q)
            dq_ref[query_rows, :] += dot_tn(grad_scores, k)
            return carry

        lax.fori_loop(back, count, pair, 0)

    column = pl.multiple_of(h * HD, HD)

    def store(i, carry):
        rows = pl.ds(pl.multiple_of(i * block, block), block)
        cosine, sine = cos_ref[rows, :], sin_ref[rows, :]
        for part, ref in enumerate((dq_ref, dk_ref)):
            value = ref[rows, :]
            turned = value * cosine - pltpu.roll(value, HD // 2, 1) * sine
            result_ref[rows, pl.ds(part * heads * HD + column, HD)] = turned.astype(BF16)
        result_ref[rows, pl.ds(2 * heads * HD + column, HD)] = dv_ref[rows, :].astype(BF16)
        return carry

    lax.fori_loop(0, count, store, 0)


def attend_backward(qkv, grad, out, lse, place, segment, key_code, cosine, sine, block):
    tokens, width = qkv.shape
    heads = width // 3 // HD
    count = tokens // block
    reach = WINDOW // block
    pairs = sum(min(i, reach) + 1 for i in range(count)) * block * block * heads
    return pl.pallas_call(
        functools.partial(backward_kernel, block, reach, heads),
        grid_spec=pltpu.PrefetchScalarGridSpec(
            num_scalar_prefetch=1,
            grid=(heads,),
            in_specs=[
                pl.BlockSpec((tokens, HD), lambda h, g: (0, h)),
                pl.BlockSpec((tokens, HD), lambda h, g: (0, heads + h)),
                pl.BlockSpec((tokens, HD), lambda h, g: (0, 2 * heads + h)),
                pl.BlockSpec((tokens, HD), lambda h, g: (0, h)),
                pl.BlockSpec((tokens, HD), lambda h, g: (0, h)),
                pl.BlockSpec((1, count, 1, block), lambda h, g: (h, 0, 0, 0)),
                pl.BlockSpec((count, 1, block), lambda h, g: (0, 0, 0)),
                pl.BlockSpec((count, block, 1), lambda h, g: (0, 0, 0)),
                pl.BlockSpec((tokens, HD), lambda h, g: (0, 0)),
                pl.BlockSpec((tokens, HD), lambda h, g: (0, 0)),
            ],
            out_specs=pl.BlockSpec((tokens, width), lambda h, g: (0, 0)),
            scratch_shapes=[
                pltpu.VMEM((tokens, HD), F32),
                pltpu.VMEM((tokens, HD), F32),
                pltpu.VMEM((tokens, HD), F32),
                pltpu.VMEM((count, 1, block), F32),
            ],
        ),
        out_shape=jax.ShapeDtypeStruct((tokens, width), BF16),
        compiler_params=pltpu.CompilerParams(vmem_limit_bytes=VMEM_LIMIT),
        cost_estimate=pl.CostEstimate(flops=20 * pairs * HD, bytes_accessed=16 * tokens * heads * HD, transcendentals=pairs),
        name="attend_backward",
    )(
        place, qkv, qkv, qkv, grad, out, lse,
        segment.reshape(count, 1, block), key_code.reshape(count, block, 1), cosine, sine,
    )


def local(inputs, att_proj, attn_out, ff_proj, ff_out, segments, pad_mask, positions, cotangent):
    tp_size = lax.axis_size("tp")
    rows, model = inputs.shape
    members = SEQ_LEN // rows
    sets = tp_size // members
    index = lax.axis_index("tp")
    mine = index // members
    place = index % members
    head_width = att_proj.shape[2]
    ffn_width = ff_proj.shape[2]
    block = min(512, rows)

    def swap(values, bit):
        return lax.ppermute(values, "tp", [(i, i ^ bit) for i in range(tp_size)])

    def turn(values, step):
        return lax.ppermute(values, "tp", [(i, (i + step * members) % tp_size) for i in range(tp_size)])

    def group_gather(values):
        blocks = {0: values}
        bit = members // 2
        while bit:
            for mask in sorted(blocks, reverse=True):
                blocks[mask | bit] = swap(blocks[mask], bit)
            bit //= 2
        return [blocks[mask] for mask in range(members)]

    def group_scatter(blocks):
        blocks = dict(enumerate(blocks))
        bit = 1
        while bit < members:
            for mask in sorted((m for m in blocks if m & bit), reverse=True):
                total = blocks[mask ^ bit].astype(F32) + swap(blocks.pop(mask), bit).astype(F32)
                blocks[mask ^ bit] = total if mask == bit else total.astype(BF16)
            bit *= 2
        return blocks[0].astype(F32)

    def spread(shard, gather):
        parts = [shard] + [turn(shard, step) for step in range(1, sets)]
        return [gather(part) for part in parts]

    def gather_first(part):
        return lax.all_gather(part, "fsdp", axis=0, tiled=True)

    def gather_new(part):
        return lax.all_gather(part, "fsdp", axis=0)

    def settle(parts, scatter):
        total = None
        for step in range(sets):
            piece = scatter(parts[step])
            if step:
                piece = turn(piece, sets - step)
            piece = piece.astype(F32)
            total = piece if total is None else total + piece
        return total

    def scatter_first(part):
        return lax.psum_scatter(part.astype(BF16), "fsdp", scatter_dimension=0, tiled=True)

    def scatter_last(part):
        return lax.psum_scatter(part.astype(BF16), "fsdp", scatter_dimension=1, tiled=True)

    w_qkv = spread(att_proj.reshape(att_proj.shape[0], 3 * head_width), gather_first)
    w_heads = spread(attn_out, gather_new)
    w_ffn = spread(ff_proj.reshape(ff_proj.shape[0], 2 * ffn_width), gather_first)
    w_down = spread(ff_out, gather_new)

    def flat(chunks):
        return jnp.concatenate([chunks[f] for f in range(chunks.shape[0])], axis=1)

    w_heads = jnp.concatenate([flat(part) for part in w_heads], axis=0)
    w_down = jnp.concatenate([flat(part) for part in w_down], axis=0)

    segment = lax.dynamic_slice_in_dim(segments, mine * SEQ_LEN, SEQ_LEN)
    padding = lax.dynamic_slice_in_dim(pad_mask, mine * SEQ_LEN, SEQ_LEN)
    key_code = jnp.where(padding == 1, segment, -1)
    spots = lax.dynamic_slice_in_dim(positions, mine * SEQ_LEN, SEQ_LEN).reshape(members, rows)
    spots = jnp.concatenate([lax.dynamic_index_in_dim(spots, place ^ mask, 0, False) for mask in range(members)])
    cosine, sine = rope_tables(spots)
    where = place.astype(jnp.int32).reshape(1)

    x_float = inputs.astype(F32)
    normed_all = jnp.concatenate(group_gather(layer_norm(x_float).astype(BF16)), axis=0)
    cotangent_all = jnp.concatenate(group_gather(cotangent), axis=0)

    qkv = [project(normed_all, w, cosine, sine) for w in w_qkv]
    attended = [attend_forward(part, where, segment, key_code, block) for part in qkv]
    heads_low = jnp.concatenate([out for out, _ in attended], axis=1)

    def row_blocks(left, right, dot):
        return [dot(left[m * rows : (m + 1) * rows], right).astype(BF16) for m in range(members)]

    resid = x_float + group_scatter(row_blocks(heads_low, w_heads, dot_nn))
    normed_two_all = jnp.concatenate(group_gather(layer_norm(resid).astype(BF16)), axis=0)

    projected = [dot_nn(normed_two_all, w) for w in w_ffn]
    up = jnp.concatenate([p[:, :ffn_width] for p in projected], axis=1)
    gate = jnp.concatenate([p[:, ffn_width:] for p in projected], axis=1)
    sigmoid = jax.nn.sigmoid(gate)
    slope_up = gate * sigmoid
    slope_gate = up * sigmoid * (1.0 + gate * (1.0 - sigmoid))
    hidden_low = (slope_up * up).astype(BF16)
    ffn_branch = group_scatter(row_blocks(hidden_low, w_down, dot_nn))
    output = (resid + ffn_branch).astype(BF16)

    grad_hidden = dot_nt(cotangent_all, w_down)
    grad_down = dot_tn(hidden_low, cotangent_all)
    grad_up = (grad_hidden * slope_up).astype(BF16)
    grad_gate = (grad_hidden * slope_gate).astype(BF16)
    grad_ffn_low = [
        jnp.concatenate([part[:, j * ffn_width : (j + 1) * ffn_width] for part in (grad_up, grad_gate)], axis=1)
        for j in range(sets)
    ]
    grad_ffn_all = jnp.concatenate(grad_ffn_low, axis=1)
    grad_normed_two = group_scatter(row_blocks(grad_ffn_all, jnp.concatenate(w_ffn, axis=1), dot_nt))
    grad_ffn = [dot_tn(normed_two_all, part) for part in grad_ffn_low]

    grad_resid = cotangent.astype(F32) + layer_norm_back(resid, grad_normed_two)
    resid_grad_all = jnp.concatenate(group_gather(grad_resid.astype(BF16)), axis=0)
    grad_heads_weight = dot_tn(heads_low, resid_grad_all)
    head_grad = dot_nt(resid_grad_all, w_heads).astype(BF16)
    grad_project = [
        attend_backward(
            qkv[j], head_grad[:, j * head_width : (j + 1) * head_width], attended[j][0], attended[j][1],
            where, segment, key_code, cosine, sine, block,
        )
        for j in range(sets)
    ]
    grad_project_all = jnp.concatenate(grad_project, axis=1)
    grad_normed = group_scatter(row_blocks(grad_project_all, jnp.concatenate(w_qkv, axis=1), dot_nt))
    grad_attn = [dot_tn(normed_all, part) for part in grad_project]
    grad_input = (grad_resid + layer_norm_back(x_float, grad_normed)).astype(BF16)

    def halves(values, width):
        return [values[j * width : (j + 1) * width] for j in range(sets)]

    return (
        output,
        grad_input,
        settle(grad_attn, scatter_first).reshape(att_proj.shape),
        settle(halves(grad_heads_weight, head_width), scatter_last),
        settle(grad_ffn, scatter_first).reshape(ff_proj.shape),
        settle(halves(grad_down, ffn_width), scatter_last),
    )


def solution(mesh):
    rows_spec = P(("fsdp", "tp"), None)
    weights = (P("fsdp", None, "tp"), P("tp", "fsdp"), P("fsdp", None, "tp"), P("tp", "fsdp"))
    return jax.shard_map(
        local,
        mesh=mesh,
        in_specs=(rows_spec,) + weights + (P("fsdp"),) * 3 + (rows_spec,),
        out_specs=(rows_spec, rows_spec) + weights,
        check_vma=False,
    )
```

```python
import functools
import math

import jax
import jax.numpy as jnp
from jax import lax
from jax.experimental import pallas as pl
from jax.experimental.pallas import tpu as pltpu
from jax.sharding import PartitionSpec as P

HD = 128
WINDOW = 1024
SEQ_LEN = 2048
EPSILON = 1e-05
NEGATIVE = -1e30
ROPE_BASE = 10000.0
LOG2E = math.log2(math.e)
VMEM_LIMIT = 56 * 1024 * 1024
F32 = jnp.float32
BF16 = jnp.bfloat16


def dot_nn(left, right):
    return lax.dot_general(left, right, (((1,), (0,)), ((), ())), preferred_element_type=F32)


def dot_nt(left, right):
    return lax.dot_general(left, right, (((1,), (1,)), ((), ())), preferred_element_type=F32)


def dot_tn(left, right):
    return lax.dot_general(left, right, (((0,), (0,)), ((), ())), preferred_element_type=F32)


def layer_norm(values):
    average = jnp.mean(values, axis=-1, keepdims=True)
    centered = values - average
    variance = jnp.mean(centered * centered, axis=-1, keepdims=True)
    return centered * lax.rsqrt(variance + EPSILON)


def layer_norm_back(values, grad):
    average = jnp.mean(values, axis=-1, keepdims=True)
    centered = values - average
    variance = jnp.mean(centered * centered, axis=-1, keepdims=True)
    root = lax.rsqrt(variance + EPSILON)
    normed = centered * root
    inner = jnp.mean(normed * grad, axis=-1, keepdims=True)
    return root * (grad - jnp.mean(grad, axis=-1, keepdims=True) - normed * inner)


def rope_tables(positions):
    half = HD // 2
    frequency = ROPE_BASE ** (-(jnp.arange(half, dtype=F32) * 2.0 / HD))
    angles = positions.astype(F32)[:, None] * frequency[None, :]
    cosine, sine = jnp.cos(angles), jnp.sin(angles)
    return jnp.concatenate([cosine, cosine], axis=-1), jnp.concatenate([-sine, sine], axis=-1)


def kernel_call(kernel, name, grid, in_specs, out_specs, out_shapes, scratch, aliases={}):
    return pl.pallas_call(
        kernel,
        grid_spec=pltpu.PrefetchScalarGridSpec(
            num_scalar_prefetch=1, grid=grid, in_specs=in_specs, out_specs=out_specs, scratch_shapes=scratch
        ),
        out_shape=out_shapes,
        input_output_aliases=aliases,
        compiler_params=pltpu.CompilerParams(vmem_limit_bytes=VMEM_LIMIT),
        cost_estimate=pl.CostEstimate(flops=1, bytes_accessed=1, transcendentals=0),
        name=name,
    )


def any_specs(arrays):
    return [pl.BlockSpec(memory_space=pl.ANY)] * len(arrays)


def slot(index, size):
    return pl.ds(pl.multiple_of(index * size, size), size)


def start_kernel(members, sets, count, x_ref, pack_ref, *refs):
    normed, refs = refs[:members], refs[members:]
    packs = [(pack_ref,) + refs[: count - 1]]
    refs = refs[count - 1 :]
    for _ in range(1, sets):
        packs.append(refs[:count])
        refs = refs[count:]
    low_ref, local_sem, send_sem, recv_sem = refs
    t, f = lax.axis_index("tp"), lax.axis_index("fsdp")
    total = members * sets
    climb = [1 << i for i in range(count.bit_length() - 1)]
    group = [1 << i for i in range(members.bit_length() - 1)][::-1]
    shifts = [lax.rem(t + step * members, total) for step in range(1, sets)]

    barrier = pltpu.get_barrier_semaphore()
    partners = [{"tp": t ^ bit} for bit in group] + [{"tp": s} for s in shifts] + [{"fsdp": f ^ bit} for bit in climb]
    for partner in partners:
        pl.semaphore_signal(barrier, inc=1, device_id=partner, device_id_type=pl.DeviceIdType.MESH)
    pl.semaphore_wait(barrier, len(partners))

    started, waited = [], []

    def send(src, dst, partner):
        n = len(started)
        copy = pltpu.make_async_remote_copy(
            src_ref=src,
            dst_ref=dst,
            send_sem=send_sem.at[n],
            recv_sem=recv_sem.at[n],
            device_id=partner,
            device_id_type=pl.DeviceIdType.MESH,
        )
        copy.start()
        started.append(copy)
        return copy

    def await_block(copy):
        copy.wait_recv()
        waited.append(copy)

    orders = (climb, climb[::-1])
    size = pack_ref.shape[0] // 2
    came = [{} for _ in range(sets)]

    def pass_on(step, half, mask):
        order = orders[half]
        here = pl.ds(half * size, size)
        for n, bit in enumerate(order):
            if all(not mask & later for later in order[n:]):
                copy = send(packs[step][mask].at[here, :], packs[step][mask | bit].at[here, :], {"fsdp": f ^ bit})
                came[step][half, mask | bit] = copy

    def pass_all(step):
        for level in range(1, len(climb)):
            for half in range(2):
                for mask in range(count):
                    if mask.bit_count() == level and not mask & orders[half][-1]:
                        await_block(came[step][half, mask])
                        pass_on(step, half, mask)

    over = [send(pack_ref, packs[step][0], {"tp": shifts[step - 1]}) for step in range(1, sets)]
    for half in range(2):
        pass_on(0, half, 0)

    rows = x_ref.shape[0]
    tile = min(32, rows)

    def norm(i, carry):
        here = pl.ds(pl.multiple_of(i * tile, tile), tile)
        low_ref[here, :] = layer_norm(x_ref[here, :].astype(F32)).astype(BF16)
        return carry

    lax.fori_loop(0, rows // tile, norm, 0)
    keep = pltpu.make_async_copy(low_ref, normed[0], local_sem)
    keep.start()
    blocks = {}
    for bit in group:
        blocks[bit] = send(low_ref, normed[bit], {"tp": t ^ bit})
    pass_all(0)
    for step in range(1, sets):
        await_block(over[step - 1])
        for half in range(2):
            pass_on(step, half, 0)
        pass_all(step)
    for mask in sorted(range(1, members), reverse=True, key=lambda m: (m & -m, m)):
        below = [bit for bit in group if bit < mask & -mask]
        if below:
            await_block(blocks[mask])
        for bit in below:
            blocks[mask | bit] = send(normed[mask], normed[mask | bit], {"tp": t ^ bit})
    keep.wait()
    for copy in started:
        copy.wait_send()
        if not any(copy is other for other in waited):
            copy.wait_recv()


def start_exchange(x, pack, members, sets, count):
    sends = 2 * (count - 1) * sets + (members - 1) + (sets - 1)
    shapes = [jax.ShapeDtypeStruct(x.shape, BF16)] * members + [jax.ShapeDtypeStruct(pack.shape, BF16)] * (count * sets - 1)
    outs = pl.pallas_call(
        functools.partial(start_kernel, members, sets, count),
        in_specs=[pl.BlockSpec(memory_space=pltpu.VMEM), pl.BlockSpec(memory_space=pl.ANY)],
        out_specs=any_specs(shapes),
        out_shape=shapes,
        scratch_shapes=[
            pltpu.VMEM(x.shape, BF16),
            pltpu.SemaphoreType.DMA,
            pltpu.SemaphoreType.DMA((sends,)),
            pltpu.SemaphoreType.DMA((sends,)),
        ],
        compiler_params=pltpu.CompilerParams(vmem_limit_bytes=VMEM_LIMIT, collective_id=0, has_side_effects=True),
        cost_estimate=pl.CostEstimate(flops=1, bytes_accessed=1, transcendentals=0),
        name="start_exchange",
    )(x, pack)
    packs = [pack] + list(outs[members:])
    return outs[:members], [packs[step * count : (step + 1) * count] for step in range(sets)]


def rows_kernel(body, plan, members, extras, count, f_ref, *refs):
    xs, refs = refs[:members], refs[members:]
    extra_refs, refs = refs[:extras], refs[extras:]
    weights, refs = refs[:count], refs[count:]
    outs, (x_buf, w_buf, x_sem, w_sem) = refs[:-4], refs[-4:]
    i, f = pl.program_id(0), f_ref[0]
    moves, use = plan
    tiles = [
        [pltpu.make_async_copy(src, dst, w_sem.at[t, n]) for n, (src, dst) in enumerate(pairs)]
        for t, pairs in enumerate(moves(weights, w_buf, f))
    ]
    x_copies = [pltpu.make_async_copy(x, x_buf.at[m], x_sem.at[m]) for m, x in enumerate(xs)]

    @pl.when(i == 0)
    def _():
        x_copies[0].start()
        for copies in tiles:
            for copy in copies:
                copy.start()
        for copy in x_copies[1:]:
            copy.start()

    def run(first):
        pltpu.make_async_copy(xs[0], x_buf.at[i], x_sem.at[i]).wait()
        for t, copies in enumerate(tiles):
            if first:
                for copy in copies:
                    copy.wait()
            body(t, use(t, x_buf[i], w_buf), extra_refs, outs)

    pl.when(i == 0)(functools.partial(run, True))
    pl.when(i > 0)(functools.partial(run, False))


def rows_call(body, name, place, xs, extras, weights, plan, tiles, copies, w_shape, widths):
    rows, model = xs[0].shape
    members, count = len(xs), len(weights)
    return kernel_call(
        functools.partial(rows_kernel, body, plan, members, len(extras), count),
        name,
        (members,),
        any_specs(xs) + [pl.BlockSpec((rows, e.shape[1]), lambda i, f: (i, 0)) for e in extras] + any_specs(weights),
        [pl.BlockSpec((rows, width), lambda i, f: (i, 0)) for width in widths],
        [jax.ShapeDtypeStruct((members * rows, width), BF16) for width in widths],
        [
            pltpu.VMEM((members, rows, model), BF16),
            pltpu.VMEM(w_shape, BF16),
            pltpu.SemaphoreType.DMA((members,)),
            pltpu.SemaphoreType.DMA((tiles, copies)),
        ],
    )(place, *xs, *extras, *weights)


def project(place, xs, packs, cosine, sine):
    model, count = xs[0].shape[1], len(packs)
    depth, width = model // count, packs[0].shape[1]

    def moves(packs, w_buf, f):
        return [
            [(pack.at[t * depth : (t + 1) * depth, :], w_buf.at[t, slot(f ^ c, depth), :]) for c, pack in enumerate(packs)]
            for t in range(3)
        ]

    def use(t, x, w_buf):
        return dot_nn(x, w_buf[t])

    def body(t, product, extras, outs):
        for column in range(0, width, HD):
            value = product[:, column : column + HD]
            if t < 2:
                value = value * extras[0][...] + pltpu.roll(value, HD // 2, 1) * extras[1][...]
            outs[0][:, t * width + column : t * width + column + HD] = value.astype(BF16)

    return rows_call(
        body, "project", place, xs, [cosine, sine], packs, (moves, use), 3, count, (3, model, width), [3 * width]
    )[0]


def head_grad_of(place, xs, packs):
    model, count = xs[0].shape[1], len(packs)
    depth, width = model // count, packs[0].shape[1]
    squares = depth // width

    def moves(packs, w_buf, f):
        return [
            [
                (
                    pack.at[3 * depth + b * width : 3 * depth + (b + 1) * width, :],
                    w_buf.at[:, slot((f ^ c) * squares + b, width)],
                )
                for c, pack in enumerate(packs)
                for b in range(squares)
            ]
        ]

    def use(t, x, w_buf):
        return dot_nt(x, w_buf[...])

    def body(t, product, extras, outs):
        outs[0][...] = product.astype(BF16)

    return rows_call(
        body, "head_grad", place, xs, [], packs, (moves, use), 1, count * squares, (width, model), [width]
    )[0]


def hidden_units(place, xs, stack):
    model = xs[0].shape[1]
    count, depth, width = stack.shape
    width //= 2
    tile = min(256, width)
    starts = range(0, width, tile)

    def moves(weights, w_buf, f):
        return [
            [
                (weights[0].at[c, :, s : s + tile], w_buf.at[c * depth : (c + 1) * depth, s : s + tile])
                for c in range(count)
                for s in (start, width + start)
            ]
            for start in starts
        ]

    def use(t, x, w_buf):
        return [dot_nn(x, w_buf[:, s : s + tile]) for s in (starts[t], width + starts[t])]

    def body(t, products, extras, outs):
        here = pl.ds(starts[t], tile)
        up, gate = products
        sigmoid = 1.0 / (1.0 + jnp.exp(-gate))
        slope_up = gate * sigmoid
        outs[0][:, here] = (slope_up * up).astype(BF16)
        outs[1][:, here] = slope_up.astype(BF16)
        outs[2][:, here] = (up * sigmoid * (1.0 + gate * (1.0 - sigmoid))).astype(BF16)

    return rows_call(
        body, "hidden_units", place, xs, [], [stack], (moves, use), len(starts), 2 * count, (model, 2 * width), [width] * 3
    )


def hidden_grad(place, xs, slope_up, slope_gate, stack):
    model = xs[0].shape[1]
    count, width, depth = stack.shape
    tile = min(512, width)
    starts = range(0, width, tile)

    def moves(weights, w_buf, f):
        return [
            [
                (weights[0].at[c, s : s + tile, :], w_buf.at[s : s + tile, c * depth : (c + 1) * depth])
                for c in range(count)
            ]
            for s in starts
        ]

    def use(t, x, w_buf):
        return dot_nt(x, w_buf[starts[t] : starts[t] + tile, :])

    def body(t, product, extras, outs):
        here = pl.ds(starts[t], tile)
        outs[0][:, here] = (product * extras[0][:, here].astype(F32)).astype(BF16)
        outs[0][:, pl.ds(width + starts[t], tile)] = (product * extras[1][:, here].astype(F32)).astype(BF16)

    return rows_call(
        body, "hidden_grad", place, xs, [slope_up, slope_gate], [stack], (moves, use),
        len(starts), count, (width, model), [2 * width],
    )[0]


def expand_kernel(sets, each, plan, dot, with_base, parts, f_ref, *refs):
    xs, refs = refs[:sets], refs[sets:]
    bases, refs = (refs[:1], refs[1:]) if with_base else ((), refs)
    weights, refs = refs[: sets * each], refs[sets * each :]
    outs, (w_buf, sem) = refs[:parts], refs[parts:]
    d, f = pl.program_id(0), f_ref[0]
    count = w_buf.shape[1]

    def copies(j, c):
        there, pairs = plan(weights[j * each : (j + 1) * each], c, f)
        return there, [
            pltpu.make_async_copy(src, w_buf.at[j, there, :, lanes], sem.at[j, there, n])
            for n, (src, lanes) in enumerate(pairs)
        ]

    @pl.when(d == 0)
    def _():
        for c in range(count):
            for j in range(sets):
                for copy in copies(j, c)[1]:
                    copy.start()

    for j in range(sets):
        for n, (src, lanes) in enumerate(plan(weights[j * each : (j + 1) * each], 0, f)[1]):
            pltpu.make_async_copy(src, w_buf.at[j, d, :, lanes], sem.at[j, d, n]).wait()
    rows = outs[0].shape[0]
    for p in range(parts):
        here = slice(p * rows, (p + 1) * rows)
        total = sum(dot(x[here, :], w_buf[j, d]) for j, x in enumerate(xs))
        for base in bases:
            total = total + base[here, :].astype(F32)
        outs[p][...] = total.astype(BF16)


def expand_call(name, place, xs, weights, each, plan, pieces, dot, chunk, rows, first, parts, base=None):
    count, w_shape = chunk
    depth = w_shape[1 if dot is dot_nn else 0]
    specs = [pl.BlockSpec((rows * parts, x.shape[1]), lambda d, f: (first // parts, 0)) for x in xs]
    bases = [] if base is None else [base]
    specs += [pl.BlockSpec((rows * parts, depth), lambda d, f: (first // parts, d)) for _ in bases]
    return kernel_call(
        functools.partial(expand_kernel, len(xs), each, plan, dot, base is not None, parts),
        name,
        (count,),
        specs + any_specs(weights),
        [pl.BlockSpec((rows, depth), lambda d, f: (0, d))] * parts,
        [jax.ShapeDtypeStruct((rows, count * depth), BF16)] * parts,
        [pltpu.VMEM((len(xs), count) + w_shape, BF16), pltpu.SemaphoreType.DMA((len(xs), count, pieces))],
    )(place, *xs, *bases, *weights)


def expand_stack(name, dot, place, xs, stacks, rows, first, parts, base=None):
    count, above, across = stacks[0].shape

    def plan(weights, c, f):
        return c, [(weights[0].at[c], pl.ds(0, across))]

    return expand_call(
        name, place, xs, stacks, 1, plan, 1, dot, (count, (above, across)), rows, first, parts, base
    )


def expand_heads(name, place, xs, packs, rows, first, parts):
    count, width = len(packs[0]), packs[0][0].shape[1]
    depth = packs_depth(packs[0][0])
    squares = depth // width

    def plan(weights, c, f):
        return f ^ c, [
            (weights[c].at[3 * depth + b * width : 3 * depth + (b + 1) * width, :], pl.ds(b * width, width))
            for b in range(squares)
        ]

    flat = [pack for list_ in packs for pack in list_]
    return expand_call(
        name, place, xs, flat, count, plan, squares, dot_nn, (count, (width, depth)), rows, first, parts
    )


def expand_project(name, place, xs, packs, rows, first, parts):
    count, width = len(packs[0]), packs[0][0].shape[1]
    depth = packs_depth(packs[0][0])

    def plan(weights, c, f):
        return f ^ c, [
            (weights[c].at[t * depth : (t + 1) * depth, :], pl.ds(t * width, width)) for t in range(3)
        ]

    flat = [pack for list_ in packs for pack in list_]
    return expand_call(
        name, place, xs, flat, count, plan, 3, dot_nt, (count, (depth, 3 * width)), rows, first, parts
    )


def pack_weights(att_proj, attn_out):
    depth, _, width = att_proj.shape
    parts = [att_proj[:, t, :] for t in range(3)]
    return jnp.concatenate(parts + [attn_out[:, s : s + width] for s in range(0, depth, width)], axis=0)


def packs_depth(pack):
    return pack.shape[0] // 4


def rows_grad_kernel(members, count, f_ref, *refs):
    xs, (g_ref, out_ref, x_buf, sem) = refs[:members], refs[-4:]
    rows, depth = xs[0].shape[0], xs[0].shape[1] // count
    chunks = [
        [
            pltpu.make_async_copy(
                x.at[:, d * depth : (d + 1) * depth], x_buf.at[d, m * rows : (m + 1) * rows, :], sem.at[d, m]
            )
            for m, x in enumerate(xs)
        ]
        for d in range(count)
    ]

    @pl.when(pl.program_id(0) == 0)
    def _():
        for copies in chunks:
            for copy in copies:
                copy.start()

    def run(first):
        for d, copies in enumerate(chunks):
            if first:
                for copy in copies:
                    copy.wait()
            out_ref[d] = dot_tn(x_buf[d], g_ref[...]).astype(BF16)

    pl.when(pl.program_id(0) == 0)(functools.partial(run, True))
    pl.when(pl.program_id(0) > 0)(functools.partial(run, False))


def rows_grad(name, place, count, tile, below, xs, g, stack=None):
    rows, model = xs[0].shape
    tokens, width = g.shape
    depth = model // count
    given = [] if stack is None else [stack]
    shape = (count, width // tile * depth + below, tile)
    return kernel_call(
        functools.partial(rows_grad_kernel, len(xs), count),
        name,
        (width // tile,),
        any_specs(xs) + any_specs(given) + [pl.BlockSpec((tokens, tile), lambda n, f: (0, n))],
        pl.BlockSpec((count, depth, tile), lambda n, f: (0, n, 0)),
        jax.ShapeDtypeStruct(shape, BF16),
        [pltpu.VMEM((count, tokens, depth), BF16), pltpu.SemaphoreType.DMA((count, len(xs)))],
        {1 + len(xs): 0} if given else {},
    )(place, *xs, *given, g)


def columns_grad_kernel(sets, members, f_ref, *refs):
    xs, gs = refs[:sets], refs[sets : sets + members]
    out_ref, g_buf, sem = refs[-3:]
    d = pl.program_id(0)
    rows = gs[0].shape[0]
    total, _, depth = g_buf.shape
    tile = out_ref.shape[2]

    @pl.when(d == 0)
    def _():
        for c in range(total):
            for m, g in enumerate(gs):
                src, dst = g.at[:, c * depth : (c + 1) * depth], g_buf.at[c, m * rows : (m + 1) * rows, :]
                pltpu.make_async_copy(src, dst, sem.at[c, m]).start()

    for m, g in enumerate(gs):
        src, dst = g.at[:, :depth], g_buf.at[d, m * rows : (m + 1) * rows, :]
        pltpu.make_async_copy(src, dst, sem.at[d, m]).wait()
    first = 0
    for x in xs:
        for start in range(0, x.shape[1], 512):
            size = min(512, x.shape[1] - start)
            product = dot_tn(x[:, start : start + size], g_buf[d]).astype(BF16)
            for column in range(0, depth, tile):
                row = first + column // tile * x.shape[1] + start
                out_ref[0, row : row + size, :] = product[:, column : column + tile]
        first += x.shape[1] * (depth // tile)


def columns_grad(name, place, count, tile, above, xs, gs, stack=None):
    model = gs[0].shape[1]
    tokens = xs[0].shape[0]
    depth = model // count
    below = sum(x.shape[1] for x in xs) * (depth // tile)
    given = [] if stack is None else [stack]
    return kernel_call(
        functools.partial(columns_grad_kernel, len(xs), len(gs)),
        name,
        (count,),
        [pl.BlockSpec(x.shape, lambda d, f: (0, 0)) for x in xs] + any_specs(gs) + any_specs(given),
        pl.BlockSpec((1, below, tile), lambda d, f: (d, above // below, 0)),
        jax.ShapeDtypeStruct((count, above + below, tile), BF16),
        [pltpu.VMEM((count, tokens, depth), BF16), pltpu.SemaphoreType.DMA((count, len(gs)))],
        {1 + len(xs) + len(gs): 0} if given else {},
    )(place, *xs, *gs, *given)


def forward_kernel(block, reach, g_ref, q_ref, k_ref, v_ref, seg_ref, key_ref, out_ref, lse_ref):
    i = pl.program_id(1)
    g = g_ref[0]
    scale = LOG2E / math.sqrt(HD)

    def run(count):
        q = q_ref[...]
        row = lax.broadcasted_iota(jnp.int32, (block, block), 0)
        column = lax.broadcasted_iota(jnp.int32, (block, block), 1)
        scores, rows = [], []
        for back in range(count):
            b = i - back
            rows.append(pl.ds(pl.multiple_of((b ^ g) * block, block), block))
            keep = seg_ref[0] == key_ref[b]
            if back == 0:
                keep = (keep & (row > column)) | (row == column)
            if back == reach:
                keep = keep & (row < column)
            scores.append(jnp.where(keep, dot_nt(q, k_ref[rows[-1], :]) * scale, NEGATIVE))
        top = functools.reduce(jnp.maximum, [jnp.max(s, axis=1, keepdims=True) for s in scores])
        weights = [jnp.exp2(s - top) for s in scores]
        total = sum(jnp.sum(w, axis=1, keepdims=True) for w in weights)
        out = sum(dot_nn(w.astype(BF16), v_ref[r, :]) for w, r in zip(weights, rows))
        out_ref[...] = (out / total).astype(BF16)
        lse = top + jnp.log2(total)
        lse_ref[0, 0] = jnp.transpose(jnp.broadcast_to(lse, (block, HD)))[0:1, :]

    for i_here in range(reach):
        pl.when(i == i_here)(functools.partial(run, i_here + 1))
    pl.when(i >= reach)(functools.partial(run, reach + 1))


def attend_forward(qkv, place, segment, key_code, block):
    tokens, width = qkv.shape
    heads = width // 3 // HD
    count = tokens // block
    reach = WINDOW // block
    return pl.pallas_call(
        functools.partial(forward_kernel, block, reach),
        grid_spec=pltpu.PrefetchScalarGridSpec(
            num_scalar_prefetch=1,
            grid=(heads, count),
            in_specs=[
                pl.BlockSpec((block, HD), lambda h, i, g: (i ^ g[0], h)),
                pl.BlockSpec((tokens, HD), lambda h, i, g: (0, heads + h)),
                pl.BlockSpec((tokens, HD), lambda h, i, g: (0, 2 * heads + h)),
                pl.BlockSpec((1, block, 1), lambda h, i, g: (i, 0, 0)),
                pl.BlockSpec((count, 1, block), lambda h, i, g: (0, 0, 0)),
            ],
            out_specs=[
                pl.BlockSpec((block, HD), lambda h, i, g: (i ^ g[0], h)),
                pl.BlockSpec((1, 1, 1, block), lambda h, i, g: (h, i, 0, 0)),
            ],
        ),
        out_shape=[
            jax.ShapeDtypeStruct((tokens, heads * HD), BF16),
            jax.ShapeDtypeStruct((heads, count, 1, block), F32),
        ],
        compiler_params=pltpu.CompilerParams(vmem_limit_bytes=VMEM_LIMIT),
        cost_estimate=pl.CostEstimate(flops=1, bytes_accessed=1, transcendentals=0),
        name="attend_forward",
    )(place, qkv, qkv, qkv, segment.reshape(count, block, 1), key_code.reshape(count, 1, block))


def backward_kernel(
    block, reach, heads, g_ref, q_ref, k_ref, v_ref, grad_ref, out_ref, lse_ref, seg_ref, key_ref, cos_ref, sin_ref, result_ref, dq_ref, dk_ref, dv_ref, inner_ref
):
    h = pl.program_id(0)
    g = g_ref[0]
    count = q_ref.shape[0] // block
    scale = 1.0 / math.sqrt(HD)

    def rows_of(b):
        return pl.ds(pl.multiple_of((b ^ g) * block, block), block)

    dq_ref[...] = jnp.zeros_like(dq_ref)
    dk_ref[...] = jnp.zeros_like(dk_ref)
    dv_ref[...] = jnp.zeros_like(dv_ref)

    def inner_block(i, carry):
        rows = rows_of(i)
        product = grad_ref[rows, :].astype(F32) * out_ref[rows, :].astype(F32)
        inner_ref[i] = jnp.sum(jnp.transpose(product), axis=0, keepdims=True)
        return carry

    lax.fori_loop(0, count, inner_block, 0)
    for back in range(reach + 1):

        def pair(i, carry, back=back):
            b = i - back
            query_rows, key_rows = rows_of(i), rows_of(b)
            q, k = q_ref[query_rows, :], k_ref[key_rows, :]
            v, grad = v_ref[key_rows, :], grad_ref[query_rows, :]
            keep = key_ref[b] == seg_ref[i]
            if back == 0 or back == reach:
                key = lax.broadcasted_iota(jnp.int32, (block, block), 0)
                query = lax.broadcasted_iota(jnp.int32, (block, block), 1)
                if back == 0:
                    keep = (keep & (query > key)) | (query == key)
                else:
                    keep = keep & (query < key)
            scores = dot_nt(k, q) * (scale * LOG2E)
            weights = jnp.where(keep, jnp.exp2(scores - lse_ref[0, i]), 0.0)
            grad_weights = dot_nt(v, grad)
            grad_scores = (weights * (grad_weights - inner_ref[i]) * scale).astype(BF16)
            dv_ref[key_rows, :] += dot_nn(weights.astype(BF16), grad)
            dk_ref[key_rows, :] += dot_nn(grad_scores, q)
            dq_ref[query_rows, :] += dot_tn(grad_scores, k)
            return carry

        lax.fori_loop(back, count, pair, 0)

    column = pl.multiple_of(h * HD, HD)

    def store(i, carry):
        rows = pl.ds(pl.multiple_of(i * block, block), block)
        cosine, sine = cos_ref[rows, :], sin_ref[rows, :]
        for part, ref in enumerate((dq_ref, dk_ref)):
            value = ref[rows, :]
            turned = value * cosine - pltpu.roll(value, HD // 2, 1) * sine
            result_ref[rows, pl.ds(part * heads * HD + column, HD)] = turned.astype(BF16)
        result_ref[rows, pl.ds(2 * heads * HD + column, HD)] = dv_ref[rows, :].astype(BF16)
        return carry

    lax.fori_loop(0, count, store, 0)


def attend_backward(qkv, grad, out, lse, place, segment, key_code, cosine, sine, block):
    tokens, width = qkv.shape
    heads = width // 3 // HD
    count = tokens // block
    reach = WINDOW // block
    return pl.pallas_call(
        functools.partial(backward_kernel, block, reach, heads),
        grid_spec=pltpu.PrefetchScalarGridSpec(
            num_scalar_prefetch=1,
            grid=(heads,),
            in_specs=[
                pl.BlockSpec((tokens, HD), lambda h, g: (0, h)),
                pl.BlockSpec((tokens, HD), lambda h, g: (0, heads + h)),
                pl.BlockSpec((tokens, HD), lambda h, g: (0, 2 * heads + h)),
                pl.BlockSpec((tokens, HD), lambda h, g: (0, h)),
                pl.BlockSpec((tokens, HD), lambda h, g: (0, h)),
                pl.BlockSpec((1, count, 1, block), lambda h, g: (h, 0, 0, 0)),
                pl.BlockSpec((count, 1, block), lambda h, g: (0, 0, 0)),
                pl.BlockSpec((count, block, 1), lambda h, g: (0, 0, 0)),
                pl.BlockSpec((tokens, HD), lambda h, g: (0, 0)),
                pl.BlockSpec((tokens, HD), lambda h, g: (0, 0)),
            ],
            out_specs=pl.BlockSpec((tokens, width), lambda h, g: (0, 0)),
            scratch_shapes=[
                pltpu.VMEM((tokens, HD), F32),
                pltpu.VMEM((tokens, HD), F32),
                pltpu.VMEM((tokens, HD), F32),
                pltpu.VMEM((count, 1, block), F32),
            ],
        ),
        out_shape=jax.ShapeDtypeStruct((tokens, width), BF16),
        compiler_params=pltpu.CompilerParams(vmem_limit_bytes=VMEM_LIMIT),
        cost_estimate=pl.CostEstimate(flops=1, bytes_accessed=1, transcendentals=0),
        name="attend_backward",
    )(
        place, qkv, qkv, qkv, grad, out, lse,
        segment.reshape(count, 1, block), key_code.reshape(count, block, 1), cosine, sine,
    )


def local(inputs, att_proj, attn_out, ff_proj, ff_out, segments, pad_mask, positions, cotangent):
    tp_size, fsdp_size = lax.axis_size("tp"), lax.axis_size("fsdp")
    rows, model = inputs.shape
    members = SEQ_LEN // rows
    sets = tp_size // members
    index = lax.axis_index("tp")
    mine = index // members
    place = index % members
    block = min(512, rows)
    depth, head_width = att_proj.shape[0], att_proj.shape[2]
    ffn_width = ff_out.shape[0]
    place_tp = place.astype(jnp.int32).reshape(1)
    place_fsdp = lax.axis_index("fsdp").astype(jnp.int32).reshape(1)

    def swap(values, bit):
        return lax.ppermute(values, "tp", [(i, i ^ bit) for i in range(tp_size)])

    def turn(values, step):
        return lax.ppermute(values, "tp", [(i, (i + step * members) % tp_size) for i in range(tp_size)])

    def cross(values, mask):
        return lax.ppermute(values, "fsdp", [(i, i ^ mask) for i in range(fsdp_size)])

    def after(value, *others):
        return lax.optimization_barrier((value, others))[0]

    chain = []

    def then(function, *args, due=()):
        args, _ = lax.optimization_barrier((args, (chain[-1], due)))
        result = function(*args)
        chain.append(jax.tree.leaves(result)[0])
        return result

    def last():
        return chain[-1]

    def group_far(values):
        blocks = {0: values}
        bit = members // 2
        while bit > 1:
            for mask in sorted(blocks, reverse=True):
                blocks[mask | bit] = swap(blocks[mask], bit)
            bit //= 2
        return blocks

    def group_near(blocks):
        blocks = dict(blocks)
        for mask in sorted(blocks, reverse=True):
            blocks[mask | 1] = swap(blocks[mask], 1)
        return [blocks[mask] for mask in range(members)]

    def group_gather(values):
        return group_near(group_far(values))

    def scatter_near(blocks):
        sums = {}
        for mask in sorted(blocks, reverse=True):
            if mask & 1:
                total = blocks[mask ^ 1].astype(F32) + swap(blocks[mask], 1).astype(F32)
                sums[mask ^ 1] = total.astype(BF16) if mask ^ 1 else total
        return sums

    def scatter_far(sums):
        sums = dict(sums)
        bit = 2
        while bit < members:
            for mask in sorted((m for m in sums if m & bit), reverse=True):
                total = sums[mask ^ bit].astype(F32) + swap(sums.pop(mask), bit).astype(F32)
                sums[mask ^ bit] = total if mask == bit else total.astype(BF16)
            bit *= 2
        return sums[0].astype(F32)

    half = members // 2

    def share(function, *args, due=((), ())):
        sums = {}
        for first in (half, 0):
            outs = then(lambda *a: function(place_fsdp, *a[:2], rows, first, half, *a[2:]), *args, due=due[first == 0])
            sums.update(scatter_near({first + p: out for p, out in enumerate(outs)}))
        return sums

    def gather(shard):
        return lax.all_gather(shard, "fsdp", axis=0)

    def scatter(stacked):
        return lax.psum_scatter(stacked.reshape(-1, stacked.shape[-1]), "fsdp", scatter_dimension=0, tiled=True)

    def settle(pieces):
        total = pieces[0].astype(F32)
        for step in range(1, sets):
            total = total + turn(pieces[step], sets - step).astype(F32)
        return total

    normed_all, packs = start_exchange(inputs, pack_weights(att_proj, attn_out), members, sets, fsdp_size)
    chain.append(normed_all[0])
    up_gate, down, cotangent_late = after((ff_proj.reshape(depth, -1), ff_out, cotangent), last())
    w_ffn, w_down = [gather(up_gate)], [gather(down)]
    turned_up_gate = [turn(up_gate, step) for step in range(1, sets)]
    cotangent_far = group_far(cotangent_late)

    segment = lax.dynamic_slice_in_dim(segments, mine * SEQ_LEN, SEQ_LEN)
    padding = lax.dynamic_slice_in_dim(pad_mask, mine * SEQ_LEN, SEQ_LEN)
    key_code = jnp.where(padding == 1, segment, -1)
    spots = lax.dynamic_slice_in_dim(positions, mine * SEQ_LEN, SEQ_LEN).reshape(members, rows)
    spots = jnp.concatenate([lax.dynamic_index_in_dim(spots, place ^ mask, 0, False) for mask in range(members)])
    cosine, sine = rope_tables(spots)

    x_float = inputs.astype(F32)
    qkv, attended = [], []
    for step in range(sets):
        qkv.append(then(functools.partial(project, place_fsdp), normed_all, packs[step], cosine, sine))
        attended.append(then(lambda part: attend_forward(part, place_tp, segment, key_code, block), qkv[step]))
    heads_low = [out for out, _ in attended]
    sums = share(functools.partial(expand_heads, "attn_branch"), heads_low, packs, due=((cotangent_far,), ()))
    for step in range(1, sets):
        w_ffn.append(gather(after(turned_up_gate[step - 1], last())))
    resid = x_float + scatter_far(sums)
    normed_two = layer_norm(resid).astype(BF16)
    turned_down = [turn(after(ff_out, normed_two), step) for step in range(1, sets)]
    cotangent_all = group_near(after(cotangent_far, normed_two))
    normed_two_all = group_gather(normed_two)

    hidden, grad_ffn, partial = [], [], None
    ffn_rows = 2 * ffn_width
    grad_expand = functools.partial(expand_stack, "grad_normed_two", dot_nt)
    down_grad = functools.partial(columns_grad, "grad_down", place_fsdp, fsdp_size, depth, ffn_rows)
    up_grad = functools.partial(rows_grad, "grad_ffn", place_fsdp, fsdp_size, depth, ffn_width)
    for step in range(sets):
        ready = (cotangent_all,) if step == 0 else ()
        low, slope_up, slope_gate = then(functools.partial(hidden_units, place_fsdp), normed_two_all, w_ffn[step], due=ready)
        hidden.append(low)
        if step == 0:
            w_down += [gather(after(down, last())) for down in turned_down]
        base = [] if partial is None else [partial]
        if step < sets - 1:
            stacked = then(down_grad, [low], cotangent_all)
        grad_low = then(functools.partial(hidden_grad, place_fsdp), cotangent_all, slope_up, slope_gate, w_down[step])
        if step < sets - 1:
            grad_ffn.append(scatter(then(up_grad, normed_two_all, grad_low, stacked)))
            call = lambda x, w, *b: grad_expand(place_fsdp, [x], [w], members * rows, 0, 1, *b)[0]
            partial = then(call, grad_low, w_ffn[step], *base)
        else:
            sums = share(grad_expand, [grad_low], [w_ffn[step]], *base)
            stacked = then(up_grad, normed_two_all, grad_low, due=sums)
            grad_normed_two = scatter_far(sums)
            grad_ffn.append(scatter(then(down_grad, [low], cotangent_all, stacked, due=(grad_normed_two,))))

    grad_resid = cotangent.astype(F32) + layer_norm_back(resid, grad_normed_two)
    resid_grad_low = grad_resid.astype(BF16)
    sums = share(functools.partial(expand_stack, "ffn_branch", dot_nn), hidden, w_down, due=((), (resid_grad_low,)))
    resid_grad_all = group_gather(resid_grad_low)

    grad_attn, grad_project = [None] * sets, [None] * sets
    heads_grad = functools.partial(columns_grad, "grad_heads", place_fsdp, fsdp_size, head_width, 3 * depth)
    project_grad = functools.partial(rows_grad, "grad_attn", place_fsdp, fsdp_size, head_width, depth)
    for step in reversed(range(sets)):
        ready = (grad_ffn[0],) if step == sets - 1 else ()
        head_grad = then(functools.partial(head_grad_of, place_fsdp), resid_grad_all, packs[step], due=ready)
        if step == sets - 1:
            ffn_branch = scatter_far(after(sums, last()))
        grad_project[step] = then(
            lambda part, grad, out, lse: attend_backward(
                part, grad, out, lse, place_tp, segment, key_code, cosine, sine, block
            ),
            qkv[step], head_grad, heads_low[step], attended[step][1],
        )
        ready = tuple(grad_ffn[1:]) if step == 0 else ()
        stacked = then(heads_grad, [heads_low[step]], resid_grad_all, due=ready)
        grad_attn[step] = scatter(then(project_grad, normed_all, grad_project[step], stacked))
    output = (resid + ffn_branch).astype(BF16)
    grad_normed = scatter_far(share(functools.partial(expand_project, "grad_normed"), grad_project, packs))
    grad_input = (grad_resid + layer_norm_back(x_float, grad_normed)).astype(BF16)

    grad_attn, grad_ffn = settle(grad_attn), settle(grad_ffn)

    def beside(values, size, count):
        return jnp.concatenate([values[i * size : (i + 1) * size] for i in range(count)], axis=1)

    return (
        output,
        grad_input,
        beside(grad_attn, depth, 3).reshape(att_proj.shape),
        beside(grad_attn[3 * depth :], head_width, depth // head_width),
        beside(grad_ffn, depth, ffn_rows // depth).reshape(ff_proj.shape),
        grad_ffn[ffn_rows:],
    )


def solution(mesh):
    rows_spec = P(("fsdp", "tp"), None)
    weights = (P("fsdp", None, "tp"), P("tp", "fsdp"), P("fsdp", None, "tp"), P("tp", "fsdp"))
    return jax.shard_map(
        local,
        mesh=mesh,
        in_specs=(rows_spec,) + weights + (P("fsdp"),) * 3 + (rows_spec,),
        out_specs=(rows_spec, rows_spec) + weights,
        check_vma=False,
    )
```

```python
import functools
import math

import jax
import jax.numpy as jnp
from jax import lax
from jax.experimental import pallas as pl
from jax.experimental.pallas import tpu as pltpu
from jax.sharding import PartitionSpec as P

HD = 128
WINDOW = 1024
SEQ_LEN = 2048
EPSILON = 1e-05
NEGATIVE = -1e30
ROPE_BASE = 10000.0
LOG2E = math.log2(math.e)
LONG = 25 * 10**10
VMEM_LIMIT = 56 * 1024 * 1024
F32 = jnp.float32
BF16 = jnp.bfloat16


def dot_nn(left, right):
    return lax.dot_general(left, right, (((1,), (0,)), ((), ())), preferred_element_type=F32)


def dot_nt(left, right):
    return lax.dot_general(left, right, (((1,), (1,)), ((), ())), preferred_element_type=F32)


def dot_tn(left, right):
    return lax.dot_general(left, right, (((0,), (0,)), ((), ())), preferred_element_type=F32)


def layer_norm(values):
    average = jnp.mean(values, axis=-1, keepdims=True)
    centered = values - average
    variance = jnp.mean(centered * centered, axis=-1, keepdims=True)
    return centered * lax.rsqrt(variance + EPSILON)


def layer_norm_back(values, grad):
    average = jnp.mean(values, axis=-1, keepdims=True)
    centered = values - average
    variance = jnp.mean(centered * centered, axis=-1, keepdims=True)
    root = lax.rsqrt(variance + EPSILON)
    normed = centered * root
    inner = jnp.mean(normed * grad, axis=-1, keepdims=True)
    return root * (grad - jnp.mean(grad, axis=-1, keepdims=True) - normed * inner)


def rope_tables(positions):
    half = HD // 2
    frequency = ROPE_BASE ** (-(jnp.arange(half, dtype=F32) * 2.0 / HD))
    angles = positions.astype(F32)[:, None] * frequency[None, :]
    cosine, sine = jnp.cos(angles), jnp.sin(angles)
    return jnp.concatenate([cosine, cosine], axis=-1), jnp.concatenate([-sine, sine], axis=-1)


def kernel_call(kernel, name, flops, grid, in_specs, out_specs, out_shapes, scratch, aliases={}):
    return pl.pallas_call(
        kernel,
        grid_spec=pltpu.PrefetchScalarGridSpec(
            num_scalar_prefetch=1, grid=grid, in_specs=in_specs, out_specs=out_specs, scratch_shapes=scratch
        ),
        out_shape=out_shapes,
        input_output_aliases=aliases,
        compiler_params=pltpu.CompilerParams(vmem_limit_bytes=VMEM_LIMIT),
        cost_estimate=pl.CostEstimate(flops=1, bytes_accessed=1, transcendentals=0),
        name=name,
    )


def any_specs(arrays):
    return [pl.BlockSpec(memory_space=pl.ANY)] * len(arrays)


def slot(index, size):
    return pl.ds(pl.multiple_of(index * size, size), size)


PIECES = 4


def start_kernel(members, sets, count, x_ref, pack_ref, *refs):
    normed, refs = refs[:members], refs[members:]
    packs = [(pack_ref,) + refs[: count - 1]]
    refs = refs[count - 1 :]
    for _ in range(1, sets):
        packs.append(refs[:count])
        refs = refs[count:]
    low_ref, local_sem, send_sem, recv_sem = refs
    t, f = lax.axis_index("tp"), lax.axis_index("fsdp")
    total = members * sets
    climb = [1 << i for i in range(count.bit_length() - 1)]
    group = [1 << i for i in range(members.bit_length() - 1)][::-1]
    shifts = [lax.rem(t + step * members, total) for step in range(1, sets)]

    barrier = pltpu.get_barrier_semaphore()
    partners = [{"tp": t ^ bit} for bit in group] + [{"tp": s} for s in shifts] + [{"fsdp": f ^ bit} for bit in climb]
    for partner in partners:
        pl.semaphore_signal(barrier, inc=1, device_id=partner, device_id_type=pl.DeviceIdType.MESH)
    pl.semaphore_wait(barrier, len(partners))

    started, waited = [], []

    def send(src, dst, partner):
        n = len(started)
        copy = pltpu.make_async_remote_copy(
            src_ref=src,
            dst_ref=dst,
            send_sem=send_sem.at[n],
            recv_sem=recv_sem.at[n],
            device_id=partner,
            device_id_type=pl.DeviceIdType.MESH,
        )
        copy.start()
        started.append(copy)
        return copy

    def await_block(copy):
        copy.wait_recv()
        waited.append(copy)

    orders = (climb, climb[::-1]) * (PIECES // 2)
    size = pack_ref.shape[0] // PIECES
    came = [{} for _ in range(sets)]

    def pass_on(step, half, mask):
        order = orders[half]
        here = pl.ds(half * size, size)
        for n, bit in enumerate(order):
            if all(not mask & later for later in order[n:]):
                copy = send(packs[step][mask].at[here, :], packs[step][mask | bit].at[here, :], {"fsdp": f ^ bit})
                came[step][half, mask | bit] = copy

    def pass_all(step, halves):
        for level in range(1, len(climb)):
            for half in halves:
                for mask in range(count):
                    if mask.bit_count() == level and not mask & orders[half][-1]:
                        await_block(came[step][half, mask])
                        pass_on(step, half, mask)

    over = {}
    for half in range(PIECES):
        here = pl.ds(half * size, size)
        for step in range(1, sets):
            over[step, half] = send(pack_ref.at[here, :], packs[step][0].at[here, :], {"tp": shifts[step - 1]})
    for half in range(PIECES):
        pass_on(0, half, 0)

    rows = x_ref.shape[0]
    tile = min(32, rows)

    def norm(i, carry):
        here = pl.ds(pl.multiple_of(i * tile, tile), tile)
        low_ref[here, :] = layer_norm(x_ref[here, :].astype(F32)).astype(BF16)
        return carry

    lax.fori_loop(0, rows // tile, norm, 0)
    keep = pltpu.make_async_copy(low_ref, normed[0], local_sem)
    keep.start()
    blocks = {}
    for bit in group:
        blocks[bit] = send(low_ref, normed[bit], {"tp": t ^ bit})
    pass_all(0, range(PIECES))
    for step in range(1, sets):
        for pair in range(0, PIECES, 2):
            for half in (pair, pair + 1):
                await_block(over[step, half])
                pass_on(step, half, 0)
            if pair:
                pass_all(step, (pair - 2, pair - 1))
        pass_all(step, (PIECES - 2, PIECES - 1))
    for mask in sorted(range(1, members), reverse=True, key=lambda m: (m & -m, m)):
        below = [bit for bit in group if bit < mask & -mask]
        if below:
            await_block(blocks[mask])
        for bit in below:
            blocks[mask | bit] = send(normed[mask], normed[mask | bit], {"tp": t ^ bit})
    keep.wait()
    for copy in started:
        copy.wait_send()
        if not any(copy is other for other in waited):
            copy.wait_recv()


def start_exchange(x, pack, members, sets, count):
    sends = PIECES * ((count - 1) * sets + sets - 1) + members - 1
    shapes = [jax.ShapeDtypeStruct(x.shape, BF16)] * members + [jax.ShapeDtypeStruct(pack.shape, BF16)] * (count * sets - 1)
    outs = pl.pallas_call(
        functools.partial(start_kernel, members, sets, count),
        in_specs=[pl.BlockSpec(memory_space=pltpu.VMEM), pl.BlockSpec(memory_space=pl.ANY)],
        out_specs=any_specs(shapes),
        out_shape=shapes,
        scratch_shapes=[
            pltpu.VMEM(x.shape, BF16),
            pltpu.SemaphoreType.DMA,
            pltpu.SemaphoreType.DMA((sends,)),
            pltpu.SemaphoreType.DMA((sends,)),
        ],
        compiler_params=pltpu.CompilerParams(vmem_limit_bytes=VMEM_LIMIT, collective_id=0, has_side_effects=True),
        cost_estimate=pl.CostEstimate(flops=1, bytes_accessed=1, transcendentals=0),
        name="start_exchange",
    )(x, pack)
    packs = [pack] + list(outs[members:])
    return outs[:members], [packs[step * count : (step + 1) * count] for step in range(sets)]


def rows_kernel(body, plan, members, extras, count, number, *refs):
    held = members // 2 if number else members
    xs, refs = refs[:held], refs[held:]
    extra_refs, refs = refs[:extras], refs[extras:]
    weights, refs = refs[:count], refs[count:]
    if number:
        *refs, send_sem, recv_sem = refs
        xs = [block for pair in zip(xs, refs[-4 - held : -4]) for block in pair]
        outs, refs = refs[: -4 - held], refs[-4:]
    else:
        outs, refs = refs[:-4], refs[-4:]
    x_buf, w_buf, x_sem, w_sem = refs
    i, f = pl.program_id(0), lax.axis_index("fsdp")
    moves, use = plan
    tiles = [
        [pltpu.make_async_copy(src, dst, w_sem.at[t, n]) for n, (src, dst) in enumerate(pairs)]
        for t, pairs in enumerate(moves(weights, w_buf, f))
    ]
    order = list(range(0, members, 2)) + list(range(1, members, 2)) if number else list(range(members))
    x_copies = [pltpu.make_async_copy(xs[m], x_buf.at[n], x_sem.at[n]) for n, m in enumerate(order)]
    exchanges = []
    if number:
        partner = {"tp": lax.axis_index("tp") ^ 1}
        exchanges = [
            pltpu.make_async_remote_copy(
                src_ref=xs[2 * q],
                dst_ref=xs[2 * q + 1],
                send_sem=send_sem.at[q],
                recv_sem=recv_sem.at[q],
                device_id=partner,
                device_id_type=pl.DeviceIdType.MESH,
            )
            for q in range(held)
        ]

    def start(n):
        if n < len(tiles):
            for copy in tiles[n]:
                copy.start()
        elif n - len(tiles) + 1 < held:
            x_copies[n - len(tiles) + 1].start()

    def run(first):
        if first:
            x_copies[0].start()
            start(0)
            start(1)
            if number:
                barrier = pltpu.get_barrier_semaphore()
                pl.semaphore_signal(barrier, inc=1, device_id=partner, device_id_type=pl.DeviceIdType.MESH)
                pl.semaphore_wait(barrier, 1)
                for exchange in exchanges:
                    exchange.start()
        pltpu.make_async_copy(xs[0], x_buf.at[i], x_sem.at[i]).wait()
        for t, copies in enumerate(tiles):
            if first:
                for copy in copies:
                    copy.wait()
                start(t + 2)
            body(t, use(t, x_buf[i], w_buf), extra_refs, outs)
        if first:
            for n in range(len(tiles) + 2, len(tiles) + held - 1):
                start(n)

    pl.when(i == 0)(functools.partial(run, True))
    pl.when(i > 0)(functools.partial(run, False))
    for q, exchange in enumerate(exchanges):

        @pl.when(i == max(held - 1, 0) + q)
        def _():
            exchange.wait()
            x_copies[held + q].start()


def rows_call(body, name, xs, extras, weights, plan, tiles, copies, w_shape, widths, number):
    rows, model = xs[0].shape
    held, count = len(xs), len(weights)
    members = 2 * held if number else held
    arrived = held if number else 0

    def here(i):
        return (i % held * 2 + i // held if number else i, 0)

    outs = pl.pallas_call(
        functools.partial(rows_kernel, body, plan, members, len(extras), count, number),
        grid_spec=pltpu.PrefetchScalarGridSpec(
            num_scalar_prefetch=0,
            grid=(members,),
            in_specs=any_specs(xs) + [pl.BlockSpec((rows, e.shape[1]), here) for e in extras] + any_specs(weights),
            out_specs=[pl.BlockSpec((rows, width), here) for width in widths] + any_specs(xs[:arrived]),
            scratch_shapes=[
                pltpu.VMEM((members, rows, model), BF16),
                pltpu.VMEM(w_shape, BF16),
                pltpu.SemaphoreType.DMA((members,)),
                pltpu.SemaphoreType.DMA((tiles, copies)),
            ]
            + [pltpu.SemaphoreType.DMA((held,))] * (2 if number else 0),
        ),
        out_shape=[jax.ShapeDtypeStruct((members * rows, width), BF16) for width in widths]
        + [jax.ShapeDtypeStruct((rows, model), BF16)] * arrived,
        compiler_params=pltpu.CompilerParams(
            vmem_limit_bytes=VMEM_LIMIT, **({"collective_id": number, "has_side_effects": True} if number else {})
        ),
        cost_estimate=pl.CostEstimate(flops=1, bytes_accessed=1, transcendentals=0),
        name=name,
    )(*xs, *extras, *weights)
    if not number:
        return outs, list(xs)
    return outs[: len(widths)], [block for pair in zip(xs, outs[len(widths) :]) for block in pair]


def project(xs, packs, cosine, sine):
    model, count = xs[0].shape[1], len(packs)
    depth, width = model // count, packs[0].shape[1]

    def moves(packs, w_buf, f):
        return [
            [(pack.at[t * depth : (t + 1) * depth, :], w_buf.at[t, slot(f ^ c, depth), :]) for c, pack in enumerate(packs)]
            for t in range(3)
        ]

    def use(t, x, w_buf):
        return dot_nn(x, w_buf[t])

    def body(t, product, extras, outs):
        for column in range(0, width, HD):
            value = product[:, column : column + HD]
            if t < 2:
                value = value * extras[0][...] + pltpu.roll(value, HD // 2, 1) * extras[1][...]
            outs[0][:, t * width + column : t * width + column + HD] = value.astype(BF16)

    return rows_call(
        body, "project", xs, [cosine, sine], packs, (moves, use), 3, count, (3, model, width), [3 * width], 0
    )[0][0]


def head_grad_of(xs, packs, number=0):
    model, count = xs[0].shape[1], len(packs)
    depth, width = model // count, packs[0].shape[1]
    squares = depth // width

    def moves(packs, w_buf, f):
        return [
            [
                (
                    pack.at[3 * depth + b * width : 3 * depth + (b + 1) * width, :],
                    w_buf.at[:, slot((f ^ c) * squares + b, width)],
                )
                for c, pack in enumerate(packs)
                for b in range(squares)
            ]
        ]

    def use(t, x, w_buf):
        return dot_nt(x, w_buf[...])

    def body(t, product, extras, outs):
        outs[0][...] = product.astype(BF16)

    return rows_call(
        body, "head_grad", xs, [], packs, (moves, use), 1, count * squares, (width, model), [width], number
    )


def hidden_units(xs, stack, number=0):
    model = xs[0].shape[1]
    count, depth, width = stack.shape
    width //= 2
    tile = min(256, width)
    starts = range(0, width, tile)

    def moves(weights, w_buf, f):
        return [
            [
                (weights[0].at[c, :, s : s + tile], w_buf.at[c * depth : (c + 1) * depth, s : s + tile])
                for c in range(count)
                for s in (start, width + start)
            ]
            for start in starts
        ]

    def use(t, x, w_buf):
        return [dot_nn(x, w_buf[:, s : s + tile]) for s in (starts[t], width + starts[t])]

    def body(t, products, extras, outs):
        here = pl.ds(starts[t], tile)
        up, gate = products
        sigmoid = 1.0 / (1.0 + jnp.exp(-gate))
        slope_up = gate * sigmoid
        outs[0][:, here] = (slope_up * up).astype(BF16)
        outs[1][:, here] = slope_up.astype(BF16)
        outs[2][:, here] = (up * sigmoid * (1.0 + gate * (1.0 - sigmoid))).astype(BF16)

    return rows_call(
        body, "hidden_units", xs, [], [stack], (moves, use), len(starts), 2 * count, (model, 2 * width), [width] * 3, number
    )


def hidden_grad(xs, slope_up, slope_gate, stack, number=0):
    model = xs[0].shape[1]
    count, width, depth = stack.shape
    tile = min(512, width)
    starts = range(0, width, tile)

    def moves(weights, w_buf, f):
        return [
            [
                (weights[0].at[c, s : s + tile, :], w_buf.at[s : s + tile, c * depth : (c + 1) * depth])
                for c in range(count)
            ]
            for s in starts
        ]

    def use(t, x, w_buf):
        return dot_nt(x, w_buf[starts[t] : starts[t] + tile, :])

    def body(t, product, extras, outs):
        here = pl.ds(starts[t], tile)
        outs[0][:, here] = (product * extras[0][:, here].astype(F32)).astype(BF16)
        outs[0][:, pl.ds(width + starts[t], tile)] = (product * extras[1][:, here].astype(F32)).astype(BF16)

    return rows_call(
        body, "hidden_grad", xs, [slope_up, slope_gate], [stack], (moves, use),
        len(starts), count, (width, model), [2 * width], number,
    )


def expand_kernel(sets, each, plan, dot, with_base, pairs, *refs):
    xs, refs = refs[:sets], refs[sets:]
    bases, refs = (refs[:1], refs[1:]) if with_base else ((), refs)
    weights, refs = refs[: sets * each], refs[sets * each :]
    outs, refs = refs[: max(pairs, 1)], refs[max(pairs, 1) :]
    w_buf, sem = refs[:2]
    d, f = pl.program_id(0), lax.axis_index("fsdp")
    count = w_buf.shape[1]

    def copies(j, c):
        there, moves = plan(weights[j * each : (j + 1) * each], c, f)
        return there, [
            pltpu.make_async_copy(src, w_buf.at[j, there, :, lanes], sem.at[j, there, n])
            for n, (src, lanes) in enumerate(moves)
        ]

    def start(place):
        for c in range(count):
            for j in range(sets):
                there, moves = copies(j, c)

                @pl.when(there == place)
                def _():
                    for copy in moves:
                        copy.start()

    if pairs:
        partner = {"tp": lax.axis_index("tp") ^ 1}
        send_buf, recv_buf, send_sem, recv_sem = refs[2:]

        def exchange(place, q):
            return pltpu.make_async_remote_copy(
                src_ref=send_buf.at[place, q],
                dst_ref=recv_buf.at[place, q],
                send_sem=send_sem.at[place, q],
                recv_sem=recv_sem.at[place, q],
                device_id=partner,
                device_id_type=pl.DeviceIdType.MESH,
            )

        @pl.when(d == 0)
        def _():
            barrier = pltpu.get_barrier_semaphore()
            pl.semaphore_signal(barrier, inc=1, device_id=partner, device_id_type=pl.DeviceIdType.MESH)
            pl.semaphore_wait(barrier, 1)

    pl.when(d == 0)(functools.partial(start, 0))
    start(d + 1)
    for j in range(sets):
        for n, (src, lanes) in enumerate(plan(weights[j * each : (j + 1) * each], 0, f)[1]):
            pltpu.make_async_copy(src, w_buf.at[j, d, :, lanes], sem.at[j, d, n]).wait()
    rows = outs[0].shape[0]

    def block(p):
        here = slice(p * rows, (p + 1) * rows)
        total = sum(dot(x[here, :], w_buf[j, d]) for j, x in enumerate(xs))
        for base in bases:
            total = total + base[here, :].astype(F32)
        return total

    if not pairs:
        outs[0][...] = block(0).astype(outs[0].dtype)
        return
    for q in range(pairs):
        send_buf[d, q] = block(2 * q + 1).astype(BF16)
        exchange(d, q).start()
    for q in range(pairs):
        total = block(2 * q)
        exchange(d, q).wait_recv()
        outs[q][...] = (total + recv_buf[d, q].astype(F32)).astype(outs[q].dtype)

    @pl.when(d == count - 1)
    def _():
        for place in range(count):
            for q in range(pairs):
                exchange(place, q).wait_send()


def expand_call(name, xs, weights, each, plan, pieces, dot, chunk, rows, base=None, first=None, members=0, number=0):
    count, w_shape = chunk
    depth = w_shape[1 if dot is dot_nn else 0]
    pairs = members // 2
    taken = rows * max(members, 1)
    block = 0 if first is None else first // members
    specs = [pl.BlockSpec((taken, x.shape[1]), lambda d: (block, 0)) for x in xs]
    bases = [] if base is None else [base]
    specs += [pl.BlockSpec((taken, depth), lambda d: (block, d)) for _ in bases]
    scratch = [pltpu.VMEM((len(xs), count) + w_shape, BF16), pltpu.SemaphoreType.DMA((len(xs), count, pieces))]
    types = [BF16]
    more = {}
    if pairs:
        types = [F32 if first == q == 0 else BF16 for q in range(pairs)]
        scratch += [pltpu.VMEM((count, pairs, rows, depth), BF16)] * 2 + [pltpu.SemaphoreType.DMA((count, pairs))] * 2
        more = {"collective_id": number, "has_side_effects": True}
    return pl.pallas_call(
        functools.partial(expand_kernel, len(xs), each, plan, dot, base is not None, pairs),
        grid_spec=pltpu.PrefetchScalarGridSpec(
            num_scalar_prefetch=0,
            grid=(count,),
            in_specs=specs + any_specs(weights),
            out_specs=[pl.BlockSpec((rows, depth), lambda d: (0, d)) for _ in types],
            scratch_shapes=scratch,
        ),
        out_shape=[jax.ShapeDtypeStruct((rows, count * depth), type_) for type_ in types],
        compiler_params=pltpu.CompilerParams(vmem_limit_bytes=VMEM_LIMIT, **more),
        cost_estimate=pl.CostEstimate(flops=1, bytes_accessed=1, transcendentals=0),
        name=name,
    )(*xs, *bases, *weights)


def expand_stack(name, dot, xs, stacks, rows, **more):
    count, above, across = stacks[0].shape

    def plan(weights, c, f):
        return c, [(weights[0].at[c], pl.ds(0, across))]

    return expand_call(name, xs, stacks, 1, plan, 1, dot, (count, (above, across)), rows, **more)


def expand_heads(name, xs, packs, rows, **more):
    count, width = len(packs[0]), packs[0][0].shape[1]
    depth = packs_depth(packs[0][0])
    squares = depth // width

    def plan(weights, c, f):
        return f ^ c, [
            (weights[c].at[3 * depth + b * width : 3 * depth + (b + 1) * width, :], pl.ds(b * width, width))
            for b in range(squares)
        ]

    flat = [pack for list_ in packs for pack in list_]
    return expand_call(name, xs, flat, count, plan, squares, dot_nn, (count, (width, depth)), rows, **more)


def expand_project(name, xs, packs, rows, **more):
    count, width = len(packs[0]), packs[0][0].shape[1]
    depth = packs_depth(packs[0][0])

    def plan(weights, c, f):
        return f ^ c, [
            (weights[c].at[t * depth : (t + 1) * depth, :], pl.ds(t * width, width)) for t in range(3)
        ]

    flat = [pack for list_ in packs for pack in list_]
    return expand_call(name, xs, flat, count, plan, 3, dot_nt, (count, (depth, 3 * width)), rows, **more)


def pack_weights(att_proj, attn_out):
    depth, _, width = att_proj.shape
    parts = [att_proj[:, t, :] for t in range(3)]
    return jnp.concatenate(parts + [attn_out[:, s : s + width] for s in range(0, depth, width)], axis=0)


def packs_depth(pack):
    return pack.shape[0] // 4


def rows_grad_kernel(members, count, f_ref, *refs):
    xs, (g_ref, out_ref, x_buf, sem) = refs[:members], refs[-4:]
    rows, depth = xs[0].shape[0], xs[0].shape[1] // count
    chunks = [
        [
            pltpu.make_async_copy(
                x.at[:, d * depth : (d + 1) * depth], x_buf.at[d, m * rows : (m + 1) * rows, :], sem.at[d, m]
            )
            for m, x in enumerate(xs)
        ]
        for d in range(count)
    ]

    def start(d):
        for copy in chunks[d] if d < count else []:
            copy.start()

    def run(first):
        if first:
            start(0)
        for d, copies in enumerate(chunks):
            if first:
                start(d + 1)
                for copy in copies:
                    copy.wait()
            out_ref[d] = dot_tn(x_buf[d], g_ref[...]).astype(BF16)

    pl.when(pl.program_id(0) == 0)(functools.partial(run, True))
    pl.when(pl.program_id(0) > 0)(functools.partial(run, False))


def rows_grad(name, place, count, tile, beside, below, xs, g, stack=None):
    rows, model = xs[0].shape
    tokens, width = g.shape
    depth = model // count
    given = [] if stack is None else [stack]
    tiles = width // tile
    shape = (count, -(-tiles // beside) * depth + below, beside * tile)
    return kernel_call(
        functools.partial(rows_grad_kernel, len(xs), count),
        name,
        2 * tokens * model * width,
        (tiles,),
        any_specs(xs) + any_specs(given) + [pl.BlockSpec((tokens, tile), lambda n, f: (0, n))],
        pl.BlockSpec((count, depth, tile), lambda n, f: (0, n // beside, n % beside)),
        jax.ShapeDtypeStruct(shape, BF16),
        [pltpu.VMEM((count, tokens, depth), BF16), pltpu.SemaphoreType.DMA((count, len(xs)))],
        {1 + len(xs): 0} if given else {},
    )(place, *xs, *given, g)


def columns_grad_kernel(sets, members, f_ref, *refs):
    xs, gs = refs[:sets], refs[sets : sets + members]
    out_ref, g_buf, sem = refs[-3:]
    d = pl.program_id(0)
    rows = gs[0].shape[0]
    total, _, depth = g_buf.shape
    tile = out_ref.shape[2]

    def start(c):
        for m, g in enumerate(gs):
            src, dst = g.at[:, slot(c, depth)], g_buf.at[c, m * rows : (m + 1) * rows, :]
            pltpu.make_async_copy(src, dst, sem.at[c, m]).start()

    @pl.when(d == 0)
    def _():
        start(0)

    @pl.when(d + 1 < total)
    def _():
        start(d + 1)

    for m, g in enumerate(gs):
        src, dst = g.at[:, :depth], g_buf.at[d, m * rows : (m + 1) * rows, :]
        pltpu.make_async_copy(src, dst, sem.at[d, m]).wait()
    first = 0
    for x in xs:
        for start in range(0, x.shape[1], 512):
            size = min(512, x.shape[1] - start)
            product = dot_tn(x[:, start : start + size], g_buf[d]).astype(BF16)
            for column in range(0, depth, tile):
                row = first + column // tile * x.shape[1] + start
                out_ref[0, row : row + size, :] = product[:, column : column + tile]
        first += x.shape[1] * (depth // tile)


def columns_grad(name, place, count, tile, shape, at, xs, gs, stack=None):
    model = gs[0].shape[1]
    tokens = xs[0].shape[0]
    depth = model // count
    height = sum(x.shape[1] for x in xs) * (depth // tile)
    given = [] if stack is None else [stack]
    return kernel_call(
        functools.partial(columns_grad_kernel, len(xs), len(gs)),
        name,
        2 * tokens * model * sum(x.shape[1] for x in xs),
        (count,),
        [pl.BlockSpec(x.shape, lambda d, f: (0, 0)) for x in xs] + any_specs(gs) + any_specs(given),
        pl.BlockSpec((1, height, tile), lambda d, f: (d, *at)),
        jax.ShapeDtypeStruct((count, *shape), BF16),
        [pltpu.VMEM((count, tokens, depth), BF16), pltpu.SemaphoreType.DMA((count, len(gs)))],
        {1 + len(xs) + len(gs): 0} if given else {},
    )(place, *xs, *gs, *given)


def forward_kernel(block, reach, g_ref, q_ref, k_ref, v_ref, seg_ref, key_ref, out_ref, lse_ref):
    i = pl.program_id(1)
    g = g_ref[0]
    scale = LOG2E / math.sqrt(HD)

    def run(count):
        q = q_ref[...]
        row = lax.broadcasted_iota(jnp.int32, (block, block), 0)
        column = lax.broadcasted_iota(jnp.int32, (block, block), 1)
        scores, rows = [], []
        for back in range(count):
            b = i - back
            rows.append(pl.ds(pl.multiple_of((b ^ g) * block, block), block))
            keep = seg_ref[0] == key_ref[b]
            if back == 0:
                keep = (keep & (row > column)) | (row == column)
            if back == reach:
                keep = keep & (row < column)
            scores.append(jnp.where(keep, dot_nt(q, k_ref[rows[-1], :]) * scale, NEGATIVE))
        top = functools.reduce(jnp.maximum, [jnp.max(s, axis=1, keepdims=True) for s in scores])
        weights = [jnp.exp2(s - top) for s in scores]
        total = sum(jnp.sum(w, axis=1, keepdims=True) for w in weights)
        out = sum(dot_nn(w.astype(BF16), v_ref[r, :]) for w, r in zip(weights, rows))
        out_ref[...] = (out / total).astype(BF16)
        lse = top + jnp.log2(total)
        lse_ref[0, 0] = jnp.transpose(jnp.broadcast_to(lse, (block, HD)))[0:1, :]

    for i_here in range(reach):
        pl.when(i == i_here)(functools.partial(run, i_here + 1))
    pl.when(i >= reach)(functools.partial(run, reach + 1))


def attend_forward(qkv, place, segment, key_code, block):
    tokens, width = qkv.shape
    heads = width // 3 // HD
    count = tokens // block
    reach = WINDOW // block
    return pl.pallas_call(
        functools.partial(forward_kernel, block, reach),
        grid_spec=pltpu.PrefetchScalarGridSpec(
            num_scalar_prefetch=1,
            grid=(heads, count),
            in_specs=[
                pl.BlockSpec((block, HD), lambda h, i, g: (i ^ g[0], h)),
                pl.BlockSpec((tokens, HD), lambda h, i, g: (0, heads + h)),
                pl.BlockSpec((tokens, HD), lambda h, i, g: (0, 2 * heads + h)),
                pl.BlockSpec((1, block, 1), lambda h, i, g: (i, 0, 0)),
                pl.BlockSpec((count, 1, block), lambda h, i, g: (0, 0, 0)),
            ],
            out_specs=[
                pl.BlockSpec((block, HD), lambda h, i, g: (i ^ g[0], h)),
                pl.BlockSpec((1, 1, 1, block), lambda h, i, g: (h, i, 0, 0)),
            ],
        ),
        out_shape=[
            jax.ShapeDtypeStruct((tokens, heads * HD), BF16),
            jax.ShapeDtypeStruct((heads, count, 1, block), F32),
        ],
        compiler_params=pltpu.CompilerParams(vmem_limit_bytes=VMEM_LIMIT),
        cost_estimate=pl.CostEstimate(flops=1, bytes_accessed=1, transcendentals=0),
        name="attend_forward",
    )(place, qkv, qkv, qkv, segment.reshape(count, block, 1), key_code.reshape(count, 1, block))


def backward_kernel(
    block, reach, heads, g_ref, q_ref, k_ref, v_ref, grad_ref, out_ref, lse_ref, seg_ref, key_ref, cos_ref, sin_ref, result_ref, dq_ref, dk_ref, dv_ref, inner_ref
):
    h = pl.program_id(0)
    g = g_ref[0]
    count = q_ref.shape[0] // block
    scale = 1.0 / math.sqrt(HD)

    def rows_of(b):
        return pl.ds(pl.multiple_of((b ^ g) * block, block), block)

    dq_ref[...] = jnp.zeros_like(dq_ref)
    dk_ref[...] = jnp.zeros_like(dk_ref)
    dv_ref[...] = jnp.zeros_like(dv_ref)

    def inner_block(i, carry):
        rows = rows_of(i)
        product = grad_ref[rows, :].astype(F32) * out_ref[rows, :].astype(F32)
        inner_ref[i] = jnp.sum(jnp.transpose(product), axis=0, keepdims=True)
        return carry

    lax.fori_loop(0, count, inner_block, 0)
    for back in range(reach + 1):

        def pair(i, carry, back=back):
            b = i - back
            query_rows, key_rows = rows_of(i), rows_of(b)
            q, k = q_ref[query_rows, :], k_ref[key_rows, :]
            v, grad = v_ref[key_rows, :], grad_ref[query_rows, :]
            keep = key_ref[b] == seg_ref[i]
            if back == 0 or back == reach:
                key = lax.broadcasted_iota(jnp.int32, (block, block), 0)
                query = lax.broadcasted_iota(jnp.int32, (block, block), 1)
                if back == 0:
                    keep = (keep & (query > key)) | (query == key)
                else:
                    keep = keep & (query < key)
            scores = dot_nt(k, q) * (scale * LOG2E)
            weights = jnp.where(keep, jnp.exp2(scores - lse_ref[0, i]), 0.0)
            grad_weights = dot_nt(v, grad)
            grad_scores = (weights * (grad_weights - inner_ref[i]) * scale).astype(BF16)
            dv_ref[key_rows, :] += dot_nn(weights.astype(BF16), grad)
            dk_ref[key_rows, :] += dot_nn(grad_scores, q)
            dq_ref[query_rows, :] += dot_tn(grad_scores, k)
            return carry

        lax.fori_loop(back, count, pair, 0)

    column = pl.multiple_of(h * HD, HD)

    def store(i, carry):
        rows = pl.ds(pl.multiple_of(i * block, block), block)
        cosine, sine = cos_ref[rows, :], sin_ref[rows, :]
        for part, ref in enumerate((dq_ref, dk_ref)):
            value = ref[rows, :]
            turned = value * cosine - pltpu.roll(value, HD // 2, 1) * sine
            result_ref[rows, pl.ds(part * heads * HD + column, HD)] = turned.astype(BF16)
        result_ref[rows, pl.ds(2 * heads * HD + column, HD)] = dv_ref[rows, :].astype(BF16)
        return carry

    lax.fori_loop(0, count, store, 0)


def attend_backward(qkv, grad, out, lse, place, segment, key_code, cosine, sine, block, cost):
    tokens, width = qkv.shape
    heads = width // 3 // HD
    count = tokens // block
    reach = WINDOW // block
    return pl.pallas_call(
        functools.partial(backward_kernel, block, reach, heads),
        grid_spec=pltpu.PrefetchScalarGridSpec(
            num_scalar_prefetch=1,
            grid=(heads,),
            in_specs=[
                pl.BlockSpec((tokens, HD), lambda h, g: (0, h)),
                pl.BlockSpec((tokens, HD), lambda h, g: (0, heads + h)),
                pl.BlockSpec((tokens, HD), lambda h, g: (0, 2 * heads + h)),
                pl.BlockSpec((tokens, HD), lambda h, g: (0, h)),
                pl.BlockSpec((tokens, HD), lambda h, g: (0, h)),
                pl.BlockSpec((1, count, 1, block), lambda h, g: (h, 0, 0, 0)),
                pl.BlockSpec((count, 1, block), lambda h, g: (0, 0, 0)),
                pl.BlockSpec((count, block, 1), lambda h, g: (0, 0, 0)),
                pl.BlockSpec((tokens, HD), lambda h, g: (0, 0)),
                pl.BlockSpec((tokens, HD), lambda h, g: (0, 0)),
            ],
            out_specs=pl.BlockSpec((tokens, width), lambda h, g: (0, 0)),
            scratch_shapes=[
                pltpu.VMEM((tokens, HD), F32),
                pltpu.VMEM((tokens, HD), F32),
                pltpu.VMEM((tokens, HD), F32),
                pltpu.VMEM((count, 1, block), F32),
            ],
        ),
        out_shape=jax.ShapeDtypeStruct((tokens, width), BF16),
        compiler_params=pltpu.CompilerParams(vmem_limit_bytes=VMEM_LIMIT),
        cost_estimate=pl.CostEstimate(flops=cost, bytes_accessed=1, transcendentals=0),
        name="attend_backward",
    )(
        place, qkv, qkv, qkv, grad, out, lse,
        segment.reshape(count, 1, block), key_code.reshape(count, block, 1), cosine, sine,
    )


def local(inputs, att_proj, attn_out, ff_proj, ff_out, segments, pad_mask, positions, cotangent):
    tp_size, fsdp_size = lax.axis_size("tp"), lax.axis_size("fsdp")
    rows, model = inputs.shape
    members = SEQ_LEN // rows
    sets = tp_size // members
    index = lax.axis_index("tp")
    mine = index // members
    place = index % members
    block = min(512, rows)
    depth, head_width = att_proj.shape[0], att_proj.shape[2]
    ffn_width = ff_out.shape[0]
    place_tp = place.astype(jnp.int32).reshape(1)
    place_fsdp = lax.axis_index("fsdp").astype(jnp.int32).reshape(1)

    def swap(values, bit):
        return lax.ppermute(values, "tp", [(i, i ^ bit) for i in range(tp_size)])

    def turn(values, step):
        return lax.ppermute(values, "tp", [(i, (i + step * members) % tp_size) for i in range(tp_size)])

    def cross(values, mask):
        return lax.ppermute(values, "fsdp", [(i, i ^ mask) for i in range(fsdp_size)])

    def after(value, *others):
        return lax.optimization_barrier((value, others))[0]

    chain = []

    def then(function, *args, due=()):
        args, _ = lax.optimization_barrier((args, (chain[-1], due)))
        result = function(*args)
        chain.append(jax.tree.leaves(result)[0])
        return result

    def last():
        return chain[-1]

    def group_far(values):
        blocks = {0: values}
        bit = members // 2
        while bit > 1:
            for mask in sorted(blocks, reverse=True):
                blocks[mask | bit] = swap(blocks[mask], bit)
            bit //= 2
        return [blocks[mask] for mask in range(0, members, 2)]

    def scatter_far(sums):
        sums = dict(sums)
        bit = 2
        while bit < members:
            for mask in sorted((m for m in sums if m & bit), reverse=True):
                total = sums[mask ^ bit].astype(F32) + swap(sums.pop(mask), bit).astype(F32)
                sums[mask ^ bit] = total if mask == bit else total.astype(BF16)
            bit *= 2
        return sums[0].astype(F32)

    half = members // 2

    def share(function, *args, number, due=(), due_near=()):
        sums = {}
        for part, first in enumerate((half, 0)):
            call = functools.partial(function, rows=rows, first=first, members=half, number=number + part)
            outs = then(lambda xs, weights, *base: call(xs, weights, base=base[0] if base else None), *args, due=due)
            sums.update({first + 2 * q: out for q, out in enumerate(outs)})
            due = due_near
        return sums

    def gather(shard):
        return lax.all_gather(shard, "fsdp", axis=0)

    def scatter(stacked):
        return lax.psum_scatter(stacked.reshape(-1, stacked.shape[-1]), "fsdp", scatter_dimension=0, tiled=True)

    def settle(pieces, *gates):
        return pieces[:1] + [turn(after(pieces[step], *gates), sets - step) for step in range(1, sets)]

    def settled(pieces):
        return sum(piece.astype(F32) for piece in pieces)

    normed_all, packs = start_exchange(inputs, pack_weights(att_proj, attn_out), members, sets, fsdp_size)
    chain.append(normed_all[0])
    up_gate, down = after((ff_proj.reshape(depth, -1), ff_out), last())
    w_ffn, w_down = [gather(up_gate)], [gather(down)]
    turned_up_gate = [turn(up_gate, step) for step in range(1, sets)]

    segment = lax.dynamic_slice_in_dim(segments, mine * SEQ_LEN, SEQ_LEN)
    padding = lax.dynamic_slice_in_dim(pad_mask, mine * SEQ_LEN, SEQ_LEN)
    key_code = jnp.where(padding == 1, segment, -1)
    spots = lax.dynamic_slice_in_dim(positions, mine * SEQ_LEN, SEQ_LEN).reshape(members, rows)
    spots = jnp.concatenate([lax.dynamic_index_in_dim(spots, place ^ mask, 0, False) for mask in range(members)])
    cosine, sine = rope_tables(spots)

    x_float = inputs.astype(F32)
    qkv, attended = [], []
    for step in range(sets):
        qkv.append(then(project, normed_all, packs[step], cosine, sine))
        attended.append(then(lambda part: attend_forward(part, place_tp, segment, key_code, block), qkv[step]))
    heads_low = [out for out, _ in attended]
    sums = share(functools.partial(expand_heads, "attn_branch"), heads_low, packs, number=1)
    w_ffn += [gather(after(part, chain[-2])) for part in turned_up_gate]
    resid = x_float + scatter_far(sums)
    normed_two_far = group_far(layer_norm(resid).astype(BF16))
    down, cotangent_late = after((ff_out, cotangent), normed_two_far[-1])
    turned_down = [turn(down, step) for step in range(1, sets)]
    cotangent_far = group_far(cotangent_late)

    hidden, slopes, grad_ffn, partial = [], [], [], None
    for step in range(sets):
        if step == 0:
            (low, *slope), normed_two_all = then(functools.partial(hidden_units, number=9), normed_two_far, w_ffn[0])
        else:
            (low, *slope), _ = then(hidden_units, normed_two_all, w_ffn[step])
        hidden.append(low)
        slopes.append(slope)
    ffn_rows = 2 * ffn_width
    grad_expand = functools.partial(expand_stack, "grad_normed_two", dot_nt)
    up_grad = functools.partial(rows_grad, "grad_ffn", place_fsdp, fsdp_size, depth, 1, 0)
    for step in range(sets):
        if step == 0:
            (grad_low,), cotangent_all = then(functools.partial(hidden_grad, number=10), cotangent_far, *slopes[0], w_down[0])
        else:
            (grad_low,), _ = then(hidden_grad, cotangent_all, *slopes[step], w_down[step])
        if step == 0:
            w_down += [gather(after(part, last())) for part in turned_down]
        grad_ffn.append(scatter(then(up_grad, normed_two_all, grad_low)))
        base = [] if partial is None else [partial]
        if step < sets - 1:
            call = lambda x, w, *b: grad_expand([x], [w], members * rows, base=b[0] if b else None)[0]
            partial = then(call, grad_low, w_ffn[step], *base)
    sums = share(grad_expand, [grad_low], [w_ffn[-1]], *base, number=3)
    ffn_sums = share(functools.partial(expand_stack, "ffn_branch", dot_nn), hidden, w_down, number=5)
    grad_normed_two = after(scatter_far(sums), ffn_sums[half])
    grad_resid = cotangent.astype(F32) + layer_norm_back(resid, grad_normed_two)
    resid_grad_low = grad_resid.astype(BF16)
    resid_grad_far = group_far(resid_grad_low)
    shape, at = (sets * ffn_width, depth), (0, 0)
    down_grad = functools.partial(columns_grad, "grad_down", place_fsdp, fsdp_size, depth, shape, at)
    grad_down = scatter(then(down_grad, hidden, cotangent_all, due=(resid_grad_low,)))

    grad_attn, grad_project = [None] * sets, [None] * sets
    shape, at = (2 * depth, 2 * head_width), (1, 1)
    heads_grad = functools.partial(columns_grad, "grad_heads", place_fsdp, fsdp_size, head_width, shape, at)
    project_grad = functools.partial(rows_grad, "grad_attn", place_fsdp, fsdp_size, head_width, 2, 0)
    held = None
    for step in reversed(range(sets)):
        ready = tuple(grad_ffn[:1]) if step == sets - 1 else (grad_up[1:], ffn_branch)
        if step == sets - 1:
            (head_grad,), resid_grad_all = then(functools.partial(head_grad_of, number=11), resid_grad_far, packs[step], due=ready)
        else:
            (head_grad,), _ = then(head_grad_of, resid_grad_all, packs[step], due=ready)
        if step == sets - 1:
            grad_up = settle([piece[:ffn_width] for piece in grad_ffn], last())
            ffn_branch = scatter_far(after(ffn_sums, last()))
        else:
            grad_gate = settle([piece[ffn_width:] for piece in grad_ffn], last(), grad_up[1:])
        if held is not None:
            grad_attn[step + 1] = scatter(after(held, last()))
        grad_project[step] = then(
            lambda part, grad, out, lse: attend_backward(
                part, grad, out, lse, place_tp, segment, key_code, cosine, sine, block, LONG
            ),
            qkv[step], head_grad, heads_low[step], attended[step][1],
        )
        if step == 0:
            grad_down = settle([grad_down[j * ffn_width : (j + 1) * ffn_width] for j in range(sets)], last(), grad_gate[1:])
        stacked = then(heads_grad, [heads_low[step]], resid_grad_all)
        ready = tuple(grad_gate[1:]) if step == 0 else ()
        held = then(project_grad, normed_all, grad_project[step], stacked, due=ready)
    grad_attn[0] = scatter(held)
    sums = share(functools.partial(expand_project, "grad_normed"), grad_project, packs, number=7)
    grad_normed = scatter_far(sums)
    output = (resid + ffn_branch).astype(BF16)
    grad_attn = settle(grad_attn)
    grad_normed = after(grad_normed, grad_attn[1:])
    grad_input = (grad_resid + layer_norm_back(x_float, grad_normed)).astype(BF16)
    grad_attn = settled(grad_attn)

    def beside(values, first, size, count):
        return jnp.concatenate([values[(first + i) * size : (first + i + 1) * size] for i in range(count)], axis=1)

    query, key = grad_attn[:depth, :head_width], grad_attn[:depth, head_width:]
    value, squares = grad_attn[depth:, :head_width], grad_attn[depth:, head_width:]
    blocks = ffn_width // depth

    return (
        output,
        grad_input,
        jnp.stack([query, key, value], axis=1),
        beside(squares, 0, head_width, depth // head_width),
        jnp.stack([beside(settled(part), 0, depth, blocks) for part in (grad_up, grad_gate)], axis=1),
        settled(grad_down),
    )


def solution(mesh):
    rows_spec = P(("fsdp", "tp"), None)
    weights = (P("fsdp", None, "tp"), P("tp", "fsdp"), P("fsdp", None, "tp"), P("tp", "fsdp"))
    return jax.shard_map(
        local,
        mesh=mesh,
        in_specs=(rows_spec,) + weights + (P("fsdp"),) * 3 + (rows_spec,),
        out_specs=(rows_spec, rows_spec) + weights,
        check_vma=False,
    )
```

```python
import functools
import math

import jax
import jax.numpy as jnp
from jax import lax
from jax.experimental import pallas as pl
from jax.experimental.pallas import tpu as pltpu
from jax.sharding import PartitionSpec as P

HD = 128
WINDOW = 1024
SEQ_LEN = 2048
EPSILON = 1e-05
NEGATIVE = -1e30
ROPE_BASE = 10000.0
LOG2E = math.log2(math.e)
LONG = 10**12
VMEM_LIMIT = 56 * 1024 * 1024
F32 = jnp.float32
BF16 = jnp.bfloat16


def dot_nn(left, right):
    return lax.dot_general(left, right, (((1,), (0,)), ((), ())), preferred_element_type=F32)


def dot_nt(left, right):
    return lax.dot_general(left, right, (((1,), (1,)), ((), ())), preferred_element_type=F32)


def dot_tn(left, right):
    return lax.dot_general(left, right, (((0,), (0,)), ((), ())), preferred_element_type=F32)


def layer_norm(values):
    average = jnp.mean(values, axis=-1, keepdims=True)
    centered = values - average
    variance = jnp.mean(centered * centered, axis=-1, keepdims=True)
    return centered * lax.rsqrt(variance + EPSILON)


def layer_norm_back(values, grad):
    average = jnp.mean(values, axis=-1, keepdims=True)
    centered = values - average
    variance = jnp.mean(centered * centered, axis=-1, keepdims=True)
    root = lax.rsqrt(variance + EPSILON)
    normed = centered * root
    inner = jnp.mean(normed * grad, axis=-1, keepdims=True)
    return root * (grad - jnp.mean(grad, axis=-1, keepdims=True) - normed * inner)


def rope_tables(positions):
    half = HD // 2
    frequency = ROPE_BASE ** (-(jnp.arange(half, dtype=F32) * 2.0 / HD))
    angles = positions.astype(F32)[:, None] * frequency[None, :]
    cosine, sine = jnp.cos(angles), jnp.sin(angles)
    return jnp.concatenate([cosine, cosine], axis=-1), jnp.concatenate([-sine, sine], axis=-1)


def kernel_call(kernel, name, cost, grid, in_specs, out_specs, out_shapes, scratch, aliases={}):
    return pl.pallas_call(
        kernel,
        grid_spec=pltpu.PrefetchScalarGridSpec(
            num_scalar_prefetch=1, grid=grid, in_specs=in_specs, out_specs=out_specs, scratch_shapes=scratch
        ),
        out_shape=out_shapes,
        input_output_aliases=aliases,
        compiler_params=pltpu.CompilerParams(vmem_limit_bytes=VMEM_LIMIT),
        cost_estimate=pl.CostEstimate(flops=cost, bytes_accessed=1, transcendentals=0),
        name=name,
    )


def any_specs(arrays):
    return [pl.BlockSpec(memory_space=pl.ANY)] * len(arrays)


def slot(index, size):
    return pl.ds(pl.multiple_of(index * size, size), size)


PIECES = 4


def start_kernel(members, sets, count, x_ref, pack_ref, *refs):
    normed, refs = refs[:members], refs[members:]
    packs = [(pack_ref,) + refs[: count - 1]]
    refs = refs[count - 1 :]
    for _ in range(1, sets):
        packs.append(refs[:count])
        refs = refs[count:]
    low_ref, local_sem, send_sem, recv_sem = refs
    t, f = lax.axis_index("tp"), lax.axis_index("fsdp")
    total = members * sets
    climb = [1 << i for i in range(count.bit_length() - 1)]
    group = [1 << i for i in range(members.bit_length() - 1)][::-1]
    shifts = [lax.rem(t + step * members, total) for step in range(1, sets)]

    barrier = pltpu.get_barrier_semaphore()
    partners = [{"tp": t ^ bit} for bit in group] + [{"tp": s} for s in shifts] + [{"fsdp": f ^ bit} for bit in climb]
    for partner in partners:
        pl.semaphore_signal(barrier, inc=1, device_id=partner, device_id_type=pl.DeviceIdType.MESH)
    pl.semaphore_wait(barrier, len(partners))

    started, waited = [], []

    def send(src, dst, partner):
        n = len(started)
        copy = pltpu.make_async_remote_copy(
            src_ref=src,
            dst_ref=dst,
            send_sem=send_sem.at[n],
            recv_sem=recv_sem.at[n],
            device_id=partner,
            device_id_type=pl.DeviceIdType.MESH,
        )
        copy.start()
        started.append(copy)
        return copy

    def await_block(copy):
        copy.wait_recv()
        waited.append(copy)

    orders = (climb, climb[::-1]) * (PIECES // 2)
    size = pack_ref.shape[0] // PIECES
    came = [{} for _ in range(sets)]

    def pass_on(step, half, mask):
        order = orders[half]
        here = pl.ds(half * size, size)
        for n, bit in enumerate(order):
            if all(not mask & later for later in order[n:]):
                copy = send(packs[step][mask].at[here, :], packs[step][mask | bit].at[here, :], {"fsdp": f ^ bit})
                came[step][half, mask | bit] = copy

    def pass_all(step, halves):
        for level in range(1, len(climb)):
            for half in halves:
                for mask in range(count):
                    if mask.bit_count() == level and not mask & orders[half][-1]:
                        await_block(came[step][half, mask])
                        pass_on(step, half, mask)

    over = {}
    for half in range(PIECES):
        here = pl.ds(half * size, size)
        for step in range(1, sets):
            over[step, half] = send(pack_ref.at[here, :], packs[step][0].at[here, :], {"tp": shifts[step - 1]})
    for half in range(PIECES):
        pass_on(0, half, 0)

    rows = x_ref.shape[0]
    tile = min(32, rows)

    def norm(i, carry):
        here = pl.ds(pl.multiple_of(i * tile, tile), tile)
        low_ref[here, :] = layer_norm(x_ref[here, :].astype(F32)).astype(BF16)
        return carry

    lax.fori_loop(0, rows // tile, norm, 0)
    keep = pltpu.make_async_copy(low_ref, normed[0], local_sem)
    keep.start()
    blocks = {}
    for bit in group:
        blocks[bit] = send(low_ref, normed[bit], {"tp": t ^ bit})
    pass_all(0, range(PIECES))
    for step in range(1, sets):
        for pair in range(0, PIECES, 2):
            for half in (pair, pair + 1):
                await_block(over[step, half])
                pass_on(step, half, 0)
            if pair:
                pass_all(step, (pair - 2, pair - 1))
        pass_all(step, (PIECES - 2, PIECES - 1))
    for mask in sorted(range(1, members), reverse=True, key=lambda m: (m & -m, m)):
        below = [bit for bit in group if bit < mask & -mask]
        if below:
            await_block(blocks[mask])
        for bit in below:
            blocks[mask | bit] = send(normed[mask], normed[mask | bit], {"tp": t ^ bit})
    keep.wait()
    for copy in started:
        copy.wait_send()
        if not any(copy is other for other in waited):
            copy.wait_recv()


def start_exchange(x, pack, members, sets, count):
    sends = PIECES * ((count - 1) * sets + sets - 1) + members - 1
    shapes = [jax.ShapeDtypeStruct(x.shape, BF16)] * members + [jax.ShapeDtypeStruct(pack.shape, BF16)] * (count * sets - 1)
    outs = pl.pallas_call(
        functools.partial(start_kernel, members, sets, count),
        in_specs=[pl.BlockSpec(memory_space=pltpu.VMEM), pl.BlockSpec(memory_space=pl.ANY)],
        out_specs=any_specs(shapes),
        out_shape=shapes,
        scratch_shapes=[
            pltpu.VMEM(x.shape, BF16),
            pltpu.SemaphoreType.DMA,
            pltpu.SemaphoreType.DMA((sends,)),
            pltpu.SemaphoreType.DMA((sends,)),
        ],
        compiler_params=pltpu.CompilerParams(vmem_limit_bytes=VMEM_LIMIT, collective_id=0, has_side_effects=True),
        cost_estimate=pl.CostEstimate(flops=1, bytes_accessed=1, transcendentals=0),
        name="start_exchange",
    )(x, pack)
    packs = [pack] + list(outs[members:])
    return outs[:members], [packs[step * count : (step + 1) * count] for step in range(sets)]


def rows_kernel(body, plan, members, extras, count, number, *refs):
    held = members // 2 if number else members
    xs, refs = refs[:held], refs[held:]
    extra_refs, refs = refs[:extras], refs[extras:]
    weights, refs = refs[:count], refs[count:]
    if number:
        *refs, send_sem, recv_sem = refs
        xs = [block for pair in zip(xs, refs[-4 - held : -4]) for block in pair]
        outs, refs = refs[: -4 - held], refs[-4:]
    else:
        outs, refs = refs[:-4], refs[-4:]
    x_buf, w_buf, x_sem, w_sem = refs
    i, f = pl.program_id(0), lax.axis_index("fsdp")
    moves, use = plan
    tiles = [
        [pltpu.make_async_copy(src, dst, w_sem.at[t, n]) for n, (src, dst) in enumerate(pairs)]
        for t, pairs in enumerate(moves(weights, w_buf, f))
    ]
    order = list(range(0, members, 2)) + list(range(1, members, 2)) if number else list(range(members))
    x_copies = [pltpu.make_async_copy(xs[m], x_buf.at[n], x_sem.at[n]) for n, m in enumerate(order)]
    exchanges = []
    if number:
        partner = {"tp": lax.axis_index("tp") ^ 1}
        exchanges = [
            pltpu.make_async_remote_copy(
                src_ref=xs[2 * q],
                dst_ref=xs[2 * q + 1],
                send_sem=send_sem.at[q],
                recv_sem=recv_sem.at[q],
                device_id=partner,
                device_id_type=pl.DeviceIdType.MESH,
            )
            for q in range(held)
        ]

    def start(n):
        if n < len(tiles):
            for copy in tiles[n]:
                copy.start()
        elif n - len(tiles) + 1 < held:
            x_copies[n - len(tiles) + 1].start()

    def run(first):
        if first:
            x_copies[0].start()
            start(0)
            start(1)
            if number:
                barrier = pltpu.get_barrier_semaphore()
                pl.semaphore_signal(barrier, inc=1, device_id=partner, device_id_type=pl.DeviceIdType.MESH)
                pl.semaphore_wait(barrier, 1)
                for exchange in exchanges:
                    exchange.start()
        pltpu.make_async_copy(xs[0], x_buf.at[i], x_sem.at[i]).wait()
        for t, copies in enumerate(tiles):
            if first:
                for copy in copies:
                    copy.wait()
                start(t + 2)
            body(t, use(t, x_buf[i], w_buf), extra_refs, outs)
        if first:
            for n in range(len(tiles) + 2, len(tiles) + held - 1):
                start(n)

    for q, exchange in enumerate(exchanges):

        @pl.when(i == 1 + q)
        def _():
            exchange.wait()
            x_copies[held + q].start()

    pl.when(i == 0)(functools.partial(run, True))
    pl.when(i > 0)(functools.partial(run, False))


def rows_call(body, name, xs, extras, weights, plan, tiles, copies, w_shape, widths, number, cost=1):
    rows, model = xs[0].shape
    held, count = len(xs), len(weights)
    members = 2 * held if number else held
    arrived = held if number else 0

    def here(i):
        return (i % held * 2 + i // held if number else i, 0)

    outs = pl.pallas_call(
        functools.partial(rows_kernel, body, plan, members, len(extras), count, number),
        grid_spec=pltpu.PrefetchScalarGridSpec(
            num_scalar_prefetch=0,
            grid=(members,),
            in_specs=any_specs(xs) + [pl.BlockSpec((rows, e.shape[1]), here) for e in extras] + any_specs(weights),
            out_specs=[pl.BlockSpec((rows, width), here) for width in widths] + any_specs(xs[:arrived]),
            scratch_shapes=[
                pltpu.VMEM((members, rows, model), BF16),
                pltpu.VMEM(w_shape, BF16),
                pltpu.SemaphoreType.DMA((members,)),
                pltpu.SemaphoreType.DMA((tiles, copies)),
            ]
            + [pltpu.SemaphoreType.DMA((held,))] * (2 if number else 0),
        ),
        out_shape=[jax.ShapeDtypeStruct((members * rows, width), BF16) for width in widths]
        + [jax.ShapeDtypeStruct((rows, model), BF16)] * arrived,
        compiler_params=pltpu.CompilerParams(
            vmem_limit_bytes=VMEM_LIMIT, **({"collective_id": number, "has_side_effects": True} if number else {})
        ),
        cost_estimate=pl.CostEstimate(flops=cost, bytes_accessed=1, transcendentals=0),
        name=name,
    )(*xs, *extras, *weights)
    if not number:
        return outs, list(xs)
    return outs[: len(widths)], [block for pair in zip(xs, outs[len(widths) :]) for block in pair]


def project(xs, packs, cosine, sine):
    model, count = xs[0].shape[1], len(packs)
    depth, width = model // count, packs[0].shape[1]

    def moves(packs, w_buf, f):
        return [
            [(pack.at[t * depth : (t + 1) * depth, :], w_buf.at[t, slot(f ^ c, depth), :]) for c, pack in enumerate(packs)]
            for t in range(3)
        ]

    def use(t, x, w_buf):
        return dot_nn(x, w_buf[t])

    def body(t, product, extras, outs):
        for column in range(0, width, HD):
            value = product[:, column : column + HD]
            if t < 2:
                value = value * extras[0][...] + pltpu.roll(value, HD // 2, 1) * extras[1][...]
            outs[0][:, t * width + column : t * width + column + HD] = value.astype(BF16)

    return rows_call(
        body, "project", xs, [cosine, sine], packs, (moves, use), 3, count, (3, model, width), [3 * width], 0
    )[0][0]


def head_grad_of(xs, packs, number=0):
    model, count = xs[0].shape[1], len(packs)
    depth, width = model // count, packs[0].shape[1]
    squares = depth // width

    def moves(packs, w_buf, f):
        return [
            [
                (
                    pack.at[3 * depth + b * width : 3 * depth + (b + 1) * width, :],
                    w_buf.at[:, slot((f ^ c) * squares + b, width)],
                )
                for c, pack in enumerate(packs)
                for b in range(squares)
            ]
        ]

    def use(t, x, w_buf):
        return dot_nt(x, w_buf[...])

    def body(t, product, extras, outs):
        outs[0][...] = product.astype(BF16)

    return rows_call(
        body, "head_grad", xs, [], packs, (moves, use), 1, count * squares, (width, model), [width], number
    )


def hidden_units(xs, stack, number=0):
    model = xs[0].shape[1]
    count, depth, width = stack.shape
    width //= 2
    tile = min(256, width)
    starts = range(0, width, tile)

    def moves(weights, w_buf, f):
        return [
            [
                (weights[0].at[c, :, s : s + tile], w_buf.at[c * depth : (c + 1) * depth, s : s + tile])
                for c in range(count)
                for s in (start, width + start)
            ]
            for start in starts
        ]

    def use(t, x, w_buf):
        return [dot_nn(x, w_buf[:, s : s + tile]) for s in (starts[t], width + starts[t])]

    def body(t, products, extras, outs):
        here = pl.ds(starts[t], tile)
        up, gate = products
        sigmoid = 1.0 / (1.0 + jnp.exp(-gate))
        slope_up = gate * sigmoid
        outs[0][:, here] = (slope_up * up).astype(BF16)
        outs[1][:, here] = slope_up.astype(BF16)
        outs[2][:, here] = (up * sigmoid * (1.0 + gate * (1.0 - sigmoid))).astype(BF16)

    return rows_call(
        body, "hidden_units", xs, [], [stack], (moves, use), len(starts), 2 * count, (model, 2 * width), [width] * 3, number
    )


def hidden_grad(xs, slope_up, slope_gate, stack, number=0, cost=1):
    model = xs[0].shape[1]
    count, width, depth = stack.shape
    tile = min(512, width)
    starts = range(0, width, tile)

    def moves(weights, w_buf, f):
        return [
            [
                (weights[0].at[c, s : s + tile, :], w_buf.at[s : s + tile, c * depth : (c + 1) * depth])
                for c in range(count)
            ]
            for s in starts
        ]

    def use(t, x, w_buf):
        return dot_nt(x, w_buf[starts[t] : starts[t] + tile, :])

    def body(t, product, extras, outs):
        here = pl.ds(starts[t], tile)
        outs[0][:, here] = (product * extras[0][:, here].astype(F32)).astype(BF16)
        outs[0][:, pl.ds(width + starts[t], tile)] = (product * extras[1][:, here].astype(F32)).astype(BF16)

    return rows_call(
        body, "hidden_grad", xs, [slope_up, slope_gate], [stack], (moves, use),
        len(starts), count, (width, model), [2 * width], number, cost,
    )


def expand_kernel(sets, each, plan, dot, with_base, pairs, *refs):
    xs, refs = refs[:sets], refs[sets:]
    bases, refs = (refs[:1], refs[1:]) if with_base else ((), refs)
    weights, refs = refs[: sets * each], refs[sets * each :]
    outs, refs = refs[: max(pairs, 1)], refs[max(pairs, 1) :]
    w_buf, sem = refs[:2]
    step, f = pl.program_id(0), lax.axis_index("fsdp")
    count = w_buf.shape[1]
    d = lax.rem(step, count)

    def copies(j, c):
        there, moves = plan(weights[j * each : (j + 1) * each], c, f)
        return there, [
            pltpu.make_async_copy(src, w_buf.at[j, there, :, lanes], sem.at[j, there, n])
            for n, (src, lanes) in enumerate(moves)
        ]

    def start(place):
        for c in range(count):
            for j in range(sets):
                there, moves = copies(j, c)

                @pl.when(there == place)
                def _():
                    for copy in moves:
                        copy.start()

    if pairs:
        partner = {"tp": lax.axis_index("tp") ^ 1}
        send_buf, recv_buf, send_sem, recv_sem = refs[2:]

        def exchange(place, q):
            return pltpu.make_async_remote_copy(
                src_ref=send_buf.at[place, q],
                dst_ref=recv_buf.at[place, q],
                send_sem=send_sem.at[place, q],
                recv_sem=recv_sem.at[place, q],
                device_id=partner,
                device_id_type=pl.DeviceIdType.MESH,
            )

        @pl.when(step == 0)
        def _():
            barrier = pltpu.get_barrier_semaphore()
            pl.semaphore_signal(barrier, inc=1, device_id=partner, device_id_type=pl.DeviceIdType.MESH)
            pl.semaphore_wait(barrier, 1)

    pl.when(step == 0)(functools.partial(start, 0))
    pl.when(step < count - 1)(lambda: start(d + 1))

    @pl.when(step < count)
    def _():
        for j in range(sets):
            for n, (src, lanes) in enumerate(plan(weights[j * each : (j + 1) * each], 0, f)[1]):
                pltpu.make_async_copy(src, w_buf.at[j, d, :, lanes], sem.at[j, d, n]).wait()

    rows = outs[0].shape[0]

    def block(p):
        here = slice(p * rows, (p + 1) * rows)
        total = sum(dot(x[here, :], w_buf[j, d]) for j, x in enumerate(xs))
        for base in bases:
            total = total + base[here, :].astype(F32)
        return total

    if not pairs:
        outs[0][...] = block(0).astype(outs[0].dtype)
        return

    @pl.when(step < count)
    def _():
        for q in range(pairs):
            send_buf[d, q] = block(2 * q + 1).astype(BF16)
            exchange(d, q).start()

    @pl.when(step >= count)
    def _():
        for q in range(pairs):
            total = block(2 * q)
            exchange(d, q).wait_recv()
            outs[q][...] = (total + recv_buf[d, q].astype(F32)).astype(outs[q].dtype)

    @pl.when(step == 2 * count - 1)
    def _():
        for place in range(count):
            for q in range(pairs):
                exchange(place, q).wait_send()


def expand_call(name, xs, weights, each, plan, pieces, dot, chunk, rows, base=None, first=None, members=0, number=0, cost=1):
    count, w_shape = chunk
    depth = w_shape[1 if dot is dot_nn else 0]
    pairs = members // 2
    taken = rows * max(members, 1)
    block = 0 if first is None else first // members
    specs = [pl.BlockSpec((taken, x.shape[1]), lambda d: (block, 0)) for x in xs]
    bases = [] if base is None else [base]
    specs += [pl.BlockSpec((taken, depth), lambda d: (block, lax.rem(d, count))) for _ in bases]
    steps = 2 * count if pairs else count
    scratch = [pltpu.VMEM((len(xs), count) + w_shape, BF16), pltpu.SemaphoreType.DMA((len(xs), count, pieces))]
    types = [BF16]
    more = {}
    if pairs:
        types = [F32 if first == q == 0 else BF16 for q in range(pairs)]
        scratch += [pltpu.VMEM((count, pairs, rows, depth), BF16)] * 2 + [pltpu.SemaphoreType.DMA((count, pairs))] * 2
        more = {"collective_id": number, "has_side_effects": True}
    return pl.pallas_call(
        functools.partial(expand_kernel, len(xs), each, plan, dot, base is not None, pairs),
        grid_spec=pltpu.PrefetchScalarGridSpec(
            num_scalar_prefetch=0,
            grid=(steps,),
            in_specs=specs + any_specs(weights),
            out_specs=[pl.BlockSpec((rows, depth), lambda d: (0, lax.max(d + count - steps, 0))) for _ in types],
            scratch_shapes=scratch,
        ),
        out_shape=[jax.ShapeDtypeStruct((rows, count * depth), type_) for type_ in types],
        compiler_params=pltpu.CompilerParams(vmem_limit_bytes=VMEM_LIMIT, **more),
        cost_estimate=pl.CostEstimate(flops=cost, bytes_accessed=1, transcendentals=0),
        name=name,
    )(*xs, *bases, *weights)


def expand_stack(name, dot, xs, stacks, rows, **more):
    count, above, across = stacks[0].shape

    def plan(weights, c, f):
        return c, [(weights[0].at[c], pl.ds(0, across))]

    return expand_call(name, xs, stacks, 1, plan, 1, dot, (count, (above, across)), rows, **more)


def expand_heads(name, xs, packs, rows, **more):
    count, width = len(packs[0]), packs[0][0].shape[1]
    depth = packs_depth(packs[0][0])
    squares = depth // width

    def plan(weights, c, f):
        return f ^ c, [
            (weights[c].at[3 * depth + b * width : 3 * depth + (b + 1) * width, :], pl.ds(b * width, width))
            for b in range(squares)
        ]

    flat = [pack for list_ in packs for pack in list_]
    return expand_call(name, xs, flat, count, plan, squares, dot_nn, (count, (width, depth)), rows, **more)


def expand_project(name, xs, packs, rows, **more):
    count, width = len(packs[0]), packs[0][0].shape[1]
    depth = packs_depth(packs[0][0])

    def plan(weights, c, f):
        return f ^ c, [
            (weights[c].at[t * depth : (t + 1) * depth, :], pl.ds(t * width, width)) for t in range(3)
        ]

    flat = [pack for list_ in packs for pack in list_]
    return expand_call(name, xs, flat, count, plan, 3, dot_nt, (count, (depth, 3 * width)), rows, **more)


def pack_weights(att_proj, attn_out):
    depth, _, width = att_proj.shape
    parts = [att_proj[:, t, :] for t in range(3)]
    return jnp.concatenate(parts + [attn_out[:, s : s + width] for s in range(0, depth, width)], axis=0)


def packs_depth(pack):
    return pack.shape[0] // 4


def rows_grad_kernel(members, count, f_ref, *refs):
    xs, (g_ref, out_ref, x_buf, sem) = refs[:members], refs[-4:]
    rows, depth = xs[0].shape[0], xs[0].shape[1] // count
    chunks = [
        [
            pltpu.make_async_copy(
                x.at[:, d * depth : (d + 1) * depth], x_buf.at[d, m * rows : (m + 1) * rows, :], sem.at[d, m]
            )
            for m, x in enumerate(xs)
        ]
        for d in range(count)
    ]

    def start(d):
        for copy in chunks[d] if d < count else []:
            copy.start()

    def run(first):
        if first:
            start(0)
        for d, copies in enumerate(chunks):
            if first:
                start(d + 1)
                for copy in copies:
                    copy.wait()
            out_ref[d] = dot_tn(x_buf[d], g_ref[...]).astype(BF16)

    pl.when(pl.program_id(0) == 0)(functools.partial(run, True))
    pl.when(pl.program_id(0) > 0)(functools.partial(run, False))


def rows_grad(name, place, count, tile, beside, below, xs, g, stack=None, cost=1):
    rows, model = xs[0].shape
    tokens, width = g.shape
    depth = model // count
    given = [] if stack is None else [stack]
    tiles = width // tile
    shape = (count, -(-tiles // beside) * depth + below, beside * tile)
    return kernel_call(
        functools.partial(rows_grad_kernel, len(xs), count),
        name,
        cost,
        (tiles,),
        any_specs(xs) + any_specs(given) + [pl.BlockSpec((tokens, tile), lambda n, f: (0, n))],
        pl.BlockSpec((count, depth, tile), lambda n, f: (0, n // beside, n % beside)),
        jax.ShapeDtypeStruct(shape, BF16),
        [pltpu.VMEM((count, tokens, depth), BF16), pltpu.SemaphoreType.DMA((count, len(xs)))],
        {1 + len(xs): 0} if given else {},
    )(place, *xs, *given, g)


def columns_grad_kernel(sets, members, f_ref, *refs):
    xs, gs = refs[:sets], refs[sets : sets + members]
    out_ref, g_buf, sem = refs[-3:]
    d = pl.program_id(0)
    rows = gs[0].shape[0]
    total, _, depth = g_buf.shape
    tile = out_ref.shape[2]

    def start(c):
        for m, g in enumerate(gs):
            src, dst = g.at[:, slot(c, depth)], g_buf.at[c, m * rows : (m + 1) * rows, :]
            pltpu.make_async_copy(src, dst, sem.at[c, m]).start()

    @pl.when(d == 0)
    def _():
        start(0)

    @pl.when(d + 1 < total)
    def _():
        start(d + 1)

    for m, g in enumerate(gs):
        src, dst = g.at[:, :depth], g_buf.at[d, m * rows : (m + 1) * rows, :]
        pltpu.make_async_copy(src, dst, sem.at[d, m]).wait()
    first = 0
    for x in xs:
        for start in range(0, x.shape[1], 512):
            size = min(512, x.shape[1] - start)
            product = dot_tn(x[:, start : start + size], g_buf[d]).astype(BF16)
            for column in range(0, depth, tile):
                row = first + column // tile * x.shape[1] + start
                out_ref[0, row : row + size, :] = product[:, column : column + tile]
        first += x.shape[1] * (depth // tile)


def columns_grad(name, place, count, tile, shape, at, xs, gs, stack=None):
    model = gs[0].shape[1]
    tokens = xs[0].shape[0]
    depth = model // count
    height = sum(x.shape[1] for x in xs) * (depth // tile)
    given = [] if stack is None else [stack]
    return kernel_call(
        functools.partial(columns_grad_kernel, len(xs), len(gs)),
        name,
        1,
        (count,),
        [pl.BlockSpec(x.shape, lambda d, f: (0, 0)) for x in xs] + any_specs(gs) + any_specs(given),
        pl.BlockSpec((1, height, tile), lambda d, f: (d, *at)),
        jax.ShapeDtypeStruct((count, *shape), BF16),
        [pltpu.VMEM((count, tokens, depth), BF16), pltpu.SemaphoreType.DMA((count, len(gs)))],
        {1 + len(xs) + len(gs): 0} if given else {},
    )(place, *xs, *gs, *given)


def forward_kernel(block, reach, g_ref, q_ref, k_ref, v_ref, seg_ref, key_ref, out_ref, lse_ref):
    i = pl.program_id(0)
    g = g_ref[0]
    scale = LOG2E / math.sqrt(HD)
    heads = q_ref.shape[1] // HD

    def run(count):
        row = lax.broadcasted_iota(jnp.int32, (block, block), 0)
        column = lax.broadcasted_iota(jnp.int32, (block, block), 1)
        keeps, rows = [], []
        for back in range(count):
            b = i - back
            rows.append(pl.ds(pl.multiple_of((b ^ g) * block, block), block))
            keep = seg_ref[0] == key_ref[b]
            if back == 0:
                keep = (keep & (row > column)) | (row == column)
            if back == reach:
                keep = keep & (row < column)
            keeps.append(keep)
        for h in range(heads):
            lanes = slice(h * HD, (h + 1) * HD)
            q = q_ref[:, lanes]
            scores = [jnp.where(keep, dot_nt(q, k_ref[r, lanes]), NEGATIVE) for keep, r in zip(keeps, rows)]
            top = functools.reduce(jnp.maximum, [jnp.max(s, axis=1, keepdims=True) for s in scores])
            weights = [jnp.exp2((s - top) * scale) for s in scores]
            total = sum(jnp.sum(w, axis=1, keepdims=True) for w in weights)
            out = sum(dot_nn(w.astype(BF16), v_ref[r, lanes]) for w, r in zip(weights, rows))
            out_ref[:, lanes] = (out / total).astype(BF16)
            lse = top * scale + jnp.log2(total)
            lse_ref[h, 0] = jnp.transpose(jnp.broadcast_to(lse, (block, HD)))[0:1, :]

    for i_here in range(reach):
        pl.when(i == i_here)(functools.partial(run, i_here + 1))
    pl.when(i >= reach)(functools.partial(run, reach + 1))


def attend_forward(qkv, place, segment, key_code, block):
    tokens, width = qkv.shape
    heads = width // 3 // HD
    count = tokens // block
    reach = WINDOW // block
    return pl.pallas_call(
        functools.partial(forward_kernel, block, reach),
        grid_spec=pltpu.PrefetchScalarGridSpec(
            num_scalar_prefetch=1,
            grid=(count,),
            in_specs=[
                pl.BlockSpec((block, heads * HD), lambda i, g: (i ^ g[0], 0)),
                pl.BlockSpec((tokens, heads * HD), lambda i, g: (0, 1)),
                pl.BlockSpec((tokens, heads * HD), lambda i, g: (0, 2)),
                pl.BlockSpec((1, block, 1), lambda i, g: (i, 0, 0)),
                pl.BlockSpec((count, 1, block), lambda i, g: (0, 0, 0)),
            ],
            out_specs=[
                pl.BlockSpec((block, heads * HD), lambda i, g: (i ^ g[0], 0)),
                pl.BlockSpec((heads, 1, 1, block), lambda i, g: (0, i, 0, 0)),
            ],
        ),
        out_shape=[
            jax.ShapeDtypeStruct((tokens, heads * HD), BF16),
            jax.ShapeDtypeStruct((heads, count, 1, block), F32),
        ],
        compiler_params=pltpu.CompilerParams(vmem_limit_bytes=VMEM_LIMIT),
        cost_estimate=pl.CostEstimate(flops=1, bytes_accessed=1, transcendentals=0),
        name="attend_forward",
    )(place, qkv, qkv, qkv, segment.reshape(count, block, 1), key_code.reshape(count, 1, block))


def backward_kernel(
    block, reach, heads, g_ref, q_ref, k_ref, v_ref, grad_ref, out_ref, lse_ref, seg_ref, key_ref, cos_ref, sin_ref, result_ref, dq_ref, dk_ref, dv_ref, inner_ref
):
    g = g_ref[0]
    count = q_ref.shape[0] // block
    scale = 1.0 / math.sqrt(HD)

    def rows_of(b):
        return pl.ds(pl.multiple_of((b ^ g) * block, block), block)

    dq_ref[...] = jnp.zeros_like(dq_ref)
    dk_ref[...] = jnp.zeros_like(dk_ref)
    dv_ref[...] = jnp.zeros_like(dv_ref)

    def inner_block(i, carry):
        rows = rows_of(i)
        for h in range(heads):
            lanes = slice(h * HD, (h + 1) * HD)
            product = grad_ref[rows, lanes].astype(F32) * out_ref[rows, lanes].astype(F32)
            inner_ref[h, i] = jnp.sum(jnp.transpose(product), axis=0, keepdims=True)
        return carry

    lax.fori_loop(0, count, inner_block, 0)
    for back in range(reach + 1):

        def pair(i, carry, back=back):
            b = i - back
            query_rows, key_rows = rows_of(i), rows_of(b)
            keep = key_ref[b] == seg_ref[i]
            if back == 0 or back == reach:
                key = lax.broadcasted_iota(jnp.int32, (block, block), 0)
                query = lax.broadcasted_iota(jnp.int32, (block, block), 1)
                if back == 0:
                    keep = (keep & (query > key)) | (query == key)
                else:
                    keep = keep & (query < key)
            for h in range(heads):
                lanes = slice(h * HD, (h + 1) * HD)
                q, k = q_ref[query_rows, lanes], k_ref[key_rows, lanes]
                v, grad = v_ref[key_rows, lanes], grad_ref[query_rows, lanes]
                scores = dot_nt(k, q)
                weights = jnp.where(keep, jnp.exp2(scores * (scale * LOG2E) - lse_ref[h, i]), 0.0)
                grad_weights = dot_nt(v, grad)
                grad_scores = (weights * (grad_weights - inner_ref[h, i])).astype(BF16)
                dv_ref[key_rows, lanes] += dot_nn(weights.astype(BF16), grad)
                dk_ref[key_rows, lanes] += dot_nn(grad_scores, q)
                dq_ref[query_rows, lanes] += dot_tn(grad_scores, k)
            return carry

        lax.fori_loop(back, count, pair, 0)

    def store(i, carry):
        rows = pl.ds(pl.multiple_of(i * block, block), block)
        cosine, sine = cos_ref[rows, :], sin_ref[rows, :]
        for h in range(heads):
            lanes = slice(h * HD, (h + 1) * HD)
            for part, ref in enumerate((dq_ref, dk_ref)):
                value = ref[rows, lanes] * scale
                turned = value * cosine - pltpu.roll(value, HD // 2, 1) * sine
                result_ref[rows, (part * heads + h) * HD : (part * heads + h + 1) * HD] = turned.astype(BF16)
            result_ref[rows, (2 * heads + h) * HD : (2 * heads + h + 1) * HD] = dv_ref[rows, lanes].astype(BF16)
        return carry

    lax.fori_loop(0, count, store, 0)


def attend_backward(qkv, grad, out, lse, place, segment, key_code, cosine, sine, block, cost):
    tokens, width = qkv.shape
    heads = width // 3 // HD
    count = tokens // block
    reach = WINDOW // block
    return pl.pallas_call(
        functools.partial(backward_kernel, block, reach, heads),
        grid_spec=pltpu.PrefetchScalarGridSpec(
            num_scalar_prefetch=1,
            grid=(1,),
            in_specs=[
                pl.BlockSpec((tokens, heads * HD), lambda h, g: (0, 0)),
                pl.BlockSpec((tokens, heads * HD), lambda h, g: (0, 1)),
                pl.BlockSpec((tokens, heads * HD), lambda h, g: (0, 2)),
                pl.BlockSpec((tokens, heads * HD), lambda h, g: (0, 0)),
                pl.BlockSpec((tokens, heads * HD), lambda h, g: (0, 0)),
                pl.BlockSpec((heads, count, 1, block), lambda h, g: (0, 0, 0, 0)),
                pl.BlockSpec((count, 1, block), lambda h, g: (0, 0, 0)),
                pl.BlockSpec((count, block, 1), lambda h, g: (0, 0, 0)),
                pl.BlockSpec((tokens, HD), lambda h, g: (0, 0)),
                pl.BlockSpec((tokens, HD), lambda h, g: (0, 0)),
            ],
            out_specs=pl.BlockSpec((tokens, width), lambda h, g: (0, 0)),
            scratch_shapes=[
                pltpu.VMEM((tokens, heads * HD), F32),
                pltpu.VMEM((tokens, heads * HD), F32),
                pltpu.VMEM((tokens, heads * HD), F32),
                pltpu.VMEM((heads, count, 1, block), F32),
            ],
        ),
        out_shape=jax.ShapeDtypeStruct((tokens, width), BF16),
        compiler_params=pltpu.CompilerParams(vmem_limit_bytes=VMEM_LIMIT),
        cost_estimate=pl.CostEstimate(flops=cost, bytes_accessed=1, transcendentals=0),
        name="attend_backward",
    )(
        place, qkv, qkv, qkv, grad, out, lse,
        segment.reshape(count, 1, block), key_code.reshape(count, block, 1), cosine, sine,
    )


def local(inputs, att_proj, attn_out, ff_proj, ff_out, segments, pad_mask, positions, cotangent):
    tp_size, fsdp_size = lax.axis_size("tp"), lax.axis_size("fsdp")
    rows, model = inputs.shape
    members = SEQ_LEN // rows
    sets = tp_size // members
    index = lax.axis_index("tp")
    mine = index // members
    place = index % members
    block = min(512, rows)
    depth, head_width = att_proj.shape[0], att_proj.shape[2]
    ffn_width = ff_out.shape[0]
    place_tp = place.astype(jnp.int32).reshape(1)
    place_fsdp = lax.axis_index("fsdp").astype(jnp.int32).reshape(1)

    def swap(values, bit):
        return lax.ppermute(values, "tp", [(i, i ^ bit) for i in range(tp_size)])

    def turn(values, step):
        return lax.ppermute(values, "tp", [(i, (i + step * members) % tp_size) for i in range(tp_size)])

    def cross(values, mask):
        return lax.ppermute(values, "fsdp", [(i, i ^ mask) for i in range(fsdp_size)])

    def after(value, *others):
        return lax.optimization_barrier((value, others))[0]

    chain = []

    def then(function, *args, due=()):
        args, _ = lax.optimization_barrier((args, (chain[-1], due)))
        result = function(*args)
        chain.append(jax.tree.leaves(result)[0])
        return result

    def last():
        return chain[-1]

    def group_far(values):
        blocks = {0: values}
        bit = members // 2
        while bit > 1:
            for mask in sorted(blocks, reverse=True):
                blocks[mask | bit] = swap(blocks[mask], bit)
            bit //= 2
        return [blocks[mask] for mask in range(0, members, 2)]

    def scatter_far(sums):
        sums = dict(sums)
        parts = [sums[0]]
        bit = 2
        while bit < members:
            for mask in sorted((m for m in sums if m & bit), reverse=True):
                received = swap(sums.pop(mask), bit)
                if mask == bit:
                    parts.append(received)
                else:
                    sums[mask ^ bit] = (sums[mask ^ bit].astype(F32) + received.astype(F32)).astype(BF16)
            bit *= 2
        return parts

    half = members // 2

    def share(function, *args, number, due=(), due_near=(), cost_near=1):
        sums = {}
        for part, first in enumerate((half, 0)):
            cost = 1 if first else cost_near
            call = functools.partial(function, rows=rows, first=first, members=half, number=number + part, cost=cost)
            outs = then(lambda xs, weights, *base: call(xs, weights, base=base[0] if base else None), *args, due=due)
            sums.update({first + 2 * q: out for q, out in enumerate(outs)})
            due = due_near
        return sums

    def gather(shard):
        return lax.all_gather(shard, "fsdp", axis=0)

    def scatter(stacked):
        return lax.psum_scatter(stacked.reshape(-1, stacked.shape[-1]), "fsdp", scatter_dimension=0, tiled=True)

    def settle(pieces, *gates):
        return pieces[:1] + [turn(after(pieces[step], *gates), sets - step) for step in range(1, sets)]

    def settled(pieces):
        return sum(piece.astype(F32) for piece in pieces)

    normed_all, packs = start_exchange(inputs, pack_weights(att_proj, attn_out), members, sets, fsdp_size)
    chain.append(normed_all[0])
    up_gate, down, cotangent_late = after((ff_proj.reshape(depth, -1), ff_out, cotangent), last())
    w_ffn, w_down = [gather(up_gate)], [gather(down)]
    turned_up_gate = [turn(up_gate, step) for step in range(1, sets)]
    cotangent_far = group_far(cotangent_late)

    segment = lax.dynamic_slice_in_dim(segments, mine * SEQ_LEN, SEQ_LEN)
    padding = lax.dynamic_slice_in_dim(pad_mask, mine * SEQ_LEN, SEQ_LEN)
    key_code = jnp.where(padding == 1, segment, -1)
    spots = lax.dynamic_slice_in_dim(positions, mine * SEQ_LEN, SEQ_LEN).reshape(members, rows)
    spots = jnp.concatenate([lax.dynamic_index_in_dim(spots, place ^ mask, 0, False) for mask in range(members)])
    cosine, sine = rope_tables(spots)

    x_float = inputs.astype(F32)
    qkv, attended = [], []
    for step in range(sets):
        qkv.append(then(project, normed_all, packs[step], cosine, sine))
        attended.append(then(lambda part: attend_forward(part, place_tp, segment, key_code, block), qkv[step]))
    heads_low = [out for out, _ in attended]
    sums = share(functools.partial(expand_heads, "attn_branch"), heads_low, packs, number=1)
    w_ffn += [gather(after(part, last(), cotangent_far)) for part in turned_up_gate]
    resid = x_float + settled(scatter_far(sums))
    normed_two_far = group_far(layer_norm(resid).astype(BF16))
    turned_down = [turn(after(ff_out, normed_two_far[-1]), step) for step in range(1, sets)]

    hidden, slopes, grad_ffn, partial = [], [], [], None
    for step in range(sets):
        if step == 0:
            (low, *slope), normed_two_all = then(functools.partial(hidden_units, number=9), normed_two_far, w_ffn[0])
        else:
            (low, *slope), _ = then(hidden_units, normed_two_all, w_ffn[step])
        hidden.append(low)
        slopes.append(slope)
    w_down += [gather(after(part, last())) for part in turned_down]
    ffn_rows = 2 * ffn_width
    grad_expand = functools.partial(expand_stack, "grad_normed_two", dot_nt)
    up_grad = functools.partial(rows_grad, "grad_ffn", place_fsdp, fsdp_size, depth, 1, 0)
    for step in range(sets):
        if step == 0:
            (grad_low,), cotangent_all = then(functools.partial(hidden_grad, number=10, cost=LONG), cotangent_far, *slopes[0], w_down[0])
        else:
            (grad_low,), _ = then(hidden_grad, cotangent_all, *slopes[step], w_down[step])
        grad_ffn.append(scatter(then(up_grad, normed_two_all, grad_low)))
        base = [] if partial is None else [partial]
        if step < sets - 1:
            call = lambda x, w, *b: grad_expand([x], [w], members * rows, base=b[0] if b else None)[0]
            partial = then(call, grad_low, w_ffn[step], *base)
    sums = share(grad_expand, [grad_low], [w_ffn[-1]], *base, number=3)
    ffn_sums = share(functools.partial(expand_stack, "ffn_branch", dot_nn), hidden, w_down, number=5)
    grad_normed_two = settled(after(scatter_far(sums), ffn_sums[half]))
    grad_resid = cotangent.astype(F32) + layer_norm_back(resid, grad_normed_two)
    resid_grad_low = grad_resid.astype(BF16)
    resid_grad_far = group_far(resid_grad_low)
    shape, at = (sets * ffn_width, depth), (0, 0)
    down_grad = functools.partial(columns_grad, "grad_down", place_fsdp, fsdp_size, depth, shape, at)
    grad_down = scatter(then(down_grad, hidden, cotangent_all, due=(resid_grad_low,)))

    grad_attn, grad_project = [None] * sets, [None] * sets
    shape, at = (2 * depth, 2 * head_width), (1, 1)
    heads_grad = functools.partial(columns_grad, "grad_heads", place_fsdp, fsdp_size, head_width, shape, at)
    project_grad = functools.partial(rows_grad, "grad_attn", place_fsdp, fsdp_size, head_width, 2, 0)
    held = None
    for step in reversed(range(sets)):
        if step == sets - 1:
            call = functools.partial(head_grad_of, number=11)
            (head_grad,), resid_grad_all = then(call, resid_grad_far, packs[step], due=tuple(grad_ffn[:1]))
            grad_up = settle([piece[:ffn_width] for piece in grad_ffn], last())
            ffn_branch = scatter_far(after(ffn_sums, last()))
            ready = ()
        else:
            (head_grad,), _ = then(head_grad_of, resid_grad_all, packs[step])
            grad_gate = settle([piece[ffn_width:] for piece in grad_ffn], last(), grad_up[1:])
            grad_attn[step + 1] = scatter(after(held, last()))
            ready = (grad_up[1:], ffn_branch[1:])
        grad_project[step] = then(
            lambda part, grad, out, lse: attend_backward(
                part, grad, out, lse, place_tp, segment, key_code, cosine, sine, block, LONG
            ),
            qkv[step], head_grad, heads_low[step], attended[step][1], due=ready,
        )
        if step == 0:
            grad_down = settle([grad_down[j * ffn_width : (j + 1) * ffn_width] for j in range(sets)], last())
        stacked = then(heads_grad, [heads_low[step]], resid_grad_all)
        held = then(project_grad, normed_all, grad_project[step], stacked)
    grad_attn[0] = scatter(held)
    call = functools.partial(expand_project, "grad_normed")
    due = (tuple(grad_gate[1:]), tuple(grad_down[1:]))
    sums = share(call, grad_project, packs, number=7, due=due[0], due_near=due[1], cost_near=LONG)
    grad_normed = scatter_far(sums)
    output = (resid + settled(ffn_branch)).astype(BF16)
    grad_attn = settle(grad_attn)
    grad_normed = settled(after(grad_normed, grad_attn[1:]))
    grad_input = (grad_resid + layer_norm_back(x_float, grad_normed)).astype(BF16)
    grad_attn = settled(grad_attn)

    def beside(values, first, size, count):
        return jnp.concatenate([values[(first + i) * size : (first + i + 1) * size] for i in range(count)], axis=1)

    query, key = grad_attn[:depth, :head_width], grad_attn[:depth, head_width:]
    value, squares = grad_attn[depth:, :head_width], grad_attn[depth:, head_width:]
    blocks = ffn_width // depth

    return (
        output,
        grad_input,
        jnp.stack([query, key, value], axis=1),
        beside(squares, 0, head_width, depth // head_width),
        jnp.stack([beside(settled(part), 0, depth, blocks) for part in (grad_up, grad_gate)], axis=1),
        settled(grad_down),
    )


def solution(mesh):
    rows_spec = P(("fsdp", "tp"), None)
    weights = (P("fsdp", None, "tp"), P("tp", "fsdp"), P("fsdp", None, "tp"), P("tp", "fsdp"))
    return jax.shard_map(
        local,
        mesh=mesh,
        in_specs=(rows_spec,) + weights + (P("fsdp"),) * 3 + (rows_spec,),
        out_specs=(rows_spec, rows_spec) + weights,
        check_vma=False,
    )
```

```python
import functools
import math

import jax
import jax.numpy as jnp
from jax import lax
from jax.experimental import pallas as pl
from jax.experimental.pallas import tpu as pltpu
from jax.sharding import PartitionSpec as P

HD = 128
WINDOW = 1024
SEQ_LEN = 2048
EPSILON = 1e-05
NEGATIVE = -1e30
ROPE_BASE = 10000.0
LOG2E = math.log2(math.e)
LONG = 10**12
VMEM_LIMIT = 56 * 1024 * 1024
F32 = jnp.float32
BF16 = jnp.bfloat16


def dot_nn(left, right):
    return lax.dot_general(left, right, (((1,), (0,)), ((), ())), preferred_element_type=F32)


def dot_nt(left, right):
    return lax.dot_general(left, right, (((1,), (1,)), ((), ())), preferred_element_type=F32)


def dot_tn(left, right):
    return lax.dot_general(left, right, (((0,), (0,)), ((), ())), preferred_element_type=F32)


def layer_norm(values):
    average = jnp.mean(values, axis=-1, keepdims=True)
    centered = values - average
    variance = jnp.mean(centered * centered, axis=-1, keepdims=True)
    return centered * lax.rsqrt(variance + EPSILON)


def layer_norm_back(values, grad):
    average = jnp.mean(values, axis=-1, keepdims=True)
    centered = values - average
    variance = jnp.mean(centered * centered, axis=-1, keepdims=True)
    root = lax.rsqrt(variance + EPSILON)
    normed = centered * root
    inner = jnp.mean(normed * grad, axis=-1, keepdims=True)
    return root * (grad - jnp.mean(grad, axis=-1, keepdims=True) - normed * inner)


def rope_tables(positions):
    half = HD // 2
    frequency = ROPE_BASE ** (-(jnp.arange(half, dtype=F32) * 2.0 / HD))
    angles = positions.astype(F32)[:, None] * frequency[None, :]
    cosine, sine = jnp.cos(angles), jnp.sin(angles)
    return jnp.concatenate([cosine, cosine], axis=-1), jnp.concatenate([-sine, sine], axis=-1)


def kernel_call(kernel, name, cost, grid, in_specs, out_specs, out_shapes, scratch, aliases={}):
    return pl.pallas_call(
        kernel,
        grid_spec=pltpu.PrefetchScalarGridSpec(
            num_scalar_prefetch=1, grid=grid, in_specs=in_specs, out_specs=out_specs, scratch_shapes=scratch
        ),
        out_shape=out_shapes,
        input_output_aliases=aliases,
        compiler_params=pltpu.CompilerParams(vmem_limit_bytes=VMEM_LIMIT),
        cost_estimate=pl.CostEstimate(flops=cost, bytes_accessed=1, transcendentals=0),
        name=name,
    )


def any_specs(arrays):
    return [pl.BlockSpec(memory_space=pl.ANY)] * len(arrays)


def slot(index, size):
    return pl.ds(pl.multiple_of(index * size, size), size)


PIECES = 4


def start_kernel(members, sets, count, x_ref, pack_ref, *refs):
    normed, refs = refs[:members], refs[members:]
    packs = [(pack_ref,) + refs[: count - 1]]
    refs = refs[count - 1 :]
    for _ in range(1, sets):
        packs.append(refs[:count])
        refs = refs[count:]
    low_ref, local_sem, send_sem, recv_sem = refs
    t, f = lax.axis_index("tp"), lax.axis_index("fsdp")
    total = members * sets
    climb = [1 << i for i in range(count.bit_length() - 1)]
    group = [1 << i for i in range(members.bit_length() - 1)][::-1]
    shifts = [lax.rem(t + step * members, total) for step in range(1, sets)]

    barrier = pltpu.get_barrier_semaphore()
    partners = [{"tp": t ^ bit} for bit in group] + [{"tp": s} for s in shifts] + [{"fsdp": f ^ bit} for bit in climb]
    for partner in partners:
        pl.semaphore_signal(barrier, inc=1, device_id=partner, device_id_type=pl.DeviceIdType.MESH)
    pl.semaphore_wait(barrier, len(partners))

    started, waited = [], []

    def send(src, dst, partner):
        n = len(started)
        copy = pltpu.make_async_remote_copy(
            src_ref=src,
            dst_ref=dst,
            send_sem=send_sem.at[n],
            recv_sem=recv_sem.at[n],
            device_id=partner,
            device_id_type=pl.DeviceIdType.MESH,
        )
        copy.start()
        started.append(copy)
        return copy

    def await_block(copy):
        copy.wait_recv()
        waited.append(copy)

    orders = (climb, climb[::-1]) * (PIECES // 2)
    size = pack_ref.shape[0] // PIECES
    came = [{} for _ in range(sets)]

    def pass_on(step, half, mask):
        order = orders[half]
        here = pl.ds(half * size, size)
        for n, bit in enumerate(order):
            if all(not mask & later for later in order[n:]):
                copy = send(packs[step][mask].at[here, :], packs[step][mask | bit].at[here, :], {"fsdp": f ^ bit})
                came[step][half, mask | bit] = copy

    def pass_all(step, halves):
        for level in range(1, len(climb)):
            for half in halves:
                for mask in range(count):
                    if mask.bit_count() == level and not mask & orders[half][-1]:
                        await_block(came[step][half, mask])
                        pass_on(step, half, mask)

    over = {}
    for half in range(PIECES):
        here = pl.ds(half * size, size)
        for step in range(1, sets):
            over[step, half] = send(pack_ref.at[here, :], packs[step][0].at[here, :], {"tp": shifts[step - 1]})
    for half in range(PIECES):
        pass_on(0, half, 0)

    rows = x_ref.shape[0]
    tile = min(32, rows)

    def norm(i, carry):
        here = pl.ds(pl.multiple_of(i * tile, tile), tile)
        low_ref[here, :] = layer_norm(x_ref[here, :].astype(F32)).astype(BF16)
        return carry

    lax.fori_loop(0, rows // tile, norm, 0)
    keep = pltpu.make_async_copy(low_ref, normed[0], local_sem)
    keep.start()
    blocks = {}
    for bit in group:
        blocks[bit] = send(low_ref, normed[bit], {"tp": t ^ bit})
    pass_all(0, range(PIECES))
    for step in range(1, sets):
        for pair in range(0, PIECES, 2):
            for half in (pair, pair + 1):
                await_block(over[step, half])
                pass_on(step, half, 0)
            if pair:
                pass_all(step, (pair - 2, pair - 1))
        pass_all(step, (PIECES - 2, PIECES - 1))
    for mask in sorted(range(1, members), reverse=True, key=lambda m: (m & -m, m)):
        below = [bit for bit in group if bit < mask & -mask]
        if below:
            await_block(blocks[mask])
        for bit in below:
            blocks[mask | bit] = send(normed[mask], normed[mask | bit], {"tp": t ^ bit})
    keep.wait()
    for copy in started:
        copy.wait_send()
        if not any(copy is other for other in waited):
            copy.wait_recv()


def start_exchange(x, pack, members, sets, count):
    sends = PIECES * ((count - 1) * sets + sets - 1) + members - 1
    shapes = [jax.ShapeDtypeStruct(x.shape, BF16)] * members + [jax.ShapeDtypeStruct(pack.shape, BF16)] * (count * sets - 1)
    outs = pl.pallas_call(
        functools.partial(start_kernel, members, sets, count),
        in_specs=[pl.BlockSpec(memory_space=pltpu.VMEM), pl.BlockSpec(memory_space=pl.ANY)],
        out_specs=any_specs(shapes),
        out_shape=shapes,
        scratch_shapes=[
            pltpu.VMEM(x.shape, BF16),
            pltpu.SemaphoreType.DMA,
            pltpu.SemaphoreType.DMA((sends,)),
            pltpu.SemaphoreType.DMA((sends,)),
        ],
        compiler_params=pltpu.CompilerParams(vmem_limit_bytes=VMEM_LIMIT, collective_id=0, has_side_effects=True),
        cost_estimate=pl.CostEstimate(flops=1, bytes_accessed=1, transcendentals=0),
        name="start_exchange",
    )(x, pack)
    packs = [pack] + list(outs[members:])
    return outs[:members], [packs[step * count : (step + 1) * count] for step in range(sets)]


def rows_kernel(body, plan, members, extras, count, number, *refs):
    held = members // 2 if number else members
    xs, refs = refs[:held], refs[held:]
    extra_refs, refs = refs[:extras], refs[extras:]
    weights, refs = refs[:count], refs[count:]
    if number:
        *refs, send_sem, recv_sem = refs
        xs = [block for pair in zip(xs, refs[-4 - held : -4]) for block in pair]
        outs, refs = refs[: -4 - held], refs[-4:]
    else:
        outs, refs = refs[:-4], refs[-4:]
    x_buf, w_buf, x_sem, w_sem = refs
    i, f = pl.program_id(0), lax.axis_index("fsdp")
    moves, use = plan
    tiles = [
        [pltpu.make_async_copy(src, dst, w_sem.at[t, n]) for n, (src, dst) in enumerate(pairs)]
        for t, pairs in enumerate(moves(weights, w_buf, f))
    ]
    order = list(range(0, members, 2)) + list(range(1, members, 2)) if number else list(range(members))
    x_copies = [pltpu.make_async_copy(xs[m], x_buf.at[n], x_sem.at[n]) for n, m in enumerate(order)]
    exchanges = []
    if number:
        partner = {"tp": lax.axis_index("tp") ^ 1}
        exchanges = [
            pltpu.make_async_remote_copy(
                src_ref=xs[2 * q],
                dst_ref=xs[2 * q + 1],
                send_sem=send_sem.at[q],
                recv_sem=recv_sem.at[q],
                device_id=partner,
                device_id_type=pl.DeviceIdType.MESH,
            )
            for q in range(held)
        ]

    def start(n):
        if n < len(tiles):
            for copy in tiles[n]:
                copy.start()
        elif n - len(tiles) + 1 < held:
            x_copies[n - len(tiles) + 1].start()

    def run(first):
        if first:
            x_copies[0].start()
            start(0)
            start(1)
            if number:
                barrier = pltpu.get_barrier_semaphore()
                pl.semaphore_signal(barrier, inc=1, device_id=partner, device_id_type=pl.DeviceIdType.MESH)
                pl.semaphore_wait(barrier, 1)
                for exchange in exchanges:
                    exchange.start()
        pltpu.make_async_copy(xs[0], x_buf.at[i], x_sem.at[i]).wait()
        for t, copies in enumerate(tiles):
            if first:
                for copy in copies:
                    copy.wait()
                start(t + 2)
            body(t, use(t, x_buf[i], w_buf), extra_refs, outs)
        if first:
            for n in range(len(tiles) + 2, len(tiles) + held - 1):
                start(n)

    for q, exchange in enumerate(exchanges):

        @pl.when(i == 1 + q)
        def _():
            exchange.wait()
            x_copies[held + q].start()

    pl.when(i == 0)(functools.partial(run, True))
    pl.when(i > 0)(functools.partial(run, False))


def rows_call(body, name, xs, extras, weights, plan, tiles, copies, w_shape, widths, number, cost=1):
    rows, model = xs[0].shape
    held, count = len(xs), len(weights)
    members = 2 * held if number else held
    arrived = held if number else 0

    def here(i):
        return (i % held * 2 + i // held if number else i, 0)

    outs = pl.pallas_call(
        functools.partial(rows_kernel, body, plan, members, len(extras), count, number),
        grid_spec=pltpu.PrefetchScalarGridSpec(
            num_scalar_prefetch=0,
            grid=(members,),
            in_specs=any_specs(xs) + [pl.BlockSpec((rows, e.shape[1]), here) for e in extras] + any_specs(weights),
            out_specs=[pl.BlockSpec((rows, width), here) for width in widths] + any_specs(xs[:arrived]),
            scratch_shapes=[
                pltpu.VMEM((members, rows, model), BF16),
                pltpu.VMEM(w_shape, BF16),
                pltpu.SemaphoreType.DMA((members,)),
                pltpu.SemaphoreType.DMA((tiles, copies)),
            ]
            + [pltpu.SemaphoreType.DMA((held,))] * (2 if number else 0),
        ),
        out_shape=[jax.ShapeDtypeStruct((members * rows, width), BF16) for width in widths]
        + [jax.ShapeDtypeStruct((rows, model), BF16)] * arrived,
        compiler_params=pltpu.CompilerParams(
            vmem_limit_bytes=VMEM_LIMIT, **({"collective_id": number, "has_side_effects": True} if number else {})
        ),
        cost_estimate=pl.CostEstimate(flops=cost, bytes_accessed=1, transcendentals=0),
        name=name,
    )(*xs, *extras, *weights)
    if not number:
        return outs, list(xs)
    return outs[: len(widths)], [block for pair in zip(xs, outs[len(widths) :]) for block in pair]


def project(xs, packs, cosine, sine):
    model, count = xs[0].shape[1], len(packs)
    depth, width = model // count, packs[0].shape[1]

    def moves(packs, w_buf, f):
        return [
            [(pack.at[t * depth : (t + 1) * depth, :], w_buf.at[t, slot(f ^ c, depth), :]) for c, pack in enumerate(packs)]
            for t in range(3)
        ]

    def use(t, x, w_buf):
        return dot_nn(x, w_buf[t])

    def body(t, product, extras, outs):
        for column in range(0, width, HD):
            value = product[:, column : column + HD]
            if t < 2:
                value = value * extras[0][...] + pltpu.roll(value, HD // 2, 1) * extras[1][...]
            outs[0][:, t * width + column : t * width + column + HD] = value.astype(BF16)

    return rows_call(
        body, "project", xs, [cosine, sine], packs, (moves, use), 3, count, (3, model, width), [3 * width], 0
    )[0][0]


def head_grad_of(xs, packs, number=0):
    model, count = xs[0].shape[1], len(packs)
    depth, width = model // count, packs[0].shape[1]
    squares = depth // width

    def moves(packs, w_buf, f):
        return [
            [
                (
                    pack.at[3 * depth + b * width : 3 * depth + (b + 1) * width, :],
                    w_buf.at[:, slot((f ^ c) * squares + b, width)],
                )
                for c, pack in enumerate(packs)
                for b in range(squares)
            ]
        ]

    def use(t, x, w_buf):
        return dot_nt(x, w_buf[...])

    def body(t, product, extras, outs):
        outs[0][...] = product.astype(BF16)

    return rows_call(
        body, "head_grad", xs, [], packs, (moves, use), 1, count * squares, (width, model), [width], number
    )


def hidden_units(xs, stack, number=0):
    model = xs[0].shape[1]
    count, depth, width = stack.shape
    width //= 2
    tile = min(256, width)
    starts = range(0, width, tile)

    def moves(weights, w_buf, f):
        return [
            [
                (weights[0].at[c, :, s : s + tile], w_buf.at[c * depth : (c + 1) * depth, s : s + tile])
                for c in range(count)
                for s in (start, width + start)
            ]
            for start in starts
        ]

    def use(t, x, w_buf):
        return [dot_nn(x, w_buf[:, s : s + tile]) for s in (starts[t], width + starts[t])]

    def body(t, products, extras, outs):
        here = pl.ds(starts[t], tile)
        up, gate = products
        sigmoid = 1.0 / (1.0 + jnp.exp(-gate))
        slope_up = gate * sigmoid
        outs[0][:, here] = (slope_up * up).astype(BF16)
        outs[1][:, here] = slope_up.astype(BF16)
        outs[2][:, here] = (up * sigmoid * (1.0 + gate * (1.0 - sigmoid))).astype(BF16)

    return rows_call(
        body, "hidden_units", xs, [], [stack], (moves, use), len(starts), 2 * count, (model, 2 * width), [width] * 3, number
    )


def hidden_grad(xs, slope_up, slope_gate, stack, number=0, cost=1):
    model = xs[0].shape[1]
    count, width, depth = stack.shape
    tile = min(512, width)
    starts = range(0, width, tile)

    def moves(weights, w_buf, f):
        return [
            [
                (weights[0].at[c, s : s + tile, :], w_buf.at[s : s + tile, c * depth : (c + 1) * depth])
                for c in range(count)
            ]
            for s in starts
        ]

    def use(t, x, w_buf):
        return dot_nt(x, w_buf[starts[t] : starts[t] + tile, :])

    def body(t, product, extras, outs):
        here = pl.ds(starts[t], tile)
        outs[0][:, here] = (product * extras[0][:, here].astype(F32)).astype(BF16)
        outs[0][:, pl.ds(width + starts[t], tile)] = (product * extras[1][:, here].astype(F32)).astype(BF16)

    return rows_call(
        body, "hidden_grad", xs, [slope_up, slope_gate], [stack], (moves, use),
        len(starts), count, (width, model), [2 * width], number, cost,
    )


def expand_kernel(sets, each, plan, dot, with_base, pairs, *refs):
    xs, refs = refs[:sets], refs[sets:]
    bases, refs = (refs[:1], refs[1:]) if with_base else ((), refs)
    weights, refs = refs[: sets * each], refs[sets * each :]
    outs, refs = refs[: max(pairs, 1)], refs[max(pairs, 1) :]
    w_buf, sem = refs[:2]
    step, f = pl.program_id(0), lax.axis_index("fsdp")
    count = w_buf.shape[1]
    d = lax.rem(step, count)

    def copies(j, c):
        there, moves = plan(weights[j * each : (j + 1) * each], c, f)
        return there, [
            pltpu.make_async_copy(src, w_buf.at[j, there, :, lanes], sem.at[j, there, n])
            for n, (src, lanes) in enumerate(moves)
        ]

    def start(place):
        for c in range(count):
            for j in range(sets):
                there, moves = copies(j, c)

                @pl.when(there == place)
                def _():
                    for copy in moves:
                        copy.start()

    if pairs:
        partner = {"tp": lax.axis_index("tp") ^ 1}
        send_buf, recv_buf, send_sem, recv_sem = refs[2:]

        def exchange(place, q):
            return pltpu.make_async_remote_copy(
                src_ref=send_buf.at[place, q],
                dst_ref=recv_buf.at[place, q],
                send_sem=send_sem.at[place, q],
                recv_sem=recv_sem.at[place, q],
                device_id=partner,
                device_id_type=pl.DeviceIdType.MESH,
            )

        @pl.when(step == 0)
        def _():
            barrier = pltpu.get_barrier_semaphore()
            pl.semaphore_signal(barrier, inc=1, device_id=partner, device_id_type=pl.DeviceIdType.MESH)
            pl.semaphore_wait(barrier, 1)

    pl.when(step == 0)(functools.partial(start, 0))
    pl.when(step < count - 1)(lambda: start(d + 1))

    @pl.when(step < count)
    def _():
        for j in range(sets):
            for n, (src, lanes) in enumerate(plan(weights[j * each : (j + 1) * each], 0, f)[1]):
                pltpu.make_async_copy(src, w_buf.at[j, d, :, lanes], sem.at[j, d, n]).wait()

    rows = outs[0].shape[0]

    def block(p):
        here = slice(p * rows, (p + 1) * rows)
        total = sum(dot(x[here, :], w_buf[j, d]) for j, x in enumerate(xs))
        for base in bases:
            total = total + base[here, :].astype(F32)
        return total

    if not pairs:
        outs[0][...] = block(0).astype(outs[0].dtype)
        return

    @pl.when(step < count)
    def _():
        for q in range(pairs):
            send_buf[d, q] = block(2 * q + 1).astype(BF16)
            exchange(d, q).start()

    @pl.when(step >= count)
    def _():
        for q in range(pairs):
            total = block(2 * q)
            exchange(d, q).wait_recv()
            outs[q][...] = (total + recv_buf[d, q].astype(F32)).astype(outs[q].dtype)

    @pl.when(step == 2 * count - 1)
    def _():
        for place in range(count):
            for q in range(pairs):
                exchange(place, q).wait_send()


def expand_call(name, xs, weights, each, plan, pieces, dot, chunk, rows, base=None, first=None, members=0, number=0, cost=1):
    count, w_shape = chunk
    depth = w_shape[1 if dot is dot_nn else 0]
    pairs = members // 2
    taken = rows * max(members, 1)
    block = 0 if first is None else first // members
    specs = [pl.BlockSpec((taken, x.shape[1]), lambda d: (block, 0)) for x in xs]
    bases = [] if base is None else [base]
    specs += [pl.BlockSpec((taken, depth), lambda d: (block, lax.rem(d, count))) for _ in bases]
    steps = 2 * count if pairs else count
    scratch = [pltpu.VMEM((len(xs), count) + w_shape, BF16), pltpu.SemaphoreType.DMA((len(xs), count, pieces))]
    types = [BF16]
    more = {}
    if pairs:
        types = [F32 if first == q == 0 else BF16 for q in range(pairs)]
        scratch += [pltpu.VMEM((count, pairs, rows, depth), BF16)] * 2 + [pltpu.SemaphoreType.DMA((count, pairs))] * 2
        more = {"collective_id": number, "has_side_effects": True}
    return pl.pallas_call(
        functools.partial(expand_kernel, len(xs), each, plan, dot, base is not None, pairs),
        grid_spec=pltpu.PrefetchScalarGridSpec(
            num_scalar_prefetch=0,
            grid=(steps,),
            in_specs=specs + any_specs(weights),
            out_specs=[pl.BlockSpec((rows, depth), lambda d: (0, lax.max(d + count - steps, 0))) for _ in types],
            scratch_shapes=scratch,
        ),
        out_shape=[jax.ShapeDtypeStruct((rows, count * depth), type_) for type_ in types],
        compiler_params=pltpu.CompilerParams(vmem_limit_bytes=VMEM_LIMIT, **more),
        cost_estimate=pl.CostEstimate(flops=cost, bytes_accessed=1, transcendentals=0),
        name=name,
    )(*xs, *bases, *weights)


def expand_stack(name, dot, xs, stacks, rows, **more):
    count, above, across = stacks[0].shape

    def plan(weights, c, f):
        return c, [(weights[0].at[c], pl.ds(0, across))]

    return expand_call(name, xs, stacks, 1, plan, 1, dot, (count, (above, across)), rows, **more)


def expand_heads(name, xs, packs, rows, **more):
    count, width = len(packs[0]), packs[0][0].shape[1]
    depth = packs_depth(packs[0][0])
    squares = depth // width

    def plan(weights, c, f):
        return f ^ c, [
            (weights[c].at[3 * depth + b * width : 3 * depth + (b + 1) * width, :], pl.ds(b * width, width))
            for b in range(squares)
        ]

    flat = [pack for list_ in packs for pack in list_]
    return expand_call(name, xs, flat, count, plan, squares, dot_nn, (count, (width, depth)), rows, **more)


def expand_project(name, xs, packs, rows, **more):
    count, width = len(packs[0]), packs[0][0].shape[1]
    depth = packs_depth(packs[0][0])

    def plan(weights, c, f):
        return f ^ c, [
            (weights[c].at[t * depth : (t + 1) * depth, :], pl.ds(t * width, width)) for t in range(3)
        ]

    flat = [pack for list_ in packs for pack in list_]
    return expand_call(name, xs, flat, count, plan, 3, dot_nt, (count, (depth, 3 * width)), rows, **more)


def pack_weights(att_proj, attn_out):
    depth, _, width = att_proj.shape
    parts = [att_proj[:, t, :] for t in range(3)]
    return jnp.concatenate(parts + [attn_out[:, s : s + width] for s in range(0, depth, width)], axis=0)


def packs_depth(pack):
    return pack.shape[0] // 4


def rows_grad_kernel(members, count, f_ref, *refs):
    xs, (g_ref, out_ref, x_buf, sem) = refs[:members], refs[-4:]
    rows, depth = xs[0].shape[0], xs[0].shape[1] // count
    chunks = [
        [
            pltpu.make_async_copy(
                x.at[:, d * depth : (d + 1) * depth], x_buf.at[d, m * rows : (m + 1) * rows, :], sem.at[d, m]
            )
            for m, x in enumerate(xs)
        ]
        for d in range(count)
    ]

    def start(d):
        for copy in chunks[d] if d < count else []:
            copy.start()

    def run(first):
        if first:
            start(0)
        for d, copies in enumerate(chunks):
            if first:
                start(d + 1)
                for copy in copies:
                    copy.wait()
            out_ref[d] = dot_tn(x_buf[d], g_ref[...]).astype(BF16)

    pl.when(pl.program_id(0) == 0)(functools.partial(run, True))
    pl.when(pl.program_id(0) > 0)(functools.partial(run, False))


def rows_grad(name, place, count, tile, beside, below, xs, g, stack=None, cost=1):
    rows, model = xs[0].shape
    tokens, width = g.shape
    depth = model // count
    given = [] if stack is None else [stack]
    tiles = width // tile
    shape = (count, -(-tiles // beside) * depth + below, beside * tile)
    return kernel_call(
        functools.partial(rows_grad_kernel, len(xs), count),
        name,
        cost,
        (tiles,),
        any_specs(xs) + any_specs(given) + [pl.BlockSpec((tokens, tile), lambda n, f: (0, n))],
        pl.BlockSpec((count, depth, tile), lambda n, f: (0, n // beside, n % beside)),
        jax.ShapeDtypeStruct(shape, BF16),
        [pltpu.VMEM((count, tokens, depth), BF16), pltpu.SemaphoreType.DMA((count, len(xs)))],
        {1 + len(xs): 0} if given else {},
    )(place, *xs, *given, g)


def columns_grad_kernel(sets, members, f_ref, *refs):
    xs, gs = refs[:sets], refs[sets : sets + members]
    out_ref, g_buf, sem = refs[-3:]
    d = pl.program_id(0)
    rows = gs[0].shape[0]
    total, _, depth = g_buf.shape
    tile = out_ref.shape[2]

    def start(c):
        for m, g in enumerate(gs):
            src, dst = g.at[:, slot(c, depth)], g_buf.at[c, m * rows : (m + 1) * rows, :]
            pltpu.make_async_copy(src, dst, sem.at[c, m]).start()

    @pl.when(d == 0)
    def _():
        start(0)

    @pl.when(d + 1 < total)
    def _():
        start(d + 1)

    for m, g in enumerate(gs):
        src, dst = g.at[:, :depth], g_buf.at[d, m * rows : (m + 1) * rows, :]
        pltpu.make_async_copy(src, dst, sem.at[d, m]).wait()
    first = 0
    for x in xs:
        for start in range(0, x.shape[1], 512):
            size = min(512, x.shape[1] - start)
            product = dot_tn(x[:, start : start + size], g_buf[d]).astype(BF16)
            for column in range(0, depth, tile):
                row = first + column // tile * x.shape[1] + start
                out_ref[0, row : row + size, :] = product[:, column : column + tile]
        first += x.shape[1] * (depth // tile)


def columns_grad(name, place, count, tile, shape, at, xs, gs, stack=None):
    model = gs[0].shape[1]
    tokens = xs[0].shape[0]
    depth = model // count
    height = sum(x.shape[1] for x in xs) * (depth // tile)
    given = [] if stack is None else [stack]
    return kernel_call(
        functools.partial(columns_grad_kernel, len(xs), len(gs)),
        name,
        1,
        (count,),
        [pl.BlockSpec(x.shape, lambda d, f: (0, 0)) for x in xs] + any_specs(gs) + any_specs(given),
        pl.BlockSpec((1, height, tile), lambda d, f: (d, *at)),
        jax.ShapeDtypeStruct((count, *shape), BF16),
        [pltpu.VMEM((count, tokens, depth), BF16), pltpu.SemaphoreType.DMA((count, len(gs)))],
        {1 + len(xs) + len(gs): 0} if given else {},
    )(place, *xs, *gs, *given)


def forward_kernel(block, reach, g_ref, q_ref, k_ref, v_ref, seg_ref, key_ref, out_ref, lse_ref):
    i = pl.program_id(0)
    g = g_ref[0]
    scale = LOG2E / math.sqrt(HD)
    heads = q_ref.shape[1] // HD

    def run(count):
        row = lax.broadcasted_iota(jnp.int32, (block, block), 0)
        column = lax.broadcasted_iota(jnp.int32, (block, block), 1)
        keeps, rows = [], []
        for back in range(count):
            b = i - back
            rows.append(pl.ds(pl.multiple_of((b ^ g) * block, block), block))
            keep = seg_ref[0] == key_ref[b]
            if back == 0:
                keep = (keep & (row > column)) | (row == column)
            if back == reach:
                keep = keep & (row < column)
            keeps.append(keep)
        for h in range(heads):
            lanes = slice(h * HD, (h + 1) * HD)
            q = q_ref[:, lanes]
            scores = [jnp.where(keep, dot_nt(q, k_ref[r, lanes]), NEGATIVE) for keep, r in zip(keeps, rows)]
            top = functools.reduce(jnp.maximum, [jnp.max(s, axis=1, keepdims=True) for s in scores])
            weights = [jnp.exp2((s - top) * scale) for s in scores]
            total = sum(jnp.sum(w, axis=1, keepdims=True) for w in weights)
            out = sum(dot_nn(w.astype(BF16), v_ref[r, lanes]) for w, r in zip(weights, rows))
            out_ref[:, lanes] = (out / total).astype(BF16)
            lse = top * scale + jnp.log2(total)
            lse_ref[h, 0] = jnp.transpose(jnp.broadcast_to(lse, (block, HD)))[0:1, :]

    for i_here in range(reach):
        pl.when(i == i_here)(functools.partial(run, i_here + 1))
    pl.when(i >= reach)(functools.partial(run, reach + 1))


def attend_forward(qkv, place, segment, key_code, block):
    tokens, width = qkv.shape
    heads = width // 3 // HD
    count = tokens // block
    reach = WINDOW // block
    return pl.pallas_call(
        functools.partial(forward_kernel, block, reach),
        grid_spec=pltpu.PrefetchScalarGridSpec(
            num_scalar_prefetch=1,
            grid=(count,),
            in_specs=[
                pl.BlockSpec((block, heads * HD), lambda i, g: (i ^ g[0], 0)),
                pl.BlockSpec((tokens, heads * HD), lambda i, g: (0, 1)),
                pl.BlockSpec((tokens, heads * HD), lambda i, g: (0, 2)),
                pl.BlockSpec((1, block, 1), lambda i, g: (i, 0, 0)),
                pl.BlockSpec((count, 1, block), lambda i, g: (0, 0, 0)),
            ],
            out_specs=[
                pl.BlockSpec((block, heads * HD), lambda i, g: (i ^ g[0], 0)),
                pl.BlockSpec((heads, 1, 1, block), lambda i, g: (0, i, 0, 0)),
            ],
        ),
        out_shape=[
            jax.ShapeDtypeStruct((tokens, heads * HD), BF16),
            jax.ShapeDtypeStruct((heads, count, 1, block), F32),
        ],
        compiler_params=pltpu.CompilerParams(vmem_limit_bytes=VMEM_LIMIT),
        cost_estimate=pl.CostEstimate(flops=1, bytes_accessed=1, transcendentals=0),
        name="attend_forward",
    )(place, qkv, qkv, qkv, segment.reshape(count, block, 1), key_code.reshape(count, 1, block))


def backward_kernel(
    block, reach, heads, g_ref, q_ref, k_ref, v_ref, grad_ref, out_ref, lse_ref, seg_ref, key_ref, cos_ref, sin_ref, result_ref, dq_ref, dk_ref, dv_ref, inner_ref
):
    g = g_ref[0]
    count = q_ref.shape[0] // block
    scale = 1.0 / math.sqrt(HD)

    def rows_of(b):
        return pl.ds(pl.multiple_of((b ^ g) * block, block), block)

    dq_ref[...] = jnp.zeros_like(dq_ref)
    dk_ref[...] = jnp.zeros_like(dk_ref)
    dv_ref[...] = jnp.zeros_like(dv_ref)

    def inner_block(i, carry):
        rows = rows_of(i)
        for h in range(heads):
            lanes = slice(h * HD, (h + 1) * HD)
            product = grad_ref[rows, lanes].astype(F32) * out_ref[rows, lanes].astype(F32)
            inner_ref[h, i] = jnp.sum(jnp.transpose(product), axis=0, keepdims=True)
        return carry

    lax.fori_loop(0, count, inner_block, 0)
    for back in range(reach + 1):

        def pair(i, carry, back=back):
            b = i - back
            query_rows, key_rows = rows_of(i), rows_of(b)
            keep = key_ref[b] == seg_ref[i]
            if back == 0 or back == reach:
                key = lax.broadcasted_iota(jnp.int32, (block, block), 0)
                query = lax.broadcasted_iota(jnp.int32, (block, block), 1)
                if back == 0:
                    keep = (keep & (query > key)) | (query == key)
                else:
                    keep = keep & (query < key)
            for h in range(heads):
                lanes = slice(h * HD, (h + 1) * HD)
                q, k = q_ref[query_rows, lanes], k_ref[key_rows, lanes]
                v, grad = v_ref[key_rows, lanes], grad_ref[query_rows, lanes]
                scores = dot_nt(k, q)
                weights = jnp.where(keep, jnp.exp2(scores * (scale * LOG2E) - lse_ref[h, i]), 0.0)
                grad_weights = dot_nt(v, grad)
                grad_scores = (weights * (grad_weights - inner_ref[h, i])).astype(BF16)
                dv_ref[key_rows, lanes] += dot_nn(weights.astype(BF16), grad)
                dk_ref[key_rows, lanes] += dot_nn(grad_scores, q)
                dq_ref[query_rows, lanes] += dot_tn(grad_scores, k)
            return carry

        lax.fori_loop(back, count, pair, 0)

    def store(i, carry):
        rows = pl.ds(pl.multiple_of(i * block, block), block)
        cosine, sine = cos_ref[rows, :], sin_ref[rows, :]
        for h in range(heads):
            lanes = slice(h * HD, (h + 1) * HD)
            for part, ref in enumerate((dq_ref, dk_ref)):
                value = ref[rows, lanes] * scale
                turned = value * cosine - pltpu.roll(value, HD // 2, 1) * sine
                result_ref[rows, (part * heads + h) * HD : (part * heads + h + 1) * HD] = turned.astype(BF16)
            result_ref[rows, (2 * heads + h) * HD : (2 * heads + h + 1) * HD] = dv_ref[rows, lanes].astype(BF16)
        return carry

    lax.fori_loop(0, count, store, 0)


def attend_backward(qkv, grad, out, lse, place, segment, key_code, cosine, sine, block, cost):
    tokens, width = qkv.shape
    heads = width // 3 // HD
    count = tokens // block
    reach = WINDOW // block
    return pl.pallas_call(
        functools.partial(backward_kernel, block, reach, heads),
        grid_spec=pltpu.PrefetchScalarGridSpec(
            num_scalar_prefetch=1,
            grid=(1,),
            in_specs=[
                pl.BlockSpec((tokens, heads * HD), lambda h, g: (0, 0)),
                pl.BlockSpec((tokens, heads * HD), lambda h, g: (0, 1)),
                pl.BlockSpec((tokens, heads * HD), lambda h, g: (0, 2)),
                pl.BlockSpec((tokens, heads * HD), lambda h, g: (0, 0)),
                pl.BlockSpec((tokens, heads * HD), lambda h, g: (0, 0)),
                pl.BlockSpec((heads, count, 1, block), lambda h, g: (0, 0, 0, 0)),
                pl.BlockSpec((count, 1, block), lambda h, g: (0, 0, 0)),
                pl.BlockSpec((count, block, 1), lambda h, g: (0, 0, 0)),
                pl.BlockSpec((tokens, HD), lambda h, g: (0, 0)),
                pl.BlockSpec((tokens, HD), lambda h, g: (0, 0)),
            ],
            out_specs=pl.BlockSpec((tokens, width), lambda h, g: (0, 0)),
            scratch_shapes=[
                pltpu.VMEM((tokens, heads * HD), F32),
                pltpu.VMEM((tokens, heads * HD), F32),
                pltpu.VMEM((tokens, heads * HD), F32),
                pltpu.VMEM((heads, count, 1, block), F32),
            ],
        ),
        out_shape=jax.ShapeDtypeStruct((tokens, width), BF16),
        compiler_params=pltpu.CompilerParams(vmem_limit_bytes=VMEM_LIMIT),
        cost_estimate=pl.CostEstimate(flops=cost, bytes_accessed=1, transcendentals=0),
        name="attend_backward",
    )(
        place, qkv, qkv, qkv, grad, out, lse,
        segment.reshape(count, 1, block), key_code.reshape(count, block, 1), cosine, sine,
    )


def local(inputs, att_proj, attn_out, ff_proj, ff_out, segments, pad_mask, positions, cotangent):
    tp_size, fsdp_size = lax.axis_size("tp"), lax.axis_size("fsdp")
    rows, model = inputs.shape
    members = SEQ_LEN // rows
    sets = tp_size // members
    index = lax.axis_index("tp")
    mine = index // members
    place = index % members
    block = min(512, rows)
    depth, head_width = att_proj.shape[0], att_proj.shape[2]
    ffn_width = ff_out.shape[0]
    place_tp = place.astype(jnp.int32).reshape(1)
    place_fsdp = lax.axis_index("fsdp").astype(jnp.int32).reshape(1)

    def swap(values, bit):
        return lax.ppermute(values, "tp", [(i, i ^ bit) for i in range(tp_size)])

    def turn(values, step):
        return lax.ppermute(values, "tp", [(i, (i + step * members) % tp_size) for i in range(tp_size)])

    def cross(values, mask):
        return lax.ppermute(values, "fsdp", [(i, i ^ mask) for i in range(fsdp_size)])

    def after(value, *others):
        return lax.optimization_barrier((value, others))[0]

    chain = []

    def then(function, *args, due=()):
        args, _ = lax.optimization_barrier((args, (chain[-1], due)))
        result = function(*args)
        chain.append(jax.tree.leaves(result)[0])
        return result

    def last():
        return chain[-1]

    def group_far(values):
        blocks = {0: values}
        bit = members // 2
        while bit > 1:
            for mask in sorted(blocks, reverse=True):
                blocks[mask | bit] = swap(blocks[mask], bit)
            bit //= 2
        return [blocks[mask] for mask in range(0, members, 2)]

    def scatter_far(sums):
        sums = dict(sums)
        parts = [sums[0]]
        bit = 2
        while bit < members:
            for mask in sorted((m for m in sums if m & bit), reverse=True):
                received = swap(sums.pop(mask), bit)
                if mask == bit:
                    parts.append(received)
                else:
                    sums[mask ^ bit] = (sums[mask ^ bit].astype(F32) + received.astype(F32)).astype(BF16)
            bit *= 2
        return parts

    half = members // 2

    def share(function, *args, number, due=(), due_near=(), cost_near=1):
        sums = {}
        for part, first in enumerate((half, 0)):
            cost = 1 if first else cost_near
            call = functools.partial(function, rows=rows, first=first, members=half, number=number + part, cost=cost)
            outs = then(lambda xs, weights, *base: call(xs, weights, base=base[0] if base else None), *args, due=due)
            sums.update({first + 2 * q: out for q, out in enumerate(outs)})
            due = due_near
        return sums

    def gather(shard):
        return lax.all_gather(shard, "fsdp", axis=0)

    def scatter(stacked):
        return lax.psum_scatter(stacked.reshape(-1, stacked.shape[-1]), "fsdp", scatter_dimension=0, tiled=True)

    def settle(pieces, *gates):
        return pieces[:1] + [turn(after(pieces[step], *gates), sets - step) for step in range(1, sets)]

    def settled(pieces):
        return sum(piece.astype(F32) for piece in pieces)

    normed_all, packs = start_exchange(inputs, pack_weights(att_proj, attn_out), members, sets, fsdp_size)
    chain.append(normed_all[0])
    up_gate, down, cotangent_late = after((ff_proj.reshape(depth, -1), ff_out, cotangent), last())
    w_ffn, w_down = [gather(up_gate)], [gather(down)]
    turned_up_gate = [turn(up_gate, step) for step in range(1, sets)]
    cotangent_far = group_far(cotangent_late)

    segment = lax.dynamic_slice_in_dim(segments, mine * SEQ_LEN, SEQ_LEN)
    padding = lax.dynamic_slice_in_dim(pad_mask, mine * SEQ_LEN, SEQ_LEN)
    key_code = jnp.where(padding == 1, segment, -1)
    spots = lax.dynamic_slice_in_dim(positions, mine * SEQ_LEN, SEQ_LEN).reshape(members, rows)
    spots = jnp.concatenate([lax.dynamic_index_in_dim(spots, place ^ mask, 0, False) for mask in range(members)])
    cosine, sine = rope_tables(spots)

    x_float = inputs.astype(F32)
    qkv, attended = [], []
    for step in range(sets):
        qkv.append(then(project, normed_all, packs[step], cosine, sine))
        attended.append(then(lambda part: attend_forward(part, place_tp, segment, key_code, block), qkv[step]))
    heads_low = [out for out, _ in attended]
    sums = share(functools.partial(expand_heads, "attn_branch"), heads_low, packs, number=1)
    w_ffn += [gather(after(part, last(), cotangent_far)) for part in turned_up_gate]
    resid = x_float + settled(scatter_far(sums))
    normed_two_far = group_far(layer_norm(resid).astype(BF16))
    turned_down = [turn(after(ff_out, normed_two_far[-1]), step) for step in range(1, sets)]

    hidden, slopes, grad_ffn, partial = [], [], [], None
    for step in range(sets):
        if step == 0:
            (low, *slope), normed_two_all = then(functools.partial(hidden_units, number=9), normed_two_far, w_ffn[0])
        else:
            (low, *slope), _ = then(hidden_units, normed_two_all, w_ffn[step])
        hidden.append(low)
        slopes.append(slope)
    w_down += [gather(after(part, last())) for part in turned_down]
    ffn_rows = 2 * ffn_width
    grad_expand = functools.partial(expand_stack, "grad_normed_two", dot_nt)
    up_grad = functools.partial(rows_grad, "grad_ffn", place_fsdp, fsdp_size, depth, 1, 0)
    for step in range(sets):
        if step == 0:
            (grad_low,), cotangent_all = then(functools.partial(hidden_grad, number=10, cost=LONG), cotangent_far, *slopes[0], w_down[0])
        else:
            (grad_low,), _ = then(hidden_grad, cotangent_all, *slopes[step], w_down[step])
        grad_ffn.append(scatter(then(up_grad, normed_two_all, grad_low)))
        base = [] if partial is None else [partial]
        if step < sets - 1:
            call = lambda x, w, *b: grad_expand([x], [w], members * rows, base=b[0] if b else None)[0]
            partial = then(call, grad_low, w_ffn[step], *base)
    sums = share(grad_expand, [grad_low], [w_ffn[-1]], *base, number=3)
    ffn_sums = share(functools.partial(expand_stack, "ffn_branch", dot_nn), hidden, w_down, number=5)
    grad_normed_two = settled(after(scatter_far(sums), ffn_sums[half]))
    grad_resid = cotangent.astype(F32) + layer_norm_back(resid, grad_normed_two)
    resid_grad_low = grad_resid.astype(BF16)
    resid_grad_far = group_far(resid_grad_low)
    shape, at = (sets * ffn_width, depth), (0, 0)
    down_grad = functools.partial(columns_grad, "grad_down", place_fsdp, fsdp_size, depth, shape, at)
    grad_down = scatter(then(down_grad, hidden, cotangent_all, due=(resid_grad_low,)))

    grad_attn, grad_project = [None] * sets, [None] * sets
    shape, at = (2 * depth, 2 * head_width), (1, 1)
    heads_grad = functools.partial(columns_grad, "grad_heads", place_fsdp, fsdp_size, head_width, shape, at)
    project_grad = functools.partial(rows_grad, "grad_attn", place_fsdp, fsdp_size, head_width, 2, 0)
    held = None
    for step in reversed(range(sets)):
        if step == sets - 1:
            call = functools.partial(head_grad_of, number=11)
            (head_grad,), resid_grad_all = then(call, resid_grad_far, packs[step], due=tuple(grad_ffn[:1]))
            grad_up = settle([piece[:ffn_width] for piece in grad_ffn], last())
            ffn_branch = scatter_far(after(ffn_sums, last()))
        else:
            (head_grad,), _ = then(head_grad_of, resid_grad_all, packs[step])
        grad_project[step] = then(
            lambda part, grad, out, lse: attend_backward(
                part, grad, out, lse, place_tp, segment, key_code, cosine, sine, block, LONG if step == sets - 1 else 1
            ),
            qkv[step], head_grad, heads_low[step], attended[step][1],
        )
        ready = (grad_up[1:], ffn_branch[1:]) if step == 0 else ()
        stacked = then(heads_grad, [heads_low[step]], resid_grad_all, due=ready)
        if held is not None:
            grad_attn[step + 1] = scatter(after(held, last()))
            grad_gate = settle([piece[ffn_width:] for piece in grad_ffn], grad_up[1:])
            grad_down = settle([grad_down[j * ffn_width : (j + 1) * ffn_width] for j in range(sets)], last())
        held = then(project_grad, normed_all, grad_project[step], stacked)
    grad_attn[0] = scatter(held)
    call = functools.partial(expand_project, "grad_normed")
    due = ((), tuple(grad_gate[1:]))
    sums = share(call, grad_project, packs, number=7, due=due[0], due_near=due[1], cost_near=100 * LONG)
    grad_normed = scatter_far(sums)
    output = (resid + settled(ffn_branch)).astype(BF16)
    grad_attn = settle(grad_attn)
    grad_normed = settled(after(grad_normed, grad_attn[1:], grad_down[1:]))
    grad_input = (grad_resid + layer_norm_back(x_float, grad_normed)).astype(BF16)
    grad_attn = settled(grad_attn)

    def beside(values, first, size, count):
        return jnp.concatenate([values[(first + i) * size : (first + i + 1) * size] for i in range(count)], axis=1)

    query, key = grad_attn[:depth, :head_width], grad_attn[:depth, head_width:]
    value, squares = grad_attn[depth:, :head_width], grad_attn[depth:, head_width:]
    blocks = ffn_width // depth

    return (
        output,
        grad_input,
        jnp.stack([query, key, value], axis=1),
        beside(squares, 0, head_width, depth // head_width),
        jnp.stack([beside(settled(part), 0, depth, blocks) for part in (grad_up, grad_gate)], axis=1),
        settled(grad_down),
    )


def solution(mesh):
    rows_spec = P(("fsdp", "tp"), None)
    weights = (P("fsdp", None, "tp"), P("tp", "fsdp"), P("fsdp", None, "tp"), P("tp", "fsdp"))
    return jax.shard_map(
        local,
        mesh=mesh,
        in_specs=(rows_spec,) + weights + (P("fsdp"),) * 3 + (rows_spec,),
        out_specs=(rows_spec, rows_spec) + weights,
        check_vma=False,
    )
```

```python
import functools
import math

import jax
import jax.numpy as jnp
from jax import lax
from jax.experimental import pallas as pl
from jax.experimental.pallas import tpu as pltpu
from jax.sharding import PartitionSpec as P

HD = 128
WINDOW = 1024
SEQ_LEN = 2048
EPSILON = 1e-05
NEGATIVE = -1e30
ROPE_BASE = 10000.0
LOG2E = math.log2(math.e)
LONG = 10**12
VMEM_LIMIT = 56 * 1024 * 1024
F32 = jnp.float32
BF16 = jnp.bfloat16


def dot_nn(left, right):
    return lax.dot_general(left, right, (((1,), (0,)), ((), ())), preferred_element_type=F32)


def dot_nt(left, right):
    return lax.dot_general(left, right, (((1,), (1,)), ((), ())), preferred_element_type=F32)


def dot_tn(left, right):
    return lax.dot_general(left, right, (((0,), (0,)), ((), ())), preferred_element_type=F32)


def layer_norm(values):
    average = jnp.mean(values, axis=-1, keepdims=True)
    centered = values - average
    variance = jnp.mean(centered * centered, axis=-1, keepdims=True)
    return centered * lax.rsqrt(variance + EPSILON)


def layer_norm_back(values, grad):
    average = jnp.mean(values, axis=-1, keepdims=True)
    centered = values - average
    variance = jnp.mean(centered * centered, axis=-1, keepdims=True)
    root = lax.rsqrt(variance + EPSILON)
    normed = centered * root
    inner = jnp.mean(normed * grad, axis=-1, keepdims=True)
    return root * (grad - jnp.mean(grad, axis=-1, keepdims=True) - normed * inner)


def rope_tables(positions):
    half = HD // 2
    frequency = ROPE_BASE ** (-(jnp.arange(half, dtype=F32) * 2.0 / HD))
    angles = positions.astype(F32)[:, None] * frequency[None, :]
    cosine, sine = jnp.cos(angles), jnp.sin(angles)
    return jnp.concatenate([cosine, cosine], axis=-1), jnp.concatenate([-sine, sine], axis=-1)


def kernel_call(kernel, name, cost, grid, in_specs, out_specs, out_shapes, scratch, aliases={}):
    return pl.pallas_call(
        kernel,
        grid_spec=pltpu.PrefetchScalarGridSpec(
            num_scalar_prefetch=1, grid=grid, in_specs=in_specs, out_specs=out_specs, scratch_shapes=scratch
        ),
        out_shape=out_shapes,
        input_output_aliases=aliases,
        compiler_params=pltpu.CompilerParams(vmem_limit_bytes=VMEM_LIMIT),
        cost_estimate=pl.CostEstimate(flops=cost, bytes_accessed=1, transcendentals=0),
        name=name,
    )


def any_specs(arrays):
    return [pl.BlockSpec(memory_space=pl.ANY)] * len(arrays)


def slot(index, size):
    return pl.ds(pl.multiple_of(index * size, size), size)


PIECES = 4


def start_kernel(members, sets, count, x_ref, pack_ref, *refs):
    normed, refs = dict(zip(range(0, members, 2), refs)), refs[members // 2 :]
    packs = [(pack_ref,) + refs[: count - 1]]
    refs = refs[count - 1 :]
    for _ in range(1, sets):
        packs.append(refs[:count])
        refs = refs[count:]
    low_ref, local_sem, send_sem, recv_sem = refs
    t, f = lax.axis_index("tp"), lax.axis_index("fsdp")
    total = members * sets
    climb = [1 << i for i in range(count.bit_length() - 1)]
    group = [1 << i for i in range(1, members.bit_length() - 1)][::-1]
    shifts = [lax.rem(t + step * members, total) for step in range(1, sets)]

    barrier = pltpu.get_barrier_semaphore()
    partners = [{"tp": t ^ bit} for bit in group] + [{"tp": s} for s in shifts] + [{"fsdp": f ^ bit} for bit in climb]
    for partner in partners:
        pl.semaphore_signal(barrier, inc=1, device_id=partner, device_id_type=pl.DeviceIdType.MESH)
    pl.semaphore_wait(barrier, len(partners))

    started, waited = [], []

    def send(src, dst, partner):
        n = len(started)
        copy = pltpu.make_async_remote_copy(
            src_ref=src,
            dst_ref=dst,
            send_sem=send_sem.at[n],
            recv_sem=recv_sem.at[n],
            device_id=partner,
            device_id_type=pl.DeviceIdType.MESH,
        )
        copy.start()
        started.append(copy)
        return copy

    def await_block(copy):
        copy.wait_recv()
        waited.append(copy)

    orders = (climb, climb[::-1]) * (PIECES // 2)
    size = pack_ref.shape[0] // PIECES
    came = [{} for _ in range(sets)]

    def pass_on(step, half, mask):
        order = orders[half]
        here = pl.ds(half * size, size)
        for n, bit in enumerate(order):
            if all(not mask & later for later in order[n:]):
                copy = send(packs[step][mask].at[here, :], packs[step][mask | bit].at[here, :], {"fsdp": f ^ bit})
                came[step][half, mask | bit] = copy

    def pass_all(step, halves):
        for level in range(1, len(climb)):
            for half in halves:
                for mask in range(count):
                    if mask.bit_count() == level and not mask & orders[half][-1]:
                        await_block(came[step][half, mask])
                        pass_on(step, half, mask)

    over = {}
    for half in range(PIECES):
        here = pl.ds(half * size, size)
        for step in range(1, sets):
            over[step, half] = send(pack_ref.at[here, :], packs[step][0].at[here, :], {"tp": shifts[step - 1]})
    for half in range(PIECES):
        pass_on(0, half, 0)

    rows = x_ref.shape[0]
    tile = min(32, rows)

    def norm(i, carry):
        here = pl.ds(pl.multiple_of(i * tile, tile), tile)
        low_ref[here, :] = layer_norm(x_ref[here, :].astype(F32)).astype(BF16)
        return carry

    lax.fori_loop(0, rows // tile, norm, 0)
    keep = pltpu.make_async_copy(low_ref, normed[0], local_sem)
    keep.start()
    blocks = {}
    for bit in group:
        blocks[bit] = send(low_ref, normed[bit], {"tp": t ^ bit})
    pass_all(0, range(PIECES))
    for step in range(1, sets):
        for pair in range(0, PIECES, 2):
            for half in (pair, pair + 1):
                await_block(over[step, half])
                pass_on(step, half, 0)
            if pair:
                pass_all(step, (pair - 2, pair - 1))
        pass_all(step, (PIECES - 2, PIECES - 1))
    for mask in sorted(range(2, members, 2), reverse=True, key=lambda m: (m & -m, m)):
        below = [bit for bit in group if bit < mask & -mask]
        if below:
            await_block(blocks[mask])
        for bit in below:
            blocks[mask | bit] = send(normed[mask], normed[mask | bit], {"tp": t ^ bit})
    keep.wait()
    for copy in started:
        copy.wait_send()
        if not any(copy is other for other in waited):
            copy.wait_recv()


def start_exchange(x, pack, members, sets, count):
    half = members // 2
    sends = PIECES * ((count - 1) * sets + sets - 1) + half - 1
    shapes = [jax.ShapeDtypeStruct(x.shape, BF16)] * half + [jax.ShapeDtypeStruct(pack.shape, BF16)] * (count * sets - 1)
    outs = pl.pallas_call(
        functools.partial(start_kernel, members, sets, count),
        in_specs=[pl.BlockSpec(memory_space=pltpu.VMEM), pl.BlockSpec(memory_space=pl.ANY)],
        out_specs=any_specs(shapes),
        out_shape=shapes,
        scratch_shapes=[
            pltpu.VMEM(x.shape, BF16),
            pltpu.SemaphoreType.DMA,
            pltpu.SemaphoreType.DMA((sends,)),
            pltpu.SemaphoreType.DMA((sends,)),
        ],
        compiler_params=pltpu.CompilerParams(vmem_limit_bytes=VMEM_LIMIT, collective_id=0, has_side_effects=True),
        cost_estimate=pl.CostEstimate(flops=1, bytes_accessed=1, transcendentals=0),
        name="start_exchange",
    )(x, pack)
    packs = [pack] + list(outs[half:])
    return outs[:half], [packs[step * count : (step + 1) * count] for step in range(sets)]


def rows_kernel(body, plan, members, extras, count, number, *refs):
    held = members // 2 if number else members
    xs, refs = refs[:held], refs[held:]
    extra_refs, refs = refs[:extras], refs[extras:]
    weights, refs = refs[:count], refs[count:]
    if number:
        *refs, send_sem, recv_sem = refs
        xs = [block for pair in zip(xs, refs[-4 - held : -4]) for block in pair]
        outs, refs = refs[: -4 - held], refs[-4:]
    else:
        outs, refs = refs[:-4], refs[-4:]
    x_buf, w_buf, x_sem, w_sem = refs
    i, f = pl.program_id(0), lax.axis_index("fsdp")
    moves, use = plan
    tiles = [
        [pltpu.make_async_copy(src, dst, w_sem.at[t, n]) for n, (src, dst) in enumerate(pairs)]
        for t, pairs in enumerate(moves(weights, w_buf, f))
    ]
    order = list(range(0, members, 2)) + list(range(1, members, 2)) if number else list(range(members))
    x_copies = [pltpu.make_async_copy(xs[m], x_buf.at[n], x_sem.at[n]) for n, m in enumerate(order)]
    exchanges = []
    if number:
        partner = {"tp": lax.axis_index("tp") ^ 1}
        exchanges = [
            pltpu.make_async_remote_copy(
                src_ref=xs[2 * q],
                dst_ref=xs[2 * q + 1],
                send_sem=send_sem.at[q],
                recv_sem=recv_sem.at[q],
                device_id=partner,
                device_id_type=pl.DeviceIdType.MESH,
            )
            for q in range(held)
        ]

    def start(n):
        if n < len(tiles):
            for copy in tiles[n]:
                copy.start()
        elif n - len(tiles) + 1 < held:
            x_copies[n - len(tiles) + 1].start()

    def run(first):
        if first:
            x_copies[0].start()
            start(0)
            start(1)
            if number:
                barrier = pltpu.get_barrier_semaphore()
                pl.semaphore_signal(barrier, inc=1, device_id=partner, device_id_type=pl.DeviceIdType.MESH)
                pl.semaphore_wait(barrier, 1)
                for exchange in exchanges:
                    exchange.start()
        pltpu.make_async_copy(xs[0], x_buf.at[i], x_sem.at[i]).wait()
        for t, copies in enumerate(tiles):
            if first:
                for copy in copies:
                    copy.wait()
                start(t + 2)
            body(t, use(t, x_buf[i], w_buf), extra_refs, outs)
        if first:
            for n in range(len(tiles) + 2, len(tiles) + held - 1):
                start(n)

    for q, exchange in enumerate(exchanges):

        @pl.when(i == 1 + q)
        def _():
            exchange.wait()
            x_copies[held + q].start()

    pl.when(i == 0)(functools.partial(run, True))
    pl.when(i > 0)(functools.partial(run, False))


def rows_call(body, name, xs, extras, weights, plan, tiles, copies, w_shape, widths, number, cost=1):
    rows, model = xs[0].shape
    held, count = len(xs), len(weights)
    members = 2 * held if number else held
    arrived = held if number else 0

    def here(i):
        return (i % held * 2 + i // held if number else i, 0)

    outs = pl.pallas_call(
        functools.partial(rows_kernel, body, plan, members, len(extras), count, number),
        grid_spec=pltpu.PrefetchScalarGridSpec(
            num_scalar_prefetch=0,
            grid=(members,),
            in_specs=any_specs(xs) + [pl.BlockSpec((rows, e.shape[1]), here) for e in extras] + any_specs(weights),
            out_specs=[pl.BlockSpec((rows, width), here) for width in widths] + any_specs(xs[:arrived]),
            scratch_shapes=[
                pltpu.VMEM((members, rows, model), BF16),
                pltpu.VMEM(w_shape, BF16),
                pltpu.SemaphoreType.DMA((members,)),
                pltpu.SemaphoreType.DMA((tiles, copies)),
            ]
            + [pltpu.SemaphoreType.DMA((held,))] * (2 if number else 0),
        ),
        out_shape=[jax.ShapeDtypeStruct((members * rows, width), BF16) for width in widths]
        + [jax.ShapeDtypeStruct((rows, model), BF16)] * arrived,
        compiler_params=pltpu.CompilerParams(
            vmem_limit_bytes=VMEM_LIMIT, **({"collective_id": number, "has_side_effects": True} if number else {})
        ),
        cost_estimate=pl.CostEstimate(flops=cost, bytes_accessed=1, transcendentals=0),
        name=name,
    )(*xs, *extras, *weights)
    if not number:
        return outs, list(xs)
    return outs[: len(widths)], [block for pair in zip(xs, outs[len(widths) :]) for block in pair]


def project(xs, packs, cosine, sine, number=0):
    model, count = xs[0].shape[1], len(packs)
    depth, width = model // count, packs[0].shape[1]

    def moves(packs, w_buf, f):
        return [
            [(pack.at[t * depth : (t + 1) * depth, :], w_buf.at[t, slot(f ^ c, depth), :]) for c, pack in enumerate(packs)]
            for t in range(3)
        ]

    def use(t, x, w_buf):
        return dot_nn(x, w_buf[t])

    def body(t, product, extras, outs):
        for column in range(0, width, HD):
            value = product[:, column : column + HD]
            if t < 2:
                value = value * extras[0][...] + pltpu.roll(value, HD // 2, 1) * extras[1][...]
            outs[0][:, t * width + column : t * width + column + HD] = value.astype(BF16)

    return rows_call(
        body, "project", xs, [cosine, sine], packs, (moves, use), 3, count, (3, model, width), [3 * width], number
    )


def head_grad_of(xs, packs, number=0):
    model, count = xs[0].shape[1], len(packs)
    depth, width = model // count, packs[0].shape[1]
    squares = depth // width

    def moves(packs, w_buf, f):
        return [
            [
                (
                    pack.at[3 * depth + b * width : 3 * depth + (b + 1) * width, :],
                    w_buf.at[:, slot((f ^ c) * squares + b, width)],
                )
                for c, pack in enumerate(packs)
                for b in range(squares)
            ]
        ]

    def use(t, x, w_buf):
        return dot_nt(x, w_buf[...])

    def body(t, product, extras, outs):
        outs[0][...] = product.astype(BF16)

    return rows_call(
        body, "head_grad", xs, [], packs, (moves, use), 1, count * squares, (width, model), [width], number
    )


def hidden_units(xs, stack, number=0):
    model = xs[0].shape[1]
    count, depth, width = stack.shape
    width //= 2
    tile = min(256, width)
    starts = range(0, width, tile)

    def moves(weights, w_buf, f):
        return [
            [
                (weights[0].at[c, :, s : s + tile], w_buf.at[c * depth : (c + 1) * depth, s : s + tile])
                for c in range(count)
                for s in (start, width + start)
            ]
            for start in starts
        ]

    def use(t, x, w_buf):
        return [dot_nn(x, w_buf[:, s : s + tile]) for s in (starts[t], width + starts[t])]

    def body(t, products, extras, outs):
        here = pl.ds(starts[t], tile)
        up, gate = products
        sigmoid = 1.0 / (1.0 + jnp.exp(-gate))
        slope_up = gate * sigmoid
        outs[0][:, here] = (slope_up * up).astype(BF16)
        outs[1][:, here] = slope_up.astype(BF16)
        outs[2][:, here] = (up * sigmoid * (1.0 + gate * (1.0 - sigmoid))).astype(BF16)

    return rows_call(
        body, "hidden_units", xs, [], [stack], (moves, use), len(starts), 2 * count, (model, 2 * width), [width] * 3, number
    )


def hidden_grad(xs, slope_up, slope_gate, stack, number=0, cost=1):
    model = xs[0].shape[1]
    count, width, depth = stack.shape
    tile = min(512, width)
    starts = range(0, width, tile)

    def moves(weights, w_buf, f):
        return [
            [
                (weights[0].at[c, s : s + tile, :], w_buf.at[s : s + tile, c * depth : (c + 1) * depth])
                for c in range(count)
            ]
            for s in starts
        ]

    def use(t, x, w_buf):
        return dot_nt(x, w_buf[starts[t] : starts[t] + tile, :])

    def body(t, product, extras, outs):
        here = pl.ds(starts[t], tile)
        outs[0][:, here] = (product * extras[0][:, here].astype(F32)).astype(BF16)
        outs[0][:, pl.ds(width + starts[t], tile)] = (product * extras[1][:, here].astype(F32)).astype(BF16)

    return rows_call(
        body, "hidden_grad", xs, [slope_up, slope_gate], [stack], (moves, use),
        len(starts), count, (width, model), [2 * width], number, cost,
    )


def expand_kernel(sets, each, plan, dot, with_base, pairs, *refs):
    xs, refs = refs[:sets], refs[sets:]
    bases, refs = (refs[:1], refs[1:]) if with_base else ((), refs)
    weights, refs = refs[: sets * each], refs[sets * each :]
    outs, refs = refs[: max(pairs, 1)], refs[max(pairs, 1) :]
    w_buf, sem = refs[:2]
    step, f = pl.program_id(0), lax.axis_index("fsdp")
    count = w_buf.shape[1]
    d = lax.rem(step, count)

    def copies(j, c):
        there, moves = plan(weights[j * each : (j + 1) * each], c, f)
        return there, [
            pltpu.make_async_copy(src, w_buf.at[j, there, :, lanes], sem.at[j, there, n])
            for n, (src, lanes) in enumerate(moves)
        ]

    def start(place):
        for c in range(count):
            for j in range(sets):
                there, moves = copies(j, c)

                @pl.when(there == place)
                def _():
                    for copy in moves:
                        copy.start()

    if pairs:
        partner = {"tp": lax.axis_index("tp") ^ 1}
        send_buf, recv_buf, send_sem, recv_sem = refs[2:]

        def exchange(place, q):
            return pltpu.make_async_remote_copy(
                src_ref=send_buf.at[place, q],
                dst_ref=recv_buf.at[place, q],
                send_sem=send_sem.at[place, q],
                recv_sem=recv_sem.at[place, q],
                device_id=partner,
                device_id_type=pl.DeviceIdType.MESH,
            )

        @pl.when(step == 0)
        def _():
            barrier = pltpu.get_barrier_semaphore()
            pl.semaphore_signal(barrier, inc=1, device_id=partner, device_id_type=pl.DeviceIdType.MESH)
            pl.semaphore_wait(barrier, 1)

    pl.when(step == 0)(functools.partial(start, 0))
    pl.when(step < count - 1)(lambda: start(d + 1))

    @pl.when(step < count)
    def _():
        for j in range(sets):
            for n, (src, lanes) in enumerate(plan(weights[j * each : (j + 1) * each], 0, f)[1]):
                pltpu.make_async_copy(src, w_buf.at[j, d, :, lanes], sem.at[j, d, n]).wait()

    rows = outs[0].shape[0]

    def block(p):
        here = slice(p * rows, (p + 1) * rows)
        total = sum(dot(x[here, :], w_buf[j, d]) for j, x in enumerate(xs))
        for base in bases:
            total = total + base[here, :].astype(F32)
        return total

    if not pairs:
        outs[0][...] = block(0).astype(outs[0].dtype)
        return

    @pl.when(step < count)
    def _():
        for q in range(pairs):
            send_buf[d, q] = block(2 * q + 1).astype(BF16)
            exchange(d, q).start()

    @pl.when(step >= count)
    def _():
        for q in range(pairs):
            total = block(2 * q)
            exchange(d, q).wait_recv()
            outs[q][...] = (total + recv_buf[d, q].astype(F32)).astype(outs[q].dtype)

    @pl.when(step == 2 * count - 1)
    def _():
        for place in range(count):
            for q in range(pairs):
                exchange(place, q).wait_send()


def expand_call(name, xs, weights, each, plan, pieces, dot, chunk, rows, base=None, first=None, members=0, number=0, cost=1):
    count, w_shape = chunk
    depth = w_shape[1 if dot is dot_nn else 0]
    pairs = members // 2
    taken = rows * max(members, 1)
    block = 0 if first is None else first // members
    specs = [pl.BlockSpec((taken, x.shape[1]), lambda d: (block, 0)) for x in xs]
    bases = [] if base is None else [base]
    specs += [pl.BlockSpec((taken, depth), lambda d: (block, lax.rem(d, count))) for _ in bases]
    steps = 2 * count if pairs else count
    scratch = [pltpu.VMEM((len(xs), count) + w_shape, BF16), pltpu.SemaphoreType.DMA((len(xs), count, pieces))]
    types = [BF16]
    more = {}
    if pairs:
        types = [F32 if first == q == 0 else BF16 for q in range(pairs)]
        scratch += [pltpu.VMEM((count, pairs, rows, depth), BF16)] * 2 + [pltpu.SemaphoreType.DMA((count, pairs))] * 2
        more = {"collective_id": number, "has_side_effects": True}
    return pl.pallas_call(
        functools.partial(expand_kernel, len(xs), each, plan, dot, base is not None, pairs),
        grid_spec=pltpu.PrefetchScalarGridSpec(
            num_scalar_prefetch=0,
            grid=(steps,),
            in_specs=specs + any_specs(weights),
            out_specs=[pl.BlockSpec((rows, depth), lambda d: (0, lax.max(d + count - steps, 0))) for _ in types],
            scratch_shapes=scratch,
        ),
        out_shape=[jax.ShapeDtypeStruct((rows, count * depth), type_) for type_ in types],
        compiler_params=pltpu.CompilerParams(vmem_limit_bytes=VMEM_LIMIT, **more),
        cost_estimate=pl.CostEstimate(flops=cost, bytes_accessed=1, transcendentals=0),
        name=name,
    )(*xs, *bases, *weights)


def expand_stack(name, dot, xs, stacks, rows, **more):
    count, above, across = stacks[0].shape

    def plan(weights, c, f):
        return c, [(weights[0].at[c], pl.ds(0, across))]

    return expand_call(name, xs, stacks, 1, plan, 1, dot, (count, (above, across)), rows, **more)


def expand_heads(name, xs, packs, rows, **more):
    count, width = len(packs[0]), packs[0][0].shape[1]
    depth = packs_depth(packs[0][0])
    squares = depth // width

    def plan(weights, c, f):
        return f ^ c, [
            (weights[c].at[3 * depth + b * width : 3 * depth + (b + 1) * width, :], pl.ds(b * width, width))
            for b in range(squares)
        ]

    flat = [pack for list_ in packs for pack in list_]
    return expand_call(name, xs, flat, count, plan, squares, dot_nn, (count, (width, depth)), rows, **more)


def expand_project(name, xs, packs, rows, **more):
    count, width = len(packs[0]), packs[0][0].shape[1]
    depth = packs_depth(packs[0][0])

    def plan(weights, c, f):
        return f ^ c, [
            (weights[c].at[t * depth : (t + 1) * depth, :], pl.ds(t * width, width)) for t in range(3)
        ]

    flat = [pack for list_ in packs for pack in list_]
    return expand_call(name, xs, flat, count, plan, 3, dot_nt, (count, (depth, 3 * width)), rows, **more)


def pack_weights(att_proj, attn_out):
    depth, _, width = att_proj.shape
    parts = [att_proj[:, t, :] for t in range(3)]
    return jnp.concatenate(parts + [attn_out[:, s : s + width] for s in range(0, depth, width)], axis=0)


def packs_depth(pack):
    return pack.shape[0] // 4


def rows_grad_kernel(members, count, f_ref, *refs):
    xs, (g_ref, out_ref, x_buf, sem) = refs[:members], refs[-4:]
    rows, depth = xs[0].shape[0], xs[0].shape[1] // count
    chunks = [
        [
            pltpu.make_async_copy(
                x.at[:, d * depth : (d + 1) * depth], x_buf.at[d, m * rows : (m + 1) * rows, :], sem.at[d, m]
            )
            for m, x in enumerate(xs)
        ]
        for d in range(count)
    ]

    def start(d):
        for copy in chunks[d] if d < count else []:
            copy.start()

    def run(first):
        if first:
            start(0)
        for d, copies in enumerate(chunks):
            if first:
                start(d + 1)
                for copy in copies:
                    copy.wait()
            out_ref[d] = dot_tn(x_buf[d], g_ref[...]).astype(BF16)

    pl.when(pl.program_id(0) == 0)(functools.partial(run, True))
    pl.when(pl.program_id(0) > 0)(functools.partial(run, False))


def rows_grad(name, place, count, tile, beside, below, xs, g, stack=None, cost=1):
    rows, model = xs[0].shape
    tokens, width = g.shape
    depth = model // count
    given = [] if stack is None else [stack]
    tiles = width // tile
    shape = (count, -(-tiles // beside) * depth + below, beside * tile)
    return kernel_call(
        functools.partial(rows_grad_kernel, len(xs), count),
        name,
        cost,
        (tiles,),
        any_specs(xs) + any_specs(given) + [pl.BlockSpec((tokens, tile), lambda n, f: (0, n))],
        pl.BlockSpec((count, depth, tile), lambda n, f: (0, n // beside, n % beside)),
        jax.ShapeDtypeStruct(shape, BF16),
        [pltpu.VMEM((count, tokens, depth), BF16), pltpu.SemaphoreType.DMA((count, len(xs)))],
        {1 + len(xs): 0} if given else {},
    )(place, *xs, *given, g)


def columns_grad_kernel(sets, members, f_ref, *refs):
    xs, gs = refs[:sets], refs[sets : sets + members]
    out_ref, g_buf, sem = refs[-3:]
    d = pl.program_id(0)
    rows = gs[0].shape[0]
    total, _, depth = g_buf.shape
    tile = out_ref.shape[2]

    def start(c):
        for m, g in enumerate(gs):
            src, dst = g.at[:, slot(c, depth)], g_buf.at[c, m * rows : (m + 1) * rows, :]
            pltpu.make_async_copy(src, dst, sem.at[c, m]).start()

    @pl.when(d == 0)
    def _():
        start(0)

    @pl.when(d + 1 < total)
    def _():
        start(d + 1)

    for m, g in enumerate(gs):
        src, dst = g.at[:, :depth], g_buf.at[d, m * rows : (m + 1) * rows, :]
        pltpu.make_async_copy(src, dst, sem.at[d, m]).wait()
    first = 0
    for x in xs:
        for start in range(0, x.shape[1], 512):
            size = min(512, x.shape[1] - start)
            product = dot_tn(x[:, start : start + size], g_buf[d]).astype(BF16)
            for column in range(0, depth, tile):
                row = first + column // tile * x.shape[1] + start
                out_ref[0, row : row + size, :] = product[:, column : column + tile]
        first += x.shape[1] * (depth // tile)


def columns_grad(name, place, count, tile, shape, at, xs, gs, stack=None):
    model = gs[0].shape[1]
    tokens = xs[0].shape[0]
    depth = model // count
    height = sum(x.shape[1] for x in xs) * (depth // tile)
    given = [] if stack is None else [stack]
    return kernel_call(
        functools.partial(columns_grad_kernel, len(xs), len(gs)),
        name,
        1,
        (count,),
        [pl.BlockSpec(x.shape, lambda d, f: (0, 0)) for x in xs] + any_specs(gs) + any_specs(given),
        pl.BlockSpec((1, height, tile), lambda d, f: (d, *at)),
        jax.ShapeDtypeStruct((count, *shape), BF16),
        [pltpu.VMEM((count, tokens, depth), BF16), pltpu.SemaphoreType.DMA((count, len(gs)))],
        {1 + len(xs) + len(gs): 0} if given else {},
    )(place, *xs, *gs, *given)


def forward_kernel(block, reach, g_ref, q_ref, k_ref, v_ref, seg_ref, key_ref, out_ref, lse_ref):
    i = pl.program_id(0)
    g = g_ref[0]
    scale = LOG2E / math.sqrt(HD)
    heads = q_ref.shape[1] // HD

    def run(count):
        row = lax.broadcasted_iota(jnp.int32, (block, block), 0)
        column = lax.broadcasted_iota(jnp.int32, (block, block), 1)
        keeps, rows = [], []
        for back in range(count):
            b = i - back
            rows.append(pl.ds(pl.multiple_of((b ^ g) * block, block), block))
            keep = seg_ref[0] == key_ref[b]
            if back == 0:
                keep = (keep & (row > column)) | (row == column)
            if back == reach:
                keep = keep & (row < column)
            keeps.append(keep)
        for h in range(heads):
            lanes = slice(h * HD, (h + 1) * HD)
            q = q_ref[:, lanes]
            scores = [jnp.where(keep, dot_nt(q, k_ref[r, lanes]), NEGATIVE) for keep, r in zip(keeps, rows)]
            top = functools.reduce(jnp.maximum, [jnp.max(s, axis=1, keepdims=True) for s in scores])
            weights = [jnp.exp2((s - top) * scale) for s in scores]
            total = sum(jnp.sum(w, axis=1, keepdims=True) for w in weights)
            out = sum(dot_nn(w.astype(BF16), v_ref[r, lanes]) for w, r in zip(weights, rows))
            out_ref[:, lanes] = (out / total).astype(BF16)
            lse = top * scale + jnp.log2(total)
            lse_ref[h, 0] = jnp.transpose(jnp.broadcast_to(lse, (block, HD)))[0:1, :]

    for i_here in range(reach):
        pl.when(i == i_here)(functools.partial(run, i_here + 1))
    pl.when(i >= reach)(functools.partial(run, reach + 1))


def attend_forward(qkv, place, segment, key_code, block):
    tokens, width = qkv.shape
    heads = width // 3 // HD
    count = tokens // block
    reach = WINDOW // block
    return pl.pallas_call(
        functools.partial(forward_kernel, block, reach),
        grid_spec=pltpu.PrefetchScalarGridSpec(
            num_scalar_prefetch=1,
            grid=(count,),
            in_specs=[
                pl.BlockSpec((block, heads * HD), lambda i, g: (i ^ g[0], 0)),
                pl.BlockSpec((tokens, heads * HD), lambda i, g: (0, 1)),
                pl.BlockSpec((tokens, heads * HD), lambda i, g: (0, 2)),
                pl.BlockSpec((1, block, 1), lambda i, g: (i, 0, 0)),
                pl.BlockSpec((count, 1, block), lambda i, g: (0, 0, 0)),
            ],
            out_specs=[
                pl.BlockSpec((block, heads * HD), lambda i, g: (i ^ g[0], 0)),
                pl.BlockSpec((heads, 1, 1, block), lambda i, g: (0, i, 0, 0)),
            ],
        ),
        out_shape=[
            jax.ShapeDtypeStruct((tokens, heads * HD), BF16),
            jax.ShapeDtypeStruct((heads, count, 1, block), F32),
        ],
        compiler_params=pltpu.CompilerParams(vmem_limit_bytes=VMEM_LIMIT),
        cost_estimate=pl.CostEstimate(flops=1, bytes_accessed=1, transcendentals=0),
        name="attend_forward",
    )(place, qkv, qkv, qkv, segment.reshape(count, block, 1), key_code.reshape(count, 1, block))


def backward_kernel(
    block, reach, heads, g_ref, q_ref, k_ref, v_ref, grad_ref, out_ref, lse_ref, seg_ref, key_ref, cos_ref, sin_ref, result_ref, dq_ref, dk_ref, dv_ref, inner_ref
):
    g = g_ref[0]
    count = q_ref.shape[0] // block
    scale = 1.0 / math.sqrt(HD)

    def rows_of(b):
        return pl.ds(pl.multiple_of((b ^ g) * block, block), block)

    dq_ref[...] = jnp.zeros_like(dq_ref)
    dk_ref[...] = jnp.zeros_like(dk_ref)
    dv_ref[...] = jnp.zeros_like(dv_ref)

    def inner_block(i, carry):
        rows = rows_of(i)
        for h in range(heads):
            lanes = slice(h * HD, (h + 1) * HD)
            product = grad_ref[rows, lanes].astype(F32) * out_ref[rows, lanes].astype(F32)
            inner_ref[h, i] = jnp.sum(jnp.transpose(product), axis=0, keepdims=True)
        return carry

    lax.fori_loop(0, count, inner_block, 0)
    for back in range(reach + 1):

        def pair(i, carry, back=back):
            b = i - back
            query_rows, key_rows = rows_of(i), rows_of(b)
            keep = key_ref[b] == seg_ref[i]
            if back == 0 or back == reach:
                key = lax.broadcasted_iota(jnp.int32, (block, block), 0)
                query = lax.broadcasted_iota(jnp.int32, (block, block), 1)
                if back == 0:
                    keep = (keep & (query > key)) | (query == key)
                else:
                    keep = keep & (query < key)
            for h in range(heads):
                lanes = slice(h * HD, (h + 1) * HD)
                q, k = q_ref[query_rows, lanes], k_ref[key_rows, lanes]
                v, grad = v_ref[key_rows, lanes], grad_ref[query_rows, lanes]
                scores = dot_nt(k, q)
                weights = jnp.where(keep, jnp.exp2(scores * (scale * LOG2E) - lse_ref[h, i]), 0.0)
                grad_weights = dot_nt(v, grad)
                grad_scores = (weights * (grad_weights - inner_ref[h, i])).astype(BF16)
                dv_ref[key_rows, lanes] += dot_nn(weights.astype(BF16), grad)
                dk_ref[key_rows, lanes] += dot_nn(grad_scores, q)
                dq_ref[query_rows, lanes] += dot_tn(grad_scores, k)
            return carry

        lax.fori_loop(back, count, pair, 0)

    def store(i, carry):
        rows = pl.ds(pl.multiple_of(i * block, block), block)
        cosine, sine = cos_ref[rows, :], sin_ref[rows, :]
        for h in range(heads):
            lanes = slice(h * HD, (h + 1) * HD)
            for part, ref in enumerate((dq_ref, dk_ref)):
                value = ref[rows, lanes] * scale
                turned = value * cosine - pltpu.roll(value, HD // 2, 1) * sine
                result_ref[rows, (part * heads + h) * HD : (part * heads + h + 1) * HD] = turned.astype(BF16)
            result_ref[rows, (2 * heads + h) * HD : (2 * heads + h + 1) * HD] = dv_ref[rows, lanes].astype(BF16)
        return carry

    lax.fori_loop(0, count, store, 0)


def attend_backward(qkv, grad, out, lse, place, segment, key_code, cosine, sine, block, cost):
    tokens, width = qkv.shape
    heads = width // 3 // HD
    count = tokens // block
    reach = WINDOW // block
    return pl.pallas_call(
        functools.partial(backward_kernel, block, reach, heads),
        grid_spec=pltpu.PrefetchScalarGridSpec(
            num_scalar_prefetch=1,
            grid=(1,),
            in_specs=[
                pl.BlockSpec((tokens, heads * HD), lambda h, g: (0, 0)),
                pl.BlockSpec((tokens, heads * HD), lambda h, g: (0, 1)),
                pl.BlockSpec((tokens, heads * HD), lambda h, g: (0, 2)),
                pl.BlockSpec((tokens, heads * HD), lambda h, g: (0, 0)),
                pl.BlockSpec((tokens, heads * HD), lambda h, g: (0, 0)),
                pl.BlockSpec((heads, count, 1, block), lambda h, g: (0, 0, 0, 0)),
                pl.BlockSpec((count, 1, block), lambda h, g: (0, 0, 0)),
                pl.BlockSpec((count, block, 1), lambda h, g: (0, 0, 0)),
                pl.BlockSpec((tokens, HD), lambda h, g: (0, 0)),
                pl.BlockSpec((tokens, HD), lambda h, g: (0, 0)),
            ],
            out_specs=pl.BlockSpec((tokens, width), lambda h, g: (0, 0)),
            scratch_shapes=[
                pltpu.VMEM((tokens, heads * HD), F32),
                pltpu.VMEM((tokens, heads * HD), F32),
                pltpu.VMEM((tokens, heads * HD), F32),
                pltpu.VMEM((heads, count, 1, block), F32),
            ],
        ),
        out_shape=jax.ShapeDtypeStruct((tokens, width), BF16),
        compiler_params=pltpu.CompilerParams(vmem_limit_bytes=VMEM_LIMIT),
        cost_estimate=pl.CostEstimate(flops=cost, bytes_accessed=1, transcendentals=0),
        name="attend_backward",
    )(
        place, qkv, qkv, qkv, grad, out, lse,
        segment.reshape(count, 1, block), key_code.reshape(count, block, 1), cosine, sine,
    )


def local(inputs, att_proj, attn_out, ff_proj, ff_out, segments, pad_mask, positions, cotangent):
    tp_size, fsdp_size = lax.axis_size("tp"), lax.axis_size("fsdp")
    rows, model = inputs.shape
    members = SEQ_LEN // rows
    sets = tp_size // members
    index = lax.axis_index("tp")
    mine = index // members
    place = index % members
    block = min(512, rows)
    depth, head_width = att_proj.shape[0], att_proj.shape[2]
    ffn_width = ff_out.shape[0]
    place_tp = place.astype(jnp.int32).reshape(1)
    place_fsdp = lax.axis_index("fsdp").astype(jnp.int32).reshape(1)

    def swap(values, bit):
        return lax.ppermute(values, "tp", [(i, i ^ bit) for i in range(tp_size)])

    def turn(values, step):
        return lax.ppermute(values, "tp", [(i, (i + step * members) % tp_size) for i in range(tp_size)])

    def cross(values, mask):
        return lax.ppermute(values, "fsdp", [(i, i ^ mask) for i in range(fsdp_size)])

    def after(value, *others):
        return lax.optimization_barrier((value, others))[0]

    chain = []

    def then(function, *args, due=()):
        args, _ = lax.optimization_barrier((args, (chain[-1], due)))
        result = function(*args)
        chain.append(jax.tree.leaves(result)[0])
        return result

    def last():
        return chain[-1]

    def group_far(values):
        blocks = {0: values}
        bit = members // 2
        while bit > 1:
            for mask in sorted(blocks, reverse=True):
                blocks[mask | bit] = swap(blocks[mask], bit)
            bit //= 2
        return [blocks[mask] for mask in range(0, members, 2)]

    def scatter_far(sums):
        sums = dict(sums)
        parts = [sums[0]]
        bit = 2
        while bit < members:
            for mask in sorted((m for m in sums if m & bit), reverse=True):
                received = swap(sums.pop(mask), bit)
                if mask == bit:
                    parts.append(received)
                else:
                    sums[mask ^ bit] = (sums[mask ^ bit].astype(F32) + received.astype(F32)).astype(BF16)
            bit *= 2
        return parts

    half = members // 2

    def share(function, *args, number, due=(), due_near=(), cost_near=1):
        sums = {}
        for part, first in enumerate((half, 0)):
            cost = 1 if first else cost_near
            call = functools.partial(function, rows=rows, first=first, members=half, number=number + part, cost=cost)
            outs = then(lambda xs, weights, *base: call(xs, weights, base=base[0] if base else None), *args, due=due)
            sums.update({first + 2 * q: out for q, out in enumerate(outs)})
            due = due_near
        return sums

    def gather(shard):
        return lax.all_gather(shard, "fsdp", axis=0)

    def scatter(stacked):
        return lax.psum_scatter(stacked.reshape(-1, stacked.shape[-1]), "fsdp", scatter_dimension=0, tiled=True)

    def settle(pieces, *gates):
        return pieces[:1] + [turn(after(pieces[step], *gates), sets - step) for step in range(1, sets)]

    def settled(pieces):
        return sum(piece.astype(F32) for piece in pieces)

    normed_far, packs = start_exchange(inputs, pack_weights(att_proj, attn_out), members, sets, fsdp_size)
    chain.append(normed_far[0])
    up_gate, down, cotangent_late = after((ff_proj.reshape(depth, -1), ff_out, cotangent), last())
    w_ffn, w_down = [gather(up_gate)], [gather(down)]
    turned_up_gate = [turn(up_gate, step) for step in range(1, sets)]
    cotangent_far = group_far(cotangent_late)

    segment = lax.dynamic_slice_in_dim(segments, mine * SEQ_LEN, SEQ_LEN)
    padding = lax.dynamic_slice_in_dim(pad_mask, mine * SEQ_LEN, SEQ_LEN)
    key_code = jnp.where(padding == 1, segment, -1)
    spots = lax.dynamic_slice_in_dim(positions, mine * SEQ_LEN, SEQ_LEN).reshape(members, rows)
    spots = jnp.concatenate([lax.dynamic_index_in_dim(spots, place ^ mask, 0, False) for mask in range(members)])
    cosine, sine = rope_tables(spots)

    x_float = inputs.astype(F32)
    qkv, attended = [], []
    for step in range(sets):
        if step == 0:
            (part,), normed_all = then(functools.partial(project, number=12), normed_far, packs[0], cosine, sine)
        else:
            (part,), _ = then(project, normed_all, packs[step], cosine, sine)
        qkv.append(part)
        attended.append(then(lambda part: attend_forward(part, place_tp, segment, key_code, block), qkv[step]))
    heads_low = [out for out, _ in attended]
    sums = share(functools.partial(expand_heads, "attn_branch"), heads_low, packs, number=1)
    w_ffn += [gather(after(part, last(), cotangent_far)) for part in turned_up_gate]
    resid = x_float + settled(scatter_far(sums))
    normed_two_far = group_far(layer_norm(resid).astype(BF16))
    turned_down = [turn(after(ff_out, normed_two_far[-1]), step) for step in range(1, sets)]

    hidden, slopes, grad_ffn, partial = [], [], [], None
    for step in range(sets):
        if step == 0:
            (low, *slope), normed_two_all = then(functools.partial(hidden_units, number=9), normed_two_far, w_ffn[0])
        else:
            (low, *slope), _ = then(hidden_units, normed_two_all, w_ffn[step])
        hidden.append(low)
        slopes.append(slope)
    w_down += [gather(after(part, last())) for part in turned_down]
    ffn_rows = 2 * ffn_width
    grad_expand = functools.partial(expand_stack, "grad_normed_two", dot_nt)
    up_grad = functools.partial(rows_grad, "grad_ffn", place_fsdp, fsdp_size, depth, 1, 0)
    for step in range(sets):
        if step == 0:
            (grad_low,), cotangent_all = then(functools.partial(hidden_grad, number=10, cost=LONG), cotangent_far, *slopes[0], w_down[0])
        else:
            (grad_low,), _ = then(hidden_grad, cotangent_all, *slopes[step], w_down[step])
        grad_ffn.append(scatter(then(up_grad, normed_two_all, grad_low)))
        base = [] if partial is None else [partial]
        if step < sets - 1:
            call = lambda x, w, *b: grad_expand([x], [w], members * rows, base=b[0] if b else None)[0]
            partial = then(call, grad_low, w_ffn[step], *base)
    sums = share(grad_expand, [grad_low], [w_ffn[-1]], *base, number=3)
    ffn_sums = share(functools.partial(expand_stack, "ffn_branch", dot_nn), hidden, w_down, number=5)
    grad_normed_two = settled(after(scatter_far(sums), ffn_sums[half]))
    grad_resid = cotangent.astype(F32) + layer_norm_back(resid, grad_normed_two)
    resid_grad_low = grad_resid.astype(BF16)
    resid_grad_far = group_far(resid_grad_low)
    shape, at = (sets * ffn_width, depth), (0, 0)
    down_grad = functools.partial(columns_grad, "grad_down", place_fsdp, fsdp_size, depth, shape, at)
    grad_down = scatter(then(down_grad, hidden, cotangent_all, due=(resid_grad_low,)))

    grad_attn, grad_project = [None] * sets, [None] * sets
    shape, at = (2 * depth, 2 * head_width), (1, 1)
    heads_grad = functools.partial(columns_grad, "grad_heads", place_fsdp, fsdp_size, head_width, shape, at)
    project_grad = functools.partial(rows_grad, "grad_attn", place_fsdp, fsdp_size, head_width, 2, 0)
    held = None
    for step in reversed(range(sets)):
        if step == sets - 1:
            call = functools.partial(head_grad_of, number=11)
            (head_grad,), resid_grad_all = then(call, resid_grad_far, packs[step], due=tuple(grad_ffn[:1]))
            grad_up = settle([piece[:ffn_width] for piece in grad_ffn], last())
            ffn_branch = scatter_far(after(ffn_sums, last()))
        else:
            (head_grad,), _ = then(head_grad_of, resid_grad_all, packs[step])
        grad_project[step] = then(
            lambda part, grad, out, lse: attend_backward(
                part, grad, out, lse, place_tp, segment, key_code, cosine, sine, block, LONG if step == sets - 1 else 1
            ),
            qkv[step], head_grad, heads_low[step], attended[step][1],
        )
        ready = (grad_up[1:], ffn_branch[1:]) if step == 0 else ()
        stacked = then(heads_grad, [heads_low[step]], resid_grad_all, due=ready)
        if held is not None:
            grad_attn[step + 1] = scatter(after(held, last()))
            grad_gate = settle([piece[ffn_width:] for piece in grad_ffn], grad_up[1:])
            grad_down = settle([grad_down[j * ffn_width : (j + 1) * ffn_width] for j in range(sets)], last())
        held = then(project_grad, normed_all, grad_project[step], stacked)
    grad_attn[0] = scatter(held)
    call = functools.partial(expand_project, "grad_normed")
    due = ((), tuple(grad_gate[1:]))
    sums = share(call, grad_project, packs, number=7, due=due[0], due_near=due[1], cost_near=100 * LONG)
    grad_normed = scatter_far(sums)
    output = (resid + settled(ffn_branch)).astype(BF16)
    grad_attn = settle(grad_attn)
    grad_normed = settled(after(grad_normed, grad_attn[1:], grad_down[1:]))
    grad_input = (grad_resid + layer_norm_back(x_float, grad_normed)).astype(BF16)
    grad_attn = settled(grad_attn)

    def beside(values, first, size, count):
        return jnp.concatenate([values[(first + i) * size : (first + i + 1) * size] for i in range(count)], axis=1)

    query, key = grad_attn[:depth, :head_width], grad_attn[:depth, head_width:]
    value, squares = grad_attn[depth:, :head_width], grad_attn[depth:, head_width:]
    blocks = ffn_width // depth

    return (
        output,
        grad_input,
        jnp.stack([query, key, value], axis=1),
        beside(squares, 0, head_width, depth // head_width),
        jnp.stack([beside(settled(part), 0, depth, blocks) for part in (grad_up, grad_gate)], axis=1),
        settled(grad_down),
    )


def solution(mesh):
    rows_spec = P(("fsdp", "tp"), None)
    weights = (P("fsdp", None, "tp"), P("tp", "fsdp"), P("fsdp", None, "tp"), P("tp", "fsdp"))
    return jax.shard_map(
        local,
        mesh=mesh,
        in_specs=(rows_spec,) + weights + (P("fsdp"),) * 3 + (rows_spec,),
        out_specs=(rows_spec, rows_spec) + weights,
        check_vma=False,
    )
```
